256 devices in a mesh: slab: 4 (over y), dom: 64 (over z, x, core).
Axes of the slice: x: 4, y: 4, z: 8, core: 2. Of those that a mesh axis runs over, the one named last changes fastest.
Arguments:
- disp: float32 [64, 96, 32, 384], P('dom', 'slab'), may hold values from -6 to 6
- f_ext: bfloat16 [64, 96, 32, 384], P('dom', 'slab'), may hold values from -6 to 6
- inv_diag: bfloat16 [64, 96, 32, 384], P('dom', 'slab'), may hold values from 0.049804688 to 0.29882812
- k_self: bfloat16 [384, 384], replicated, may hold values from -0.3125 to 0.3125
- k_layer: bfloat16 [384, 384], replicated, may hold values from -0.3125 to 0.3125
- k_side: bfloat16 [384, 384], replicated, may hold values from -0.3125 to 0.3125
- mortar: bfloat16 [64, 4, 128, 128, 128], P('dom', 'slab'), as said below
- gap0: float32 [64, 4, 128, 128], P('dom', 'slab'), may hold values from -1 to 1
- normals: float32 [64, 4, 32, 384], P('dom', 'slab'), may hold values from -4 to 4
- seg_slave: int32 [64, 4, 128], P('dom', 'slab'), may hold values from 0 to 31
- seg_src: int32 [64, 4, 128], P('dom', 'slab'), may hold values from 0 to 63, as said below
- seg_master: int32 [64, 4, 128], P('dom', 'slab'), may hold values from 0 to 31
Outputs:
- field: float32 [64, 96, 32, 384], P('dom', 'slab')
The draws below stay inside these ranges and needn't reach their ends.
Inputs may be any that keep to these rules, and one draw needn't show every extreme that they name: `seg_src`: among the 128 segments of one partition no dom index is named more than 4 times, and one is named exactly 4 times. `mortar`: each segment's projection has independent entries off its diagonal.
All inputs are finite; a program needn't handle non-finite values.
Results may differ from the reference program's by a relative error of at most 0.0017.
Values may be sent and summed in bfloat16 or wider, within the bound.
No kernel may reach another device: no remote copies, remote signals or barrier semaphores. Data moves between devices by JAX's collectives and lax.ppermute only.
A program may use at most 64 MiB of HBM per device.

```python
import math
import jax
import jax.numpy as jnp
from jax import lax

NB = 128
BLK_L = 32
SEG = 128
ITERS = 2
LT = 96
N_SLAB = 4
N_DOM = 64


def source_list(key):
    capacity = 2 * SEG // N_DOM
    half = capacity // 2
    key_order, key_shift, key_mix = jax.random.split(key, 3)
    order = jax.random.permutation(key_order, N_DOM)
    shifts = jax.random.randint(key_shift, (N_DOM // 2,), -half, half + 1)
    shifts = shifts.at[0].set(half)
    paired = jnp.stack([half + shifts, half - shifts], axis=1).reshape(-1).astype(jnp.int32)
    counts = jnp.zeros((N_DOM,), jnp.int32).at[order].set(paired)
    ends = jnp.cumsum(counts)
    places = jnp.arange(SEG, dtype=jnp.int32)
    sources = jnp.sum((places[:, None] >= ends[None, :]).astype(jnp.int32), axis=1)
    mixing = jax.random.permutation(key_mix, SEG)
    return sources[mixing].astype(jnp.int32)


def draw_seg_src(key, part):
    key = jax.random.fold_in(key, 11)
    keys = jax.random.split(key, N_DOM * N_SLAB)
    return jax.vmap(source_list)(keys).reshape(N_DOM, N_SLAB, SEG)


def draw_mortar(key, part):
    key = jax.random.fold_in(key, 5)
    key_diag, key_off = jax.random.split(key)
    diagonal = jax.random.uniform(key_diag, (N_DOM, N_SLAB, SEG, NB), jnp.float32, 0.5, 1.0)
    off = jax.random.normal(key_off, (N_DOM, N_SLAB, SEG, NB, NB), jnp.float32) * (0.35 / NB ** 0.5)
    eye = jnp.eye(NB, dtype=jnp.float32)
    return (off + eye * diagonal[..., None]).astype(jnp.bfloat16)


def plant(drawn, own_key, least, high):
    place = [jax.random.randint(jax.random.fold_in(own_key, axis), (), 0, length) for axis, length in enumerate(drawn.shape)]
    main_axis = drawn.shape.index(max(drawn.shape))
    beside = place[:main_axis] + [(place[main_axis] + 1) % drawn.shape[main_axis]] + place[main_axis + 1:]
    return drawn.at[tuple(place)].set(least).at[tuple(beside)].set(high)


def block_scale(stream_key, dims, cuts, least, high):
    gain = 1.0
    for dim, shards_of in cuts:
        steps = jax.random.uniform(jax.random.fold_in(jax.random.fold_in(stream_key, 6), dim), (shards_of,), jnp.float32, least / len(cuts), high / len(cuts))
        gain = gain * jnp.repeat(jnp.exp(steps), dims[dim] // shards_of).reshape((-1,) + (1,) * (len(dims) - 1 - dim))
    return gain


def gaussian(stream_key, extent, scale, limit, cuts=(), kind=jnp.bfloat16):
    gain = block_scale(stream_key, extent, cuts, -0.22, 0.18) if cuts else 1.0
    entries = jax.random.normal(stream_key, extent, jnp.float32) * scale * gain
    return jnp.minimum(jnp.maximum(entries, -limit), limit).astype(kind)


def setup_inputs(seed: int = 0) -> dict:
    arg_keys = jax.random.split(jax.random.key(seed), 13)
    disp = gaussian(arg_keys[0], (N_DOM, LT, BLK_L, 3 * NB), 1.0, 6.0, ((0, 64), (1, 4)), jnp.float32)
    f_ext = gaussian(arg_keys[1], (N_DOM, LT, BLK_L, 3 * NB), 1.0, 6.0, ((0, 64), (1, 4)))
    inv_diag = jnp.clip(jnp.exp(math.log(0.29882812) - 1.7917595 * jax.random.uniform(arg_keys[2], (N_DOM, LT, BLK_L, 3 * NB), jnp.float32) ** block_scale(arg_keys[2], (N_DOM, LT, BLK_L, 3 * NB), ((0, 64), (1, 4)), -0.2, 0.2)), 0.049804688, 0.29882812).astype(jnp.bfloat16)
    k_self = gaussian(arg_keys[3], (3 * NB, 3 * NB), (3 * NB) ** -0.5, 0.3125)
    k_layer = gaussian(arg_keys[4], (3 * NB, 3 * NB), (3 * NB) ** -0.5, 0.3125)
    k_side = gaussian(arg_keys[5], (3 * NB, 3 * NB), (3 * NB) ** -0.5, 0.3125)
    mortar = draw_mortar(jax.random.fold_in(arg_keys[12], 71), 0)
    gap0 = jnp.clip(jax.random.uniform(arg_keys[7], (N_DOM, N_SLAB, SEG, NB), jnp.float32, -1.0, 1.0) * block_scale(arg_keys[7], (N_DOM, N_SLAB, SEG, NB), ((0, 64), (1, 4)), -0.4, 0.0), -1.0, 1.0)
    normals = gaussian(arg_keys[8], (N_DOM, N_SLAB, BLK_L, 3 * NB), 0.6, 4.0, ((0, 64), (1, 4)), jnp.float32)
    seg_slave = plant(jax.random.randint(arg_keys[9], (N_DOM, N_SLAB, SEG), 0, BLK_L), jax.random.fold_in(arg_keys[9], 1), 0, BLK_L - 1).astype(jnp.int32)
    seg_src = draw_seg_src(jax.random.fold_in(arg_keys[12], 71), 0)
    seg_master = plant(jax.random.randint(arg_keys[11], (N_DOM, N_SLAB, SEG), 0, BLK_L), jax.random.fold_in(arg_keys[11], 1), 0, BLK_L - 1).astype(jnp.int32)
    return dict(disp=disp, f_ext=f_ext, inv_diag=inv_diag, k_self=k_self, k_layer=k_layer, k_side=k_side, mortar=mortar, gap0=gap0, normals=normals, seg_slave=seg_slave, seg_src=seg_src, seg_master=seg_master)


PENALTY = 2.0


def column_force(rounded, k_self, k_layer, k_side):
    width = rounded.shape[-1]
    padded = jnp.pad(rounded, ((1, 1), (0, 0), (0, 0)))
    sides = jnp.pad(rounded, ((0, 0), (1, 1), (0, 0)))

    def product(block, weight):
        return jnp.dot(block.reshape(-1, width), weight, preferred_element_type=jnp.float32)

    total = product(rounded, k_self) + product(padded[:-2], k_layer) + product(padded[2:], k_layer)
    total = total + product(sides[:, :-2], k_side) + product(sides[:, 2:], k_side)
    return total.reshape(rounded.shape)


def contact_terms(slave_rows, master_rows, mortar_part, gap_part, normal_rows):
    segs, width = master_rows.shape
    nodes = width // 3
    mortar32 = mortar_part.astype(jnp.float32)
    mapped = jnp.einsum("snm,scm->scn", mortar32, master_rows.astype(jnp.float32).reshape(segs, 3, nodes))
    normal3 = normal_rows.reshape(segs, 3, nodes)
    gap = gap_part + jnp.sum(normal3 * (mapped - slave_rows.reshape(segs, 3, nodes)), axis=1)
    pressure = PENALTY * jnp.maximum(-gap, 0.0)
    pushed = pressure[:, None, :] * normal3
    pushed_b = pushed.astype(jnp.bfloat16).astype(jnp.float32)
    back = -jnp.einsum("snm,scn->scm", mortar32, pushed_b)
    return pushed.reshape(segs, width), back.reshape(segs, width)


def reference(disp, f_ext, inv_diag, k_self, k_layer, k_side, mortar, gap0, normals, seg_slave, seg_src, seg_master):
    field = disp
    load = f_ext.astype(jnp.float32)
    scale = inv_diag.astype(jnp.float32)
    domains, total_layers, blocks, width = disp.shape
    slabs = N_SLAB
    layers = total_layers // slabs
    slab_ids = jnp.arange(slabs, dtype=jnp.int32)[:, None]
    slab_full = jnp.broadcast_to(jnp.arange(slabs, dtype=jnp.int32)[None, :, None], seg_src.shape)
    for step in range(ITERS):
        rounded = field.astype(jnp.bfloat16)
        internal = lax.map(lambda column: column_force(column, k_self, k_layer, k_side), rounded)
        surfaces = rounded[:, ::layers]
        slave_surf = field[:, ::layers]

        def one_domain(items):
            slave_part, mortar_part, gap_part, normal_part, slave_ids, source_ids, master_ids = items
            master_rows = surfaces[source_ids, slab_ids, master_ids]
            slave_rows = slave_part[slab_ids, slave_ids]
            normal_rows = normal_part[slab_ids, slave_ids]
            pushed, back = jax.vmap(contact_terms)(slave_rows, master_rows, mortar_part, gap_part, normal_rows)
            slave_force = jnp.zeros((slabs, blocks, width), jnp.float32).at[slab_ids, slave_ids].add(pushed)
            return slave_force, back

        slave_force, back = lax.map(one_domain, (slave_surf, mortar, gap0, normals, seg_slave, seg_src, seg_master))
        master_force = jnp.zeros((domains, slabs, blocks, width), jnp.float32).at[seg_src, slab_full, seg_master].add(back)
        contact = slave_force + master_force
        residual = load - internal
        residual = residual.at[:, ::layers].add(-contact)
        field = field + scale * residual
    return field
```

```python
import jax
import jax.numpy as jnp
from jax import lax
from jax.sharding import PartitionSpec as P

ITERS = 2
PENALTY = 2.0
CAPACITY = 4


def shift(block, axis, step):
    count = lax.axis_size(axis)
    pairs = [(i, i + step) for i in range(count) if 0 <= i + step < count]
    return lax.ppermute(block, axis, pairs)


def stiffness(rounded, low, high, k_all):
    layers, blocks, width = rounded.shape
    stacked = jnp.concatenate([low, rounded, high], axis=0)
    prod = jnp.dot(
        stacked.reshape(-1, width), k_all, preferred_element_type=jnp.float32
    ).reshape(layers + 2, blocks, 3 * width)
    own, layer, side = prod[1:-1, :, :width], prod[:, :, width : 2 * width], prod[1:-1, :, 2 * width :]
    side = jnp.pad(side, ((0, 0), (1, 1), (0, 0)))
    return own + layer[:-2] + layer[2:] + side[:, :-2] + side[:, 2:]


def exchange(rows):
    domains = lax.axis_size("dom")
    parts = rows.reshape(domains, CAPACITY, -1)
    return lax.all_to_all(parts, "dom", 0, 0, tiled=True).reshape(rows.shape)


def on_device(
    disp, f_ext, inv_diag, k_self, k_layer, k_side, mortar, gap0, normals, seg_slave, seg_src, seg_master
):
    field = disp[0]
    load = f_ext[0].astype(jnp.float32)
    scale = inv_diag[0].astype(jnp.float32)
    mortar_own = mortar[0, 0]
    gap_own = gap0[0, 0]
    normal_own = normals[0, 0]
    slave_ids = seg_slave[0, 0]
    source_ids = seg_src[0, 0]
    master_ids = seg_master[0, 0]
    blocks, width = field.shape[1:]
    segs = slave_ids.shape[0]
    nodes = width // 3
    slots = lax.axis_size("dom") * CAPACITY
    bf16 = jnp.bfloat16

    places = jnp.arange(segs, dtype=jnp.int32)
    same = (source_ids[:, None] == source_ids[None, :]) & (places[None, :] < places[:, None])
    slot = source_ids * CAPACITY + jnp.sum(same.astype(jnp.int32), axis=1)
    hit = slot[:, None] == jnp.arange(slots, dtype=jnp.int32)[None, :]
    asked = jnp.sum(jnp.where(hit, master_ids[:, None] + 1, 0), axis=0) - 1
    wanted = exchange(asked[:, None])
    block_ids = jnp.arange(blocks, dtype=jnp.int32)
    send_pick = (wanted == block_ids[None, :]).astype(bf16)
    recv_pick = hit.astype(bf16)
    slave_pick = (slave_ids[:, None] == block_ids[None, :]).astype(jnp.float32)

    def pick(mask, rows):
        return jnp.dot(mask, rows, preferred_element_type=jnp.float32)

    normal3 = jnp.dot(slave_pick, normal_own, precision=lax.Precision.HIGHEST).reshape(segs, 3, nodes)
    k_all = jnp.concatenate([k_self, k_layer, k_side], axis=1)
    for step in range(ITERS):
        rounded = field.astype(bf16)
        arrived = exchange(pick(send_pick, rounded[0]).astype(bf16))
        low = shift(rounded[-1:], "slab", 1)
        high = shift(rounded[:1], "slab", -1)
        internal = stiffness(rounded, low, high, k_all)
        master_rows = pick(recv_pick, arrived).astype(bf16).reshape(segs, 3, nodes)
        slave_rows = jnp.dot(slave_pick, field[0], precision=lax.Precision.HIGHEST).reshape(segs, 3, nodes)
        mapped = jnp.einsum("snm,scm->scn", mortar_own, master_rows, preferred_element_type=jnp.float32)
        gap = gap_own + jnp.sum(normal3 * (mapped - slave_rows), axis=1)
        pressure = PENALTY * jnp.maximum(-gap, 0.0)
        pushed = pressure[:, None, :] * normal3
        back = -jnp.einsum("snm,scn->scm", mortar_own, pushed.astype(bf16), preferred_element_type=jnp.float32)
        returned = exchange(pick(recv_pick.T, back.astype(bf16).reshape(segs, width)).astype(bf16))
        master_force = pick(send_pick.T, returned)
        slave_force = jnp.dot(slave_pick.T, pushed.reshape(segs, width), precision=lax.Precision.HIGHEST)
        residual = load - internal
        residual = residual.at[0].add(-(slave_force + master_force))
        field = field + scale * residual
    return field[None]


def solution(mesh):
    in_specs = (
        P("dom", "slab", None, None),
        P("dom", "slab", None, None),
        P("dom", "slab", None, None),
        P(),
        P(),
        P(),
        P("dom", "slab", None, None, None),
        P("dom", "slab", None, None),
        P("dom", "slab", None, None),
        P("dom", "slab", None),
        P("dom", "slab", None),
        P("dom", "slab", None),
    )
    return jax.shard_map(
        on_device, mesh=mesh, in_specs=in_specs, out_specs=P("dom", "slab", None, None), check_vma=False
    )
```

```python
import jax
import jax.numpy as jnp
from jax import lax
from jax.experimental import pallas as pl
from jax.experimental.pallas import tpu as pltpu
from jax.sharding import PartitionSpec as P

PENALTY = 2.0
CAPACITY = 4
GROUP = 16
PARTS = 2
VMEM = pltpu.VMEM
HBM = pl.BlockSpec(memory_space=pltpu.HBM)
BF16 = jnp.bfloat16
F32 = jnp.float32


def dot(a, b, dims=((1,), (0,))):
    return lax.dot_general(a, b, (dims, ((), ())), preferred_element_type=F32)


def iota(shape, axis):
    return lax.broadcasted_iota(jnp.int32, shape, axis)


def shaped(shape, dtype):
    return jax.ShapeDtypeStruct(shape, dtype)


def in_hbm(*arrays):
    return [pltpu.with_memory_space_constraint(array, pltpu.HBM) for array in arrays]


def staged(body, ins, outs, scratch=(), tokens=(), loose=(), free_outs=False):
    ins = [item if isinstance(item, tuple) else (item, ()) for item in ins]
    operands = [array if i in loose else in_hbm(array)[0] for i, (array, _) in enumerate(ins)]
    held = [VMEM(part_shape(array, index), array.dtype) for array, index in ins]
    given = [VMEM(out.shape, out.dtype) for out in outs]

    def kernel(*refs):
        refs = list(refs)

        def pop(count):
            taken = refs[:count]
            del refs[:count]
            return taken

        sources, _, targets = pop(len(ins)), pop(len(tokens)), pop(len(outs))
        inside, leaving, (in_sems, out_sems), extra = pop(len(ins)), pop(len(outs)), pop(2), refs
        loads = {}
        for i, (source, ref, (_, index)) in enumerate(zip(sources, inside, ins)):
            loads[i] = pltpu.make_async_copy(source.at[index] if index else source, ref, in_sems.at[i])
            loads[i].start()

        def take(i):
            if i in loads:
                loads.pop(i).wait()
            return inside[i]

        stores = []

        def give(i, index=None):
            source, target = leaving[i], targets[i]
            if index is not None:
                source, target = source.at[index], target.at[index]
            stores.append(pltpu.make_async_copy(source, target, out_sems.at[i]))
            stores[-1].start()

        body(take, leaving, give, *extra)
        assert not loads
        for store in stores:
            store.wait()

    sems = [pltpu.SemaphoreType.DMA((len(ins),)), pltpu.SemaphoreType.DMA((len(outs),))]
    return pl.pallas_call(
        kernel,
        out_shape=tuple(out if free_outs else pltpu.HBM(out.shape, out.dtype) for out in outs),
        in_specs=[pl.BlockSpec(memory_space=pl.ANY)] * (len(ins) + len(tokens)),
        out_specs=(pl.BlockSpec(memory_space=pl.ANY),) * len(outs),
        scratch_shapes=held + given + sems + list(scratch),
        compiler_params=pltpu.CompilerParams(vmem_limit_bytes=32 * 2**20),
    )(*operands, *tokens)


def part_shape(array, index):
    kept = [i.size for i in index if not isinstance(i, int)]
    return tuple(kept) + array.shape[len(index) :]


def slots_of(src, count):
    segs = src.shape[1]
    named = (iota((count, segs), 0) == src).astype(BF16)
    earlier = (iota((segs, segs), 0) < iota((segs, segs), 1)).astype(BF16)
    before = dot(named, earlier)
    rank = jnp.sum(named.astype(F32) * before, axis=0, keepdims=True).astype(jnp.int32)
    return named, rank


def request_kernel(blocks, take, out, give):
    src, master = take(0)[0], take(1)[0]
    count = out[0].shape[0]
    named, rank = slots_of(src, count)
    segs = named.shape[1]
    wants = (iota((CAPACITY * blocks, segs), 0) == rank * blocks + master).astype(BF16)
    out[0][...] = dot(named, wants, ((1,), (1,)))
    give(0)


def split3(rows):
    high = rows.astype(BF16)
    rest = rows - high.astype(F32)
    mid = rest.astype(BF16)
    low = (rest - mid.astype(F32)).astype(BF16)
    return jnp.concatenate([high, mid, low], axis=0)


def prep_kernel(take, out, give):
    put_ref, get_ref, take_ref, sum_ref, normal_rows_ref, low_ref, high_ref = out
    high_ref[...] = take(3)[...].astype(BF16)
    low_ref[...] = take(4)[...].astype(BF16)
    give(5)
    give(6)
    src, slave, normals = take(0)[0], take(1)[0], take(2)[...]
    blocks = normals.shape[0]
    slots, segs = put_ref.shape
    _, rank = slots_of(src, slots // CAPACITY)
    put = (iota((slots, segs), 0) == src * CAPACITY + rank).astype(F32)
    put_ref[...] = put.astype(BF16)
    give(0)
    get_ref[...] = jnp.transpose(put).astype(BF16)
    give(1)
    spread = (lax.rem(iota((4 * blocks, segs), 0), blocks) == slave).astype(F32)
    pick = jnp.transpose(spread)[:, : 3 * blocks].astype(BF16)
    take_ref[...] = pick
    give(2)
    once = spread[:blocks].astype(BF16)
    sum_ref[...] = jnp.concatenate([once, once], axis=1)
    give(3)
    normal_rows_ref[...] = dot(pick, split3(normals))
    give(4)


def place(rows, scratch, out_ref):
    scratch[...] = rows
    for i in range(out_ref.shape[0]):
        out_ref[i] = scratch[CAPACITY * i : CAPACITY * (i + 1), :].astype(BF16)


def gathered(in_ref, scratch):
    for i in range(in_ref.shape[0]):
        scratch[CAPACITY * i : CAPACITY * (i + 1), :] = in_ref[i].astype(F32)
    return scratch[...].astype(BF16)


def copies(rows):
    return jnp.concatenate([rows] * CAPACITY, axis=0)


def first_kernel(take, out, give, scratch):
    pick_ref, out_ref = out
    slots, wide = pick_ref.shape
    count, blocks = slots // CAPACITY, wide // CAPACITY
    expand = (lax.div(iota((slots, count), 0), CAPACITY) == iota((slots, count), 1)).astype(BF16)
    mine = lax.div(iota((slots, wide), 1), blocks) == lax.rem(iota((slots, wide), 0), CAPACITY)
    rows = dot(expand, take(0)[...].astype(BF16))
    pick = jnp.where(mine, rows, 0.0).astype(BF16)
    pick_ref[...] = pick
    give(0)
    place(dot(pick, copies(take(1)[...].astype(BF16))), scratch, out_ref)
    give(1)


def contact_kernel(take, out, give, scratch, back_ref):
    out_ref, pushed_ref = out
    segs = back_ref.shape[0]
    nodes = back_ref.shape[1] // 3
    member = lax.rem(iota((3 * GROUP, nodes), 0), GROUP)
    place_in = lax.rem(member, 4)
    block_of = lax.div(member, 4)
    odd = lax.rem(place_in, 2) == 1
    late = place_in >= 2
    zero = jnp.zeros((3 * GROUP, nodes), BF16)
    slave = dot(take(3)[...], split3(take(4)[...]))
    arrived = gathered(take(0), scratch)
    master = dot(take(1)[...], arrived).astype(BF16)
    normal_ref, gap_ref = take(5), take(6)

    def columns(rows):
        return [rows[:, c * nodes : (c + 1) * nodes] for c in range(3)]

    def choose(parts):
        result = parts[0]
        for b in range(1, GROUP // 4):
            result = jnp.where(block_of == b, parts[b], result)
        return result

    for g in range(segs // GROUP):
        own = slice(GROUP * g, GROUP * (g + 1))
        um = jnp.concatenate(columns(master[own]), axis=0)
        us = jnp.concatenate(columns(slave[own]), axis=0)
        normal = jnp.concatenate(columns(normal_ref[own, :]), axis=0)
        mortar_ref = take(7 + g)
        weights = []
        for s in range(0, GROUP, 4):
            left = mortar_ref[s : s + 2].reshape(2 * nodes, nodes)
            right = mortar_ref[s + 2 : s + 4].reshape(2 * nodes, nodes)
            weights.append(jnp.concatenate([left, right], axis=1))
        lhs = jnp.concatenate([jnp.where(late, zero, um), jnp.where(late, um, zero)], axis=1)
        parts = []
        for w in weights:
            r = dot(lhs, w, ((1,), (1,)))
            parts.append(jnp.where(odd, r[:, nodes:], r[:, :nodes]))
        mapped = choose(parts)
        terms = normal * (mapped - us)
        gap = gap_ref[own, :] + (terms[:GROUP] + terms[GROUP : 2 * GROUP] + terms[2 * GROUP :])
        pressure = PENALTY * jnp.maximum(-gap, 0.0)
        pushed = jnp.concatenate([pressure] * 3, axis=0) * normal
        high = pushed.astype(BF16)
        rest = (pushed - high.astype(F32)).astype(BF16)
        lhs = jnp.concatenate([jnp.where(odd, zero, high), jnp.where(odd, high, zero)], axis=1)
        parts = []
        for w in weights:
            r = dot(lhs, w)
            parts.append(jnp.where(late, r[:, nodes:], r[:, :nodes]))
        back = (-choose(parts)).astype(BF16)
        for c in range(3):
            rows = slice(GROUP * c, GROUP * (c + 1))
            cols = slice(nodes * c, nodes * (c + 1))
            back_ref[own, cols] = back[rows]
            pushed_ref[own, cols] = high[rows]
            pushed_ref[segs + GROUP * g : segs + GROUP * (g + 1), cols] = rest[rows]
    give(1)
    place(dot(take(2)[...], back_ref[...]), scratch, out_ref)
    give(0)


def bulk_kernel(take, out, give, rounded_ref, product_ref):
    out_ref, base_ref, *last_refs = out
    _, layers, blocks, width = out_ref.shape
    rows = layers * blocks
    step = (rows + 2 * blocks) // PARTS
    low_ref, high_ref, field_ref, layer_ref = take(0), take(1), take(2), take(3)
    rounded_ref[:blocks] = low_ref[...]
    rounded_ref[blocks : 2 * blocks] = layer_ref[...].astype(BF16)
    for l in range(1, layers):
        rounded_ref[(l + 1) * blocks : (l + 2) * blocks] = field_ref[0, l].astype(BF16)
    rounded_ref[rows + blocks :] = high_ref[...]
    weight_refs = [take(i) for i in (4, 5, 6)]

    @pl.loop(0, PARTS)
    def multiply(p):
        here = pl.ds(pl.multiple_of(p * step, 16), step)
        part = rounded_ref[here]
        for k, weight_ref in enumerate(weight_refs):
            product_ref[here, k * width : (k + 1) * width] = dot(part, weight_ref[...])

    block = iota((blocks, width), 0)

    def inner(l):
        def product(layer, k):
            return product_ref[pl.ds(pl.multiple_of(layer * blocks, blocks), blocks), k * width : (k + 1) * width]

        side = product(l + 1, 2)
        left = jnp.where(block == 0, 0.0, pltpu.roll(side, 1, 0))
        right = jnp.where(block == blocks - 1, 0.0, pltpu.roll(side, blocks - 1, 0))
        return product(l + 1, 0) + (product(l, 1) + product(l + 2, 1)) + (left + right)

    load_ref, scale_ref = take(7), take(8)

    def stepped(old, l, force):
        return old + scale_ref[0, l].astype(F32) * (load_ref[0, l].astype(F32) - force)

    base_ref[...] = stepped(layer_ref[...], 0, inner(0) + dot(take(10)[...], take(9)[...]))
    give(1)

    @pl.loop(1, layers)
    def update(l):
        out_ref[0, l] = stepped(field_ref[0, l], l, inner(l))

    give(0, (0, pl.ds(1, layers - 1)))
    for last_ref in last_refs:
        last_ref[...] = out_ref[0, layers - 1].astype(BF16)
        give(2)


def summed(take, scratch):
    sums = dot(take(1)[...], gathered(take(0), scratch), ((0,), (0,)))
    base, scale = take(2)[...], take(3)[...].astype(F32)
    blocks = base.shape[0]
    total = sums[:blocks]
    for k in range(1, CAPACITY):
        total = total + sums[k * blocks : (k + 1) * blocks]
    return base - scale * total


def next_kernel(take, out, give, scratch):
    out_ref, layer_ref, high_ref = out
    first = summed(take, scratch)
    layer_ref[...] = first
    give(1)
    surface = first.astype(BF16)
    high_ref[...] = surface
    give(2)
    place(dot(take(1)[...], copies(surface)), scratch, out_ref)
    give(0)


def last_kernel(in_hbm, pick_hbm, base_hbm, scale_hbm, field_hbm, out_hbm, in_ref, pick_ref, base_ref, scale_ref, scratch, layer_ref, sems):
    pairs = [(in_hbm, in_ref), (pick_hbm, pick_ref), (base_hbm, base_ref), (scale_hbm.at[0, 0], scale_ref)]
    loads = {i: pltpu.make_async_copy(source, ref, sems.at[i]) for i, (source, ref) in enumerate(pairs)}
    for load in loads.values():
        load.start()

    def take(i):
        loads[i].wait()
        return pairs[i][1]

    layer_ref[...] = summed(take, scratch)
    store = pltpu.make_async_copy(layer_ref, out_hbm.at[0, 0], sems.at[4])
    store.start()
    store.wait()


def shift(block, step):
    count = lax.axis_size("slab")
    pairs = [(i, i + step) for i in range(count) if 0 <= i + step < count]
    return lax.ppermute(block, "slab", pairs)


def exchange(parts):
    return lax.all_to_all(parts, "dom", 0, 0, tiled=True)


def on_device(
    disp, f_ext, inv_diag, k_self, k_layer, k_side, mortar, gap0, normals, seg_slave, seg_src, seg_master
):
    _, layers, blocks, width = disp.shape
    segs = seg_slave.shape[2]
    count = lax.axis_size("dom")
    slots = count * CAPACITY
    wide = CAPACITY * blocks
    rows_scratch = VMEM((slots, width), F32)
    message = shaped((count, CAPACITY, width), BF16)
    edge = shaped((blocks, width), BF16)
    layer = shaped((blocks, width), F32)

    (asked,) = staged(
        lambda *refs: request_kernel(blocks, *refs), [seg_src, seg_master], [shaped((count, wide), F32)], free_outs=True
    )
    put, get, pick3, back_sum, normal_rows, low, high = staged(
        prep_kernel,
        [seg_src, seg_slave, (normals, (0, 0)), (disp, (0, 0)), (disp, (0, layers - 1))],
        [
            shaped((slots, segs), BF16),
            shaped((segs, slots), BF16),
            shaped((segs, 3 * blocks), BF16),
            shaped((blocks, 2 * segs), BF16),
            shaped((segs, width), F32),
            edge,
            edge,
        ],
        tokens=[asked],
    )
    asked = exchange(asked.reshape(count, 1, wide)).reshape(count, wide)
    pick, sent = staged(
        first_kernel, [asked, (disp, (0, 0))], [shaped((slots, wide), BF16), message], [rows_scratch], tokens=in_hbm(put), loose=(0,)
    )

    def contact(arrived, layer0, low, high):
        pieces = [(mortar, (0, 0, pl.ds(GROUP * g, GROUP))) for g in range(segs // GROUP)]
        return staged(
            contact_kernel,
            [arrived, get, put, pick3, layer0, normal_rows, (gap0, (0, 0))] + pieces,
            [message, shaped((2 * segs, width), BF16)],
            [rows_scratch, VMEM((segs, width), BF16)],
            tokens=[low, high],
        )

    def bulk(field, layer0, low, high, pushed, keep_last):
        outs = [shaped(disp.shape, F32), layer] + ([edge] if keep_last else [])
        rows = (layers + 2) * blocks
        return staged(
            bulk_kernel,
            [low, high, field, layer0, k_self, k_layer, k_side, f_ext, inv_diag, pushed, back_sum],
            outs,
            [VMEM((rows, width), BF16), VMEM((rows, 3 * width), F32)],
            loose=(0, 1),
        )

    arrived = exchange(sent)
    low, high = shift(low, 1), shift(high, -1)
    sent, pushed = contact(arrived, (disp, (0, 0)), low, high)
    returned = exchange(sent)
    field, base, last = bulk(disp, (disp, (0, 0)), low, high, pushed, True)
    sent, layer0, high = staged(
        next_kernel, [returned, pick, base, (inv_diag, (0, 0))], [message, layer, edge], [rows_scratch]
    )
    arrived = exchange(sent)
    low, high = shift(last, 1), shift(high, -1)
    sent, pushed = contact(arrived, layer0, low, high)
    returned = exchange(sent)
    field, base = bulk(field, layer0, low, high, pushed, False)
    return pl.pallas_call(
        last_kernel,
        out_shape=pltpu.HBM(disp.shape, F32),
        in_specs=[HBM] * 5,
        out_specs=HBM,
        scratch_shapes=[
            VMEM(message.shape, BF16),
            VMEM(pick.shape, BF16),
            VMEM(base.shape, F32),
            VMEM(base.shape, BF16),
            rows_scratch,
            VMEM(base.shape, F32),
            pltpu.SemaphoreType.DMA((5,)),
        ],
        input_output_aliases={4: 0},
        compiler_params=pltpu.CompilerParams(vmem_limit_bytes=32 * 2**20),
    )(*in_hbm(returned, pick, base, inv_diag, field))


def solution(mesh):
    in_specs = (
        P("dom", "slab", None, None),
        P("dom", "slab", None, None),
        P("dom", "slab", None, None),
        P(),
        P(),
        P(),
        P("dom", "slab", None, None, None),
        P("dom", "slab", None, None),
        P("dom", "slab", None, None),
        P("dom", "slab", None),
        P("dom", "slab", None),
        P("dom", "slab", None),
    )
    return jax.shard_map(
        on_device, mesh=mesh, in_specs=in_specs, out_specs=P("dom", "slab", None, None), check_vma=False
    )
```

```python
import jax
import jax.numpy as jnp
from jax import lax
from jax.experimental import pallas as pl
from jax.experimental.pallas import tpu as pltpu
from jax.sharding import PartitionSpec as P

PENALTY = 2.0
CAPACITY = 4
GROUP = 16
STREAMS = 4
PARTS = 2
VMEM = pltpu.VMEM
HBM = pl.BlockSpec(memory_space=pltpu.HBM)
ANY = pl.BlockSpec(memory_space=pl.ANY)
BF16 = jnp.bfloat16
F32 = jnp.float32


def dot(a, b, dims=((1,), (0,))):
    return lax.dot_general(a, b, (dims, ((), ())), preferred_element_type=F32)


def iota(shape, axis):
    return lax.broadcasted_iota(jnp.int32, shape, axis)


def shaped(shape, dtype):
    return jax.ShapeDtypeStruct(shape, dtype)


def in_hbm(*arrays):
    return [pltpu.with_memory_space_constraint(array, pltpu.HBM) for array in arrays]


def staged(body, ins, outs, scratch=(), tokens=(), loose=(), free_outs=False, direct=None):
    ins = [item if isinstance(item, tuple) else (item, ()) for item in ins]
    operands = [array if i in loose else in_hbm(array)[0] for i, (array, _) in enumerate(ins)]
    held = [VMEM(part_shape(array, index), array.dtype) for array, index in ins]
    given = [VMEM(out.shape, out.dtype) for out in outs]

    def kernel(*refs):
        refs = list(refs)

        def pop(count):
            taken = refs[:count]
            del refs[:count]
            return taken

        landed = pop(0 if direct is None else 1)
        sources, _, targets = pop(len(ins)), pop(len(tokens)), pop(len(outs))
        inside, leaving, (in_sems, out_sems), extra = pop(len(ins)), pop(len(outs)), pop(2), refs
        loads = {}
        for i, (source, ref, (_, index)) in enumerate(zip(sources, inside, ins)):
            loads[i] = pltpu.make_async_copy(source.at[index] if index else source, ref, in_sems.at[i])
            loads[i].start()

        def take(i):
            if i in loads:
                loads.pop(i).wait()
            return inside[i]

        stores = []

        def give(i, index=None):
            source, target = leaving[i], targets[i]
            if index is not None:
                source, target = source.at[index], target.at[index]
            stores.append(pltpu.make_async_copy(source, target, out_sems.at[i]))
            stores[-1].start()

        body(*landed, take, leaving, give, *extra)
        assert not loads
        for store in stores:
            store.wait()

    sems = [pltpu.SemaphoreType.DMA((len(ins),)), pltpu.SemaphoreType.DMA((len(outs),))]
    first, first_specs = [], []
    if direct is not None:
        first.append(pltpu.with_memory_space_constraint(direct, pltpu.VMEM))
        first_specs.append(pl.BlockSpec(memory_space=VMEM))
    return pl.pallas_call(
        kernel,
        out_shape=tuple(out if free_outs else pltpu.HBM(out.shape, out.dtype) for out in outs),
        in_specs=first_specs + [ANY] * (len(ins) + len(tokens)),
        out_specs=(ANY,) * len(outs),
        scratch_shapes=held + given + sems + list(scratch),
        compiler_params=pltpu.CompilerParams(vmem_limit_bytes=32 * 2**20),
    )(*first, *operands, *tokens)


def part_shape(array, index):
    kept = [i.size for i in index if not isinstance(i, int)]
    return tuple(kept) + array.shape[len(index) :]


def slots_of(src, count):
    segs = src.shape[1]
    named = (iota((count, segs), 0) == src).astype(BF16)
    earlier = (iota((segs, segs), 0) < iota((segs, segs), 1)).astype(BF16)
    before = dot(named, earlier)
    rank = jnp.sum(named.astype(F32) * before, axis=0, keepdims=True).astype(jnp.int32)
    return named, rank


def request_kernel(blocks, take, out, give):
    src, master = take(0)[0], take(1)[0]
    count = out[0].shape[0]
    named, rank = slots_of(src, count)
    segs = named.shape[1]
    wants = (iota((CAPACITY * blocks, segs), 0) == rank * blocks + master).astype(BF16)
    out[0][...] = dot(named, wants, ((1,), (1,)))
    give(0)


def split3(rows):
    high = rows.astype(BF16)
    rest = rows - high.astype(F32)
    mid = rest.astype(BF16)
    low = (rest - mid.astype(F32)).astype(BF16)
    return jnp.concatenate([high, mid, low], axis=0)


def prep_kernel(take, out, give):
    put_ref, get_ref, take_ref, sum_ref, normal_rows_ref, low_ref, high_ref = out
    high_ref[...] = take(3)[...].astype(BF16)
    low_ref[...] = take(4)[...].astype(BF16)
    give(5)
    give(6)
    src, slave, normals = take(0)[0], take(1)[0], take(2)[...]
    blocks = normals.shape[0]
    slots, segs = put_ref.shape
    _, rank = slots_of(src, slots // CAPACITY)
    put = (iota((slots, segs), 0) == src * CAPACITY + rank).astype(F32)
    put_ref[...] = put.astype(BF16)
    give(0)
    get_ref[...] = jnp.transpose(put).astype(BF16)
    give(1)
    spread = (lax.rem(iota((4 * blocks, segs), 0), blocks) == slave).astype(F32)
    pick = jnp.transpose(spread)[:, : 3 * blocks].astype(BF16)
    take_ref[...] = pick
    give(2)
    once = spread[:blocks].astype(BF16)
    sum_ref[...] = jnp.concatenate([once, once], axis=1)
    give(3)
    normal_rows_ref[...] = dot(pick, split3(normals))
    give(4)


def place(rows, scratch, out_ref):
    scratch[...] = rows
    for j in range(out_ref.shape[0] // 2):
        both = scratch[2 * CAPACITY * j : 2 * CAPACITY * (j + 1), :].astype(BF16)
        out_ref[2 * j] = both[:CAPACITY]
        out_ref[2 * j + 1] = both[CAPACITY:]


def gathered(in_ref, scratch):
    for j in range(in_ref.shape[0] // 2):
        both = jnp.concatenate([in_ref[2 * j].astype(F32), in_ref[2 * j + 1].astype(F32)], axis=0)
        scratch[2 * CAPACITY * j : 2 * CAPACITY * (j + 1), :] = both
    return scratch[...].astype(BF16)


def copies(rows):
    return jnp.concatenate([rows] * CAPACITY, axis=0)


def first_kernel(take, out, give, scratch):
    pick_ref, out_ref = out
    slots, wide = pick_ref.shape
    count, blocks = slots // CAPACITY, wide // CAPACITY
    expand = (lax.div(iota((slots, count), 0), CAPACITY) == iota((slots, count), 1)).astype(BF16)
    mine = lax.div(iota((slots, wide), 1), blocks) == lax.rem(iota((slots, wide), 0), CAPACITY)
    rows = dot(expand, take(0)[...].astype(BF16))
    pick = jnp.where(mine, rows, 0.0).astype(BF16)
    pick_ref[...] = pick
    give(0)
    place(dot(pick, copies(take(1)[...].astype(BF16))), scratch, out_ref)
    give(1)


def columns(rows):
    nodes = rows.shape[1] // 3
    return [rows[:, c * nodes : (c + 1) * nodes] for c in range(3)]


def stage_kernel(
    token, mortar_hbm, get_hbm, put_hbm, normal_hbm, gap_hbm, pick_hbm, layer_hbm,
    mortar_ref, get_ref, put_ref, normal_ref, known_ref, gap_ref, pick_ref, layer_ref, sems,
):
    pairs = [(layer_hbm.at[0, 0], layer_ref), (pick_hbm, pick_ref), (normal_hbm, normal_ref), (gap_hbm.at[0, 0], gap_ref)]
    pairs += [(get_hbm, get_ref), (put_hbm, put_ref)]
    part = mortar_ref.shape[0] // STREAMS
    for k in range(STREAMS):
        here = pl.ds(k * part, part)
        pairs.append((mortar_hbm.at[0, 0, here], mortar_ref.at[here]))
    loads = [pltpu.make_async_copy(source, target, sems.at[i]) for i, (source, target) in enumerate(pairs)]
    for load in loads:
        load.start()
    for load in loads[:4]:
        load.wait()
    slave = dot(pick_ref[...], split3(layer_ref[...]))
    x, y, z = columns(normal_ref[...] * slave)
    known_ref[...] = gap_ref[...] - (x + y + z)
    for load in loads[4:]:
        load.wait()


def contact_kernel(
    in_ref, mortar_ref, get_ref, put_ref, normal_ref, known_ref, low_token, high_token,
    out_hbm, pushed_hbm, scratch, back_ref, out_ref, pushed_ref, sems,
):
    segs, _, nodes = mortar_ref.shape
    member = lax.rem(iota((3 * GROUP, nodes), 0), GROUP)
    place_in = lax.rem(member, 4)
    block_of = lax.div(member, 4)
    odd = lax.rem(place_in, 2) == 1
    late = place_in >= 2
    zero = jnp.zeros((3 * GROUP, nodes), BF16)
    master = dot(get_ref[...], gathered(in_ref, scratch)).astype(BF16)

    def choose(parts):
        result = parts[0]
        for b in range(1, GROUP // 4):
            result = jnp.where(block_of == b, parts[b], result)
        return result

    for g in range(segs // GROUP):
        own = slice(GROUP * g, GROUP * (g + 1))
        um = jnp.concatenate(columns(master[own]), axis=0)
        normal = jnp.concatenate(columns(normal_ref[own, :]), axis=0)
        weights = []
        for s in range(GROUP * g, GROUP * (g + 1), 4):
            left = mortar_ref[s : s + 2].reshape(2 * nodes, nodes)
            right = mortar_ref[s + 2 : s + 4].reshape(2 * nodes, nodes)
            weights.append(jnp.concatenate([left, right], axis=1))
        lhs = jnp.concatenate([jnp.where(late, zero, um), jnp.where(late, um, zero)], axis=1)
        parts = []
        for w in weights:
            r = dot(lhs, w, ((1,), (1,)))
            parts.append(jnp.where(odd, r[:, nodes:], r[:, :nodes]))
        terms = normal * choose(parts)
        gap = known_ref[own, :] + (terms[:GROUP] + terms[GROUP : 2 * GROUP] + terms[2 * GROUP :])
        pressure = PENALTY * jnp.maximum(-gap, 0.0)
        pushed = jnp.concatenate([pressure] * 3, axis=0) * normal
        high = pushed.astype(BF16)
        rest = (pushed - high.astype(F32)).astype(BF16)
        lhs = jnp.concatenate([jnp.where(odd, zero, high), jnp.where(odd, high, zero)], axis=1)
        parts = []
        for w in weights:
            r = dot(lhs, w)
            parts.append(jnp.where(late, r[:, nodes:], r[:, :nodes]))
        back = (-choose(parts)).astype(BF16)
        for c in range(3):
            rows = slice(GROUP * c, GROUP * (c + 1))
            cols = slice(nodes * c, nodes * (c + 1))
            back_ref[own, cols] = back[rows]
            pushed_ref[own, cols] = high[rows]
            pushed_ref[segs + GROUP * g : segs + GROUP * (g + 1), cols] = rest[rows]
    store = pltpu.make_async_copy(pushed_ref, pushed_hbm, sems.at[0])
    store.start()
    place(dot(put_ref[...], back_ref[...]), scratch, out_ref)
    send = pltpu.make_async_copy(out_ref, out_hbm, sems.at[1])
    send.start()
    store.wait()
    send.wait()


def bulk_kernel(take, out, give, rounded_ref, product_ref):
    out_ref, base_ref, *last_refs = out
    _, layers, blocks, width = out_ref.shape
    rows = layers * blocks
    step = (rows + 2 * blocks) // PARTS
    low_ref, high_ref, field_ref, layer_ref = take(0), take(1), take(2), take(3)
    rounded_ref[:blocks] = low_ref[...]
    rounded_ref[blocks : 2 * blocks] = layer_ref[...].astype(BF16)
    for l in range(1, layers):
        rounded_ref[(l + 1) * blocks : (l + 2) * blocks] = field_ref[0, l].astype(BF16)
    rounded_ref[rows + blocks :] = high_ref[...]
    weight_refs = [take(i) for i in (4, 5, 6)]

    @pl.loop(0, PARTS)
    def multiply(p):
        here = pl.ds(pl.multiple_of(p * step, 16), step)
        part = rounded_ref[here]
        for k, weight_ref in enumerate(weight_refs):
            product_ref[here, k * width : (k + 1) * width] = dot(part, weight_ref[...])

    block = iota((blocks, width), 0)

    def inner(l):
        def product(layer, k):
            return product_ref[pl.ds(pl.multiple_of(layer * blocks, blocks), blocks), k * width : (k + 1) * width]

        side = product(l + 1, 2)
        left = jnp.where(block == 0, 0.0, pltpu.roll(side, 1, 0))
        right = jnp.where(block == blocks - 1, 0.0, pltpu.roll(side, blocks - 1, 0))
        return product(l + 1, 0) + (product(l, 1) + product(l + 2, 1)) + (left + right)

    load_ref, scale_ref = take(7), take(8)

    def stepped(old, l, force):
        return old + scale_ref[0, l].astype(F32) * (load_ref[0, l].astype(F32) - force)

    base_ref[...] = stepped(layer_ref[...], 0, inner(0) + dot(take(10)[...], take(9)[...]))
    give(1)

    @pl.loop(1, layers)
    def update(l):
        out_ref[0, l] = stepped(field_ref[0, l], l, inner(l))

    give(0, (0, pl.ds(1, layers - 1)))
    for last_ref in last_refs:
        last_ref[...] = out_ref[0, layers - 1].astype(BF16)
        give(2)


def summed(in_ref, take, scratch):
    arrived = gathered(in_ref, scratch)
    sums = dot(take(0)[...], arrived, ((0,), (0,)))
    base, scale = take(1)[...], take(2)[...].astype(F32)
    blocks = base.shape[0]
    total = sums[:blocks]
    for k in range(1, CAPACITY):
        total = total + sums[k * blocks : (k + 1) * blocks]
    return base - scale * total


def next_kernel(in_ref, take, out, give, scratch):
    out_ref, layer_ref, high_ref = out
    first = summed(in_ref, take, scratch)
    layer_ref[0, 0] = first
    give(1)
    surface = first.astype(BF16)
    high_ref[...] = surface
    give(2)
    place(dot(take(0)[...], copies(surface)), scratch, out_ref)
    give(0)


def last_kernel(in_ref, pick_hbm, base_hbm, scale_hbm, field_hbm, out_hbm, pick_ref, base_ref, scale_ref, scratch, layer_ref, sems):
    pairs = [(pick_hbm, pick_ref), (base_hbm, base_ref), (scale_hbm.at[0, 0], scale_ref)]
    loads = {i: pltpu.make_async_copy(source, ref, sems.at[i]) for i, (source, ref) in enumerate(pairs)}
    for load in loads.values():
        load.start()

    def take(i):
        loads[i].wait()
        return pairs[i][1]

    layer_ref[...] = summed(in_ref, take, scratch)
    store = pltpu.make_async_copy(layer_ref, out_hbm.at[0, 0], sems.at[3])
    store.start()
    store.wait()


def shift(block, step):
    count = lax.axis_size("slab")
    pairs = [(i, i + step) for i in range(count) if 0 <= i + step < count]
    return lax.ppermute(block, "slab", pairs)


def exchange(parts):
    return lax.all_to_all(parts, "dom", 0, 0, tiled=True)


def on_device(
    disp, f_ext, inv_diag, k_self, k_layer, k_side, mortar, gap0, normals, seg_slave, seg_src, seg_master
):
    _, layers, blocks, width = disp.shape
    segs = seg_slave.shape[2]
    count = lax.axis_size("dom")
    slots = count * CAPACITY
    wide = CAPACITY * blocks
    rows_scratch = VMEM((slots, width), F32)
    message = shaped((count, CAPACITY, width), BF16)
    edge = shaped((blocks, width), BF16)
    layer = shaped((blocks, width), F32)

    (asked,) = staged(
        lambda *refs: request_kernel(blocks, *refs), [seg_src, seg_master], [shaped((count, wide), F32)], free_outs=True
    )
    put, get, pick3, back_sum, normal_rows, low, high = staged(
        prep_kernel,
        [seg_src, seg_slave, (normals, (0, 0)), (disp, (0, 0)), (disp, (0, layers - 1))],
        [
            shaped((slots, segs), BF16),
            shaped((segs, slots), BF16),
            shaped((segs, 3 * blocks), BF16),
            shaped((blocks, 2 * segs), BF16),
            shaped((segs, width), F32),
            edge,
            edge,
        ],
        tokens=[asked],
    )
    asked = exchange(asked.reshape(count, 1, wide)).reshape(count, wide)
    pick, sent = staged(
        first_kernel, [asked, (disp, (0, 0))], [shaped((slots, wide), BF16), message], [rows_scratch], tokens=in_hbm(put), loose=(0,)
    )

    def stage(token, layer0):
        held = [
            pltpu.VMEM(mortar.shape[2:], BF16),
            pltpu.VMEM(get.shape, BF16),
            pltpu.VMEM(put.shape, BF16),
            pltpu.VMEM(normal_rows.shape, F32),
            pltpu.VMEM(gap0.shape[2:], F32),
        ]
        return pl.pallas_call(
            stage_kernel,
            out_shape=held,
            in_specs=[ANY] * 8,
            out_specs=[pl.BlockSpec(memory_space=VMEM)] * 5,
            scratch_shapes=[
                VMEM(gap0.shape[2:], F32),
                VMEM(pick3.shape, BF16),
                VMEM((blocks, width), F32),
                pltpu.SemaphoreType.DMA((6 + STREAMS,)),
            ],
            compiler_params=pltpu.CompilerParams(vmem_limit_bytes=16 * 2**20),
        )(*in_hbm(token, mortar, get, put, normal_rows, gap0, pick3, layer0))

    def contact(arrived, staged_arrays, low, high):
        ready = [pltpu.with_memory_space_constraint(array, pltpu.VMEM) for array in (arrived, *staged_arrays)]
        pushed = shaped((2 * segs, width), BF16)
        return pl.pallas_call(
            contact_kernel,
            out_shape=[pltpu.HBM(message.shape, BF16), pltpu.HBM(pushed.shape, BF16)],
            in_specs=[pl.BlockSpec(memory_space=VMEM)] * 6 + [ANY] * 2,
            out_specs=[ANY] * 2,
            scratch_shapes=[
                rows_scratch,
                VMEM((segs, width), BF16),
                VMEM(message.shape, BF16),
                VMEM(pushed.shape, BF16),
                pltpu.SemaphoreType.DMA((2,)),
            ],
            compiler_params=pltpu.CompilerParams(vmem_limit_bytes=16 * 2**20),
        )(*ready, low, high)

    def bulk(field, layer0, low, high, pushed, keep_last):
        outs = [shaped(disp.shape, F32), layer] + ([edge] if keep_last else [])
        rows = (layers + 2) * blocks
        return staged(
            bulk_kernel,
            [low, high, field, layer0, k_self, k_layer, k_side, f_ext, inv_diag, pushed, back_sum],
            outs,
            [VMEM((rows, width), BF16), VMEM((rows, 3 * width), F32)],
            loose=(0, 1),
        )

    arrived = exchange(sent)
    low, high = shift(low, 1), shift(high, -1)
    sent, pushed = contact(arrived, stage(pick, disp), low, high)
    returned = exchange(sent)
    field, base, last = bulk(disp, (disp, (0, 0)), low, high, pushed, True)
    sent, layer0, high = staged(
        next_kernel, [pick, base, (inv_diag, (0, 0))], [message, shaped((1, 1, blocks, width), F32), edge], [rows_scratch], direct=returned
    )
    arrived = exchange(sent)
    low, high = shift(last, 1), shift(high, -1)
    sent, pushed = contact(arrived, stage(pick, layer0), low, high)
    returned = exchange(sent)
    field, base = bulk(field, (layer0, (0, 0)), low, high, pushed, False)
    return pl.pallas_call(
        last_kernel,
        out_shape=pltpu.HBM(disp.shape, F32),
        in_specs=[pl.BlockSpec(memory_space=VMEM)] + [HBM] * 4,
        out_specs=HBM,
        scratch_shapes=[
            VMEM(pick.shape, BF16),
            VMEM(base.shape, F32),
            VMEM(base.shape, BF16),
            rows_scratch,
            VMEM(base.shape, F32),
            pltpu.SemaphoreType.DMA((4,)),
        ],
        input_output_aliases={4: 0},
        compiler_params=pltpu.CompilerParams(vmem_limit_bytes=32 * 2**20),
    )(pltpu.with_memory_space_constraint(returned, pltpu.VMEM), *in_hbm(pick, base, inv_diag, field))


def solution(mesh):
    in_specs = (
        P("dom", "slab", None, None),
        P("dom", "slab", None, None),
        P("dom", "slab", None, None),
        P(),
        P(),
        P(),
        P("dom", "slab", None, None, None),
        P("dom", "slab", None, None),
        P("dom", "slab", None, None),
        P("dom", "slab", None),
        P("dom", "slab", None),
        P("dom", "slab", None),
    )
    return jax.shard_map(
        on_device, mesh=mesh, in_specs=in_specs, out_specs=P("dom", "slab", None, None), check_vma=False
    )
```

```python
import jax
import jax.numpy as jnp
from jax import lax
from jax.experimental import pallas as pl
from jax.experimental.pallas import tpu as pltpu
from jax.sharding import PartitionSpec as P

PENALTY = 2.0
CAPACITY = 4
GROUP = 16
STREAMS = 4
PARTS = 2
VMEM = pltpu.VMEM
HBM = pl.BlockSpec(memory_space=pltpu.HBM)
ANY = pl.BlockSpec(memory_space=pl.ANY)
IN_VMEM = pl.BlockSpec(memory_space=VMEM)
BF16 = jnp.bfloat16
F32 = jnp.float32


def dot(a, b, dims=((1,), (0,))):
    return lax.dot_general(a, b, (dims, ((), ())), preferred_element_type=F32)


def iota(shape, axis):
    return lax.broadcasted_iota(jnp.int32, shape, axis)


def shaped(shape, dtype):
    return jax.ShapeDtypeStruct(shape, dtype)


def in_hbm(*arrays):
    return [pltpu.with_memory_space_constraint(array, pltpu.HBM) for array in arrays]


def staged(body, ins, outs, scratch=(), tokens=(), loose=(), free_outs=False, direct=(), kept=()):
    ins = [item if isinstance(item, tuple) else (item, ()) for item in ins]
    operands = [array if i in loose else in_hbm(array)[0] for i, (array, _) in enumerate(ins)]
    held = [VMEM(part_shape(array, index), array.dtype) for array, index in ins]
    given = [VMEM(out.shape, out.dtype) for i, out in enumerate(outs) if i not in kept]
    here = [pltpu.with_memory_space_constraint(array, pltpu.VMEM) for array in direct]

    def kernel(*refs):
        refs = list(refs)

        def pop(count):
            taken = refs[:count]
            del refs[:count]
            return taken

        landed, sources, _, targets = pop(len(here)), pop(len(ins)), pop(len(tokens)), pop(len(outs))
        inside, leaving, (in_sems, out_sems), extra = pop(len(ins)), pop(len(given)), pop(2), refs
        leaving = [targets[i] if i in kept else leaving.pop(0) for i in range(len(outs))]
        loads = {}
        for i, (source, ref, (_, index)) in enumerate(zip(sources, inside, ins)):
            loads[i] = pltpu.make_async_copy(source.at[index] if index else source, ref, in_sems.at[i])
            loads[i].start()

        def take(i):
            if i in loads:
                loads.pop(i).wait()
            return inside[i]

        stores = []

        def give(i, index=None):
            source, target = leaving[i], targets[i]
            if index is not None:
                source, target = source.at[index], target.at[index]
            stores.append(pltpu.make_async_copy(source, target, out_sems.at[i]))
            stores[-1].start()

        body(*landed, take, leaving, give, *extra)
        assert not loads
        for store in stores:
            store.wait()

    def space(i, out):
        return out if free_outs else (pltpu.VMEM if i in kept else pltpu.HBM)(out.shape, out.dtype)

    return pl.pallas_call(
        kernel,
        out_shape=tuple(space(i, out) for i, out in enumerate(outs)),
        in_specs=[IN_VMEM] * len(here) + [ANY] * (len(ins) + len(tokens)),
        out_specs=tuple(IN_VMEM if i in kept else ANY for i in range(len(outs))),
        scratch_shapes=held
        + given
        + [pltpu.SemaphoreType.DMA((max(len(ins), 1),)), pltpu.SemaphoreType.DMA((len(outs),))]
        + list(scratch),
        compiler_params=pltpu.CompilerParams(vmem_limit_bytes=32 * 2**20),
    )(*here, *operands, *tokens)


def part_shape(array, index):
    kept = [i.size for i in index if not isinstance(i, int)]
    return tuple(kept) + array.shape[len(index) :]


def slots_of(src, count):
    segs = src.shape[1]
    named = (iota((count, segs), 0) == src).astype(BF16)
    earlier = (iota((segs, segs), 0) < iota((segs, segs), 1)).astype(BF16)
    before = dot(named, earlier)
    rank = jnp.sum(named.astype(F32) * before, axis=0, keepdims=True).astype(jnp.int32)
    return named, rank


def request_kernel(blocks, take, out, give):
    src, master = take(0)[0], take(1)[0]
    count = out[0].shape[0]
    named, rank = slots_of(src, count)
    segs = named.shape[1]
    wants = (iota((CAPACITY * blocks, segs), 0) == rank * blocks + master).astype(BF16)
    out[0][...] = dot(named, wants, ((1,), (1,)))
    give(0)


def split3(rows):
    high = rows.astype(BF16)
    rest = rows - high.astype(F32)
    mid = rest.astype(BF16)
    low = (rest - mid.astype(F32)).astype(BF16)
    return jnp.concatenate([high, mid, low], axis=0)


def prep_kernel(take, out, give):
    put_ref, get_ref, take_ref, sum_ref, normal_rows_ref, low_ref, high_ref, surface_ref = out
    surface = take(3)[...].astype(BF16)
    surface_ref[...] = copies(surface)
    high_ref[...] = surface
    low_ref[...] = take(4)[...].astype(BF16)
    give(5)
    give(6)
    src, slave, normals = take(0)[0], take(1)[0], take(2)[...]
    blocks = normals.shape[0]
    slots, segs = put_ref.shape
    _, rank = slots_of(src, slots // CAPACITY)
    put = (iota((slots, segs), 0) == src * CAPACITY + rank).astype(F32)
    put_ref[...] = put.astype(BF16)
    give(0)
    get_ref[...] = jnp.transpose(put).astype(BF16)
    give(1)
    spread = (lax.rem(iota((4 * blocks, segs), 0), blocks) == slave).astype(F32)
    pick = jnp.transpose(spread)[:, : 3 * blocks].astype(BF16)
    take_ref[...] = pick
    give(2)
    once = spread[:blocks].astype(BF16)
    sum_ref[...] = jnp.concatenate([once, once], axis=1)
    give(3)
    normal_rows_ref[...] = dot(pick, split3(normals))
    give(4)


def place(rows, scratch, out_ref):
    scratch[...] = rows
    for j in range(out_ref.shape[0] // 2):
        both = scratch[2 * CAPACITY * j : 2 * CAPACITY * (j + 1), :].astype(BF16)
        out_ref[2 * j] = both[:CAPACITY]
        out_ref[2 * j + 1] = both[CAPACITY:]


def gathered(in_ref, scratch):
    for j in range(in_ref.shape[0] // 2):
        both = jnp.concatenate([in_ref[2 * j].astype(F32), in_ref[2 * j + 1].astype(F32)], axis=0)
        scratch[2 * CAPACITY * j : 2 * CAPACITY * (j + 1), :] = both
    return scratch[...].astype(BF16)


def copies(rows):
    return jnp.concatenate([rows] * CAPACITY, axis=0)


def first_kernel(asked_ref, surface_ref, take, out, give, scratch):
    pick_ref, out_ref = out
    slots, wide = pick_ref.shape
    count, blocks = slots // CAPACITY, wide // CAPACITY
    expand = (lax.div(iota((slots, count), 0), CAPACITY) == iota((slots, count), 1)).astype(BF16)
    mine = lax.div(iota((slots, wide), 1), blocks) == lax.rem(iota((slots, wide), 0), CAPACITY)
    rows = dot(expand, asked_ref[...].astype(BF16))
    pick = jnp.where(mine, rows, 0.0).astype(BF16)
    pick_ref[...] = pick
    give(0)
    place(dot(pick, surface_ref[...]), scratch, out_ref)
    give(1)


def columns(rows):
    nodes = rows.shape[1] // 3
    return [rows[:, c * nodes : (c + 1) * nodes] for c in range(3)]


def stage_kernel(
    token, mortar_hbm, get_hbm, put_hbm, normal_hbm, gap_hbm, pick_hbm, layer_hbm,
    mortar_ref, get_ref, put_ref, normal_ref, known_ref, gap_ref, pick_ref, layer_ref, sems,
):
    pairs = [(layer_hbm.at[0, 0], layer_ref), (pick_hbm, pick_ref), (normal_hbm, normal_ref), (gap_hbm.at[0, 0], gap_ref)]
    pairs += [(get_hbm, get_ref), (put_hbm, put_ref)]
    part = mortar_ref.shape[0] // STREAMS
    for k in range(STREAMS):
        here = pl.ds(k * part, part)
        pairs.append((mortar_hbm.at[0, 0, here], mortar_ref.at[here]))
    loads = [pltpu.make_async_copy(source, target, sems.at[i]) for i, (source, target) in enumerate(pairs)]
    for load in loads:
        load.start()
    for load in loads[:4]:
        load.wait()
    slave = dot(pick_ref[...], split3(layer_ref[...]))
    x, y, z = columns(normal_ref[...] * slave)
    known_ref[...] = gap_ref[...] - (x + y + z)
    for load in loads[4:]:
        load.wait()


def contact_kernel(
    in_ref, early_ref, get_ref, put_ref, normal_ref, known_ref, mortar_hbm, low_token, high_token,
    out_hbm, pushed_hbm, scratch, back_ref, out_ref, pushed_ref, later_ref, sems, later_sems,
):
    early, _, nodes = early_ref.shape
    segs = early + later_ref.shape[0]
    later = []
    for k in range(0, segs - early, GROUP):
        copy = pltpu.make_async_copy(
            mortar_hbm.at[0, 0, pl.ds(early + k, GROUP)], later_ref.at[pl.ds(k, GROUP)], later_sems.at[k // GROUP]
        )
        copy.start()
        later.append(copy)
    member = lax.rem(iota((3 * GROUP, nodes), 0), GROUP)
    place_in = lax.rem(member, 4)
    block_of = lax.div(member, 4)
    odd = lax.rem(place_in, 2) == 1
    late = place_in >= 2
    zero = jnp.zeros((3 * GROUP, nodes), BF16)
    master = dot(get_ref[...], gathered(in_ref, scratch)).astype(BF16)

    def choose(parts):
        result = parts[0]
        for b in range(1, GROUP // 4):
            result = jnp.where(block_of == b, parts[b], result)
        return result

    for g in range(segs // GROUP):
        own = slice(GROUP * g, GROUP * (g + 1))
        um = jnp.concatenate(columns(master[own]), axis=0)
        normal = jnp.concatenate(columns(normal_ref[own, :]), axis=0)
        mortar_ref, start = early_ref, GROUP * g
        if start >= early:
            mortar_ref, start = later_ref, start - early
            later[start // GROUP].wait()
        weights = []
        for s in range(start, start + GROUP, 4):
            left = mortar_ref[s : s + 2].reshape(2 * nodes, nodes)
            right = mortar_ref[s + 2 : s + 4].reshape(2 * nodes, nodes)
            weights.append(jnp.concatenate([left, right], axis=1))
        lhs = jnp.concatenate([jnp.where(late, zero, um), jnp.where(late, um, zero)], axis=1)
        parts = []
        for w in weights:
            r = dot(lhs, w, ((1,), (1,)))
            parts.append(jnp.where(odd, r[:, nodes:], r[:, :nodes]))
        terms = normal * choose(parts)
        gap = known_ref[own, :] + (terms[:GROUP] + terms[GROUP : 2 * GROUP] + terms[2 * GROUP :])
        pressure = PENALTY * jnp.maximum(-gap, 0.0)
        pushed = jnp.concatenate([pressure] * 3, axis=0) * normal
        high = pushed.astype(BF16)
        rest = (pushed - high.astype(F32)).astype(BF16)
        lhs = jnp.concatenate([jnp.where(odd, zero, high), jnp.where(odd, high, zero)], axis=1)
        parts = []
        for w in weights:
            r = dot(lhs, w)
            parts.append(jnp.where(late, r[:, nodes:], r[:, :nodes]))
        back = (-choose(parts)).astype(BF16)
        for c in range(3):
            rows = slice(GROUP * c, GROUP * (c + 1))
            cols = slice(nodes * c, nodes * (c + 1))
            back_ref[own, cols] = back[rows]
            pushed_ref[own, cols] = high[rows]
            pushed_ref[segs + GROUP * g : segs + GROUP * (g + 1), cols] = rest[rows]
    store = pltpu.make_async_copy(pushed_ref, pushed_hbm, sems.at[0])
    store.start()
    place(dot(put_ref[...], back_ref[...]), scratch, out_ref)
    send = pltpu.make_async_copy(out_ref, out_hbm, sems.at[1])
    send.start()
    store.wait()
    send.wait()


def bulk_kernel(take, out, give, rounded_ref, product_ref):
    out_ref, base_ref, near_ref, pick_ref, *last_refs = out
    pick_ref[...] = take(11)[...]
    _, layers, blocks, width = out_ref.shape
    rows = layers * blocks
    step = (rows + 2 * blocks) // PARTS
    low_ref, high_ref, field_ref, layer_ref = take(0), take(1), take(2), take(3)
    rounded_ref[:blocks] = low_ref[...]
    rounded_ref[blocks : 2 * blocks] = layer_ref[...].astype(BF16)
    for l in range(1, layers):
        rounded_ref[(l + 1) * blocks : (l + 2) * blocks] = field_ref[0, l].astype(BF16)
    rounded_ref[rows + blocks :] = high_ref[...]
    weight_refs = [take(i) for i in (4, 5, 6)]

    @pl.loop(0, PARTS)
    def multiply(p):
        here = pl.ds(pl.multiple_of(p * step, 16), step)
        part = rounded_ref[here]
        for k, weight_ref in enumerate(weight_refs):
            product_ref[here, k * width : (k + 1) * width] = dot(part, weight_ref[...])

    block = iota((blocks, width), 0)

    def inner(l):
        def product(layer, k):
            return product_ref[pl.ds(pl.multiple_of(layer * blocks, blocks), blocks), k * width : (k + 1) * width]

        side = product(l + 1, 2)
        left = jnp.where(block == 0, 0.0, pltpu.roll(side, 1, 0))
        right = jnp.where(block == blocks - 1, 0.0, pltpu.roll(side, blocks - 1, 0))
        return product(l + 1, 0) + (product(l, 1) + product(l + 2, 1)) + (left + right)

    load_ref, scale_ref = take(7), take(8)

    def stepped(old, l, force):
        return old + scale_ref[0, l].astype(F32) * (load_ref[0, l].astype(F32) - force)

    base_ref[...] = stepped(layer_ref[...], 0, inner(0) + dot(take(10)[...], take(9)[...]))
    near_ref[...] = scale_ref[0, 0].astype(F32)

    @pl.loop(1, layers)
    def update(l):
        out_ref[0, l] = stepped(field_ref[0, l], l, inner(l))

    give(0, (0, pl.ds(1, layers - 1)))
    for last_ref in last_refs:
        last_ref[...] = out_ref[0, layers - 1].astype(BF16)
        give(4)


def summed(in_ref, pick_ref, base_ref, scale_ref, scratch):
    sums = dot(pick_ref[...], gathered(in_ref, scratch), ((0,), (0,)))
    blocks = base_ref.shape[0]
    total = sums[:blocks]
    for k in range(1, CAPACITY):
        total = total + sums[k * blocks : (k + 1) * blocks]
    return base_ref[...] - scale_ref[...] * total


def next_kernel(in_ref, pick_ref, base_ref, scale_ref, take, out, give, scratch):
    out_ref, layer_ref, high_ref = out
    first = summed(in_ref, pick_ref, base_ref, scale_ref, scratch)
    layer_ref[0, 0] = first
    give(1)
    surface = first.astype(BF16)
    high_ref[...] = surface
    give(2)
    place(dot(pick_ref[...], copies(surface)), scratch, out_ref)
    give(0)


def last_kernel(in_ref, pick_ref, base_ref, scale_ref, field_hbm, out_hbm, scratch, layer_ref, sem):
    layer_ref[...] = summed(in_ref, pick_ref, base_ref, scale_ref, scratch)
    store = pltpu.make_async_copy(layer_ref, out_hbm.at[0, 0], sem)
    store.start()
    store.wait()


def shift(block, step):
    count = lax.axis_size("slab")
    pairs = [(i, i + step) for i in range(count) if 0 <= i + step < count]
    return lax.ppermute(block, "slab", pairs)


def exchange(parts):
    return lax.all_to_all(parts, "dom", 0, 0, tiled=True)


def on_device(
    disp, f_ext, inv_diag, k_self, k_layer, k_side, mortar, gap0, normals, seg_slave, seg_src, seg_master
):
    _, layers, blocks, width = disp.shape
    segs = seg_slave.shape[2]
    count = lax.axis_size("dom")
    slots = count * CAPACITY
    wide = CAPACITY * blocks
    rows_scratch = VMEM((slots, width), F32)
    message = shaped((count, CAPACITY, width), BF16)
    edge = shaped((blocks, width), BF16)
    layer = shaped((blocks, width), F32)

    (asked,) = staged(
        lambda *refs: request_kernel(blocks, *refs), [seg_src, seg_master], [shaped((count, wide), F32)], free_outs=True
    )
    put, get, pick3, back_sum, normal_rows, low, high, surface = staged(
        prep_kernel,
        [seg_src, seg_slave, (normals, (0, 0)), (disp, (0, 0)), (disp, (0, layers - 1))],
        [
            shaped((slots, segs), BF16),
            shaped((segs, slots), BF16),
            shaped((segs, 3 * blocks), BF16),
            shaped((blocks, 2 * segs), BF16),
            shaped((segs, width), F32),
            edge,
            edge,
            shaped((CAPACITY * blocks, width), BF16),
        ],
        tokens=[asked],
        kept=(7,),
    )
    asked = exchange(asked.reshape(count, 1, wide)).reshape(count, wide)
    pick, sent = staged(
        first_kernel, [], [shaped((slots, wide), BF16), message], [rows_scratch], direct=(asked, surface)
    )

    early = max(segs // 2, GROUP)

    def stage(token, layer0):
        held = [
            pltpu.VMEM((early,) + mortar.shape[3:], BF16),
            pltpu.VMEM(get.shape, BF16),
            pltpu.VMEM(put.shape, BF16),
            pltpu.VMEM(normal_rows.shape, F32),
            pltpu.VMEM(gap0.shape[2:], F32),
        ]
        return pl.pallas_call(
            stage_kernel,
            out_shape=held,
            in_specs=[ANY] * 8,
            out_specs=[IN_VMEM] * 5,
            scratch_shapes=[
                VMEM(gap0.shape[2:], F32),
                VMEM(pick3.shape, BF16),
                VMEM((blocks, width), F32),
                pltpu.SemaphoreType.DMA((6 + STREAMS,)),
            ],
            compiler_params=pltpu.CompilerParams(vmem_limit_bytes=16 * 2**20),
        )(*in_hbm(token, mortar, get, put, normal_rows, gap0, pick3, layer0))

    def contact(arrived, staged_arrays, low, high):
        ready = [pltpu.with_memory_space_constraint(array, pltpu.VMEM) for array in (arrived, *staged_arrays)]
        pushed = shaped((2 * segs, width), BF16)
        return pl.pallas_call(
            contact_kernel,
            out_shape=[pltpu.HBM(message.shape, BF16), pltpu.HBM(pushed.shape, BF16)],
            in_specs=[IN_VMEM] * 6 + [ANY] * 3,
            out_specs=[ANY] * 2,
            scratch_shapes=[
                rows_scratch,
                VMEM((segs, width), BF16),
                VMEM(message.shape, BF16),
                VMEM(pushed.shape, BF16),
                VMEM((segs - early,) + mortar.shape[3:], BF16),
                pltpu.SemaphoreType.DMA((2,)),
                pltpu.SemaphoreType.DMA(((segs - early) // GROUP,)),
            ],
            compiler_params=pltpu.CompilerParams(vmem_limit_bytes=16 * 2**20),
        )(*ready, *in_hbm(mortar), low, high)

    def bulk(field, layer0, low, high, pushed, keep_last):
        outs = [shaped(disp.shape, F32), layer, layer, shaped(pick.shape, BF16)] + ([edge] if keep_last else [])
        rows = (layers + 2) * blocks
        return staged(
            bulk_kernel,
            [low, high, field, layer0, k_self, k_layer, k_side, f_ext, inv_diag, pushed, back_sum, pick],
            outs,
            [VMEM((rows, width), BF16), VMEM((rows, 3 * width), F32)],
            loose=(0, 1),
            kept=(1, 2, 3),
        )

    arrived = exchange(sent)
    low, high = shift(low, 1), shift(high, -1)
    sent, pushed = contact(arrived, stage(pick, disp), low, high)
    returned = exchange(sent)
    field, base, scale, near, last = bulk(disp, (disp, (0, 0)), low, high, pushed, True)
    sent, layer0, high = staged(
        next_kernel, [], [message, shaped((1, 1, blocks, width), F32), edge], [rows_scratch], direct=(returned, near, base, scale)
    )
    arrived = exchange(sent)
    low, high = shift(last, 1), shift(high, -1)
    sent, pushed = contact(arrived, stage(pick, layer0), low, high)
    returned = exchange(sent)
    field, base, scale, near = bulk(field, (layer0, (0, 0)), low, high, pushed, False)
    return pl.pallas_call(
        last_kernel,
        out_shape=pltpu.HBM(disp.shape, F32),
        in_specs=[IN_VMEM] * 4 + [HBM],
        out_specs=HBM,
        scratch_shapes=[rows_scratch, VMEM(base.shape, F32), pltpu.SemaphoreType.DMA],
        input_output_aliases={4: 0},
        compiler_params=pltpu.CompilerParams(vmem_limit_bytes=16 * 2**20),
    )(
        *[pltpu.with_memory_space_constraint(array, pltpu.VMEM) for array in (returned, near, base, scale)],
        *in_hbm(field),
    )


def solution(mesh):
    in_specs = (
        P("dom", "slab", None, None),
        P("dom", "slab", None, None),
        P("dom", "slab", None, None),
        P(),
        P(),
        P(),
        P("dom", "slab", None, None, None),
        P("dom", "slab", None, None),
        P("dom", "slab", None, None),
        P("dom", "slab", None),
        P("dom", "slab", None),
        P("dom", "slab", None),
    )
    return jax.shard_map(
        on_device, mesh=mesh, in_specs=in_specs, out_specs=P("dom", "slab", None, None), check_vma=False
    )
```

```python
import jax
import jax.numpy as jnp
from jax import lax
from jax.experimental import pallas as pl
from jax.experimental.pallas import tpu as pltpu
from jax.sharding import PartitionSpec as P

PENALTY = 2.0
CAPACITY = 4
GROUP = 16
PIECES = 4
PARTS = 2
VMEM = pltpu.VMEM
HBM = pl.BlockSpec(memory_space=pltpu.HBM)
ANY = pl.BlockSpec(memory_space=pl.ANY)
IN_VMEM = pl.BlockSpec(memory_space=VMEM)
BF16 = jnp.bfloat16
F32 = jnp.float32


def dot(a, b, dims=((1,), (0,))):
    return lax.dot_general(a, b, (dims, ((), ())), preferred_element_type=F32)


def iota(shape, axis):
    return lax.broadcasted_iota(jnp.int32, shape, axis)


def shaped(shape, dtype):
    return jax.ShapeDtypeStruct(shape, dtype)


def in_hbm(*arrays):
    return [pltpu.with_memory_space_constraint(array, pltpu.HBM) for array in arrays]


def staged(body, ins, outs, scratch=(), tokens=(), loose=(), free_outs=False, direct=(), kept=(), fills=()):
    ins = [item if isinstance(item, tuple) else (item, ()) for item in ins]
    operands = [array if i in loose else in_hbm(array)[0] for i, (array, _) in enumerate(ins)]
    held = [VMEM(part_shape(array, index), array.dtype) for array, index in ins]
    given = [VMEM(out.shape, out.dtype) for i, out in enumerate(outs) if i not in kept]
    here = [pltpu.with_memory_space_constraint(array, pltpu.VMEM) for array in direct]

    def kernel(*refs):
        refs = list(refs)

        def pop(count):
            taken = refs[:count]
            del refs[:count]
            return taken

        landed, sources, fill_sources = pop(len(here)), pop(len(ins)), pop(len(fills))
        _, targets = pop(len(tokens)), pop(len(outs))
        inside, leaving, (in_sems, out_sems, fill_sems), extra = pop(len(ins)), pop(len(given)), pop(3), refs
        leaving = [targets[i] if i in kept else leaving.pop(0) for i in range(len(outs))]
        loads = {}
        for i, (source, ref, (_, index)) in enumerate(zip(sources, inside, ins)):
            loads[i] = pltpu.make_async_copy(source.at[index] if index else source, ref, in_sems.at[i])
            loads[i].start()

        stores = []
        for i, (source, (_, index, out)) in enumerate(zip(fill_sources, fills)):
            stores.append(pltpu.make_async_copy(source.at[index] if index else source, targets[out], fill_sems.at[i]))
            stores[-1].start()

        def take(i):
            if i in loads:
                loads.pop(i).wait()
            return inside[i]

        def give(i, index=None, piece=None):
            source, target = leaving[i], targets[i]
            if index is not None:
                source, target = source.at[index], target.at[index]
            sem = out_sems.at[i if piece is None else len(outs) + piece]
            stores.append(pltpu.make_async_copy(source, target, sem))
            stores[-1].start()

        body(*landed, take, leaving, give, *extra)
        assert not loads
        for store in stores:
            store.wait()

    def space(i, out):
        return out if free_outs else (pltpu.VMEM if i in kept else pltpu.HBM)(out.shape, out.dtype)

    return pl.pallas_call(
        kernel,
        out_shape=tuple(space(i, out) for i, out in enumerate(outs)),
        in_specs=[IN_VMEM] * len(here) + [ANY] * (len(ins) + len(fills) + len(tokens)),
        out_specs=tuple(IN_VMEM if i in kept else ANY for i in range(len(outs))),
        scratch_shapes=held
        + given
        + [pltpu.SemaphoreType.DMA((max(count, 1),)) for count in (len(ins), len(outs) + PIECES, len(fills))]
        + list(scratch),
        compiler_params=pltpu.CompilerParams(vmem_limit_bytes=32 * 2**20),
    )(*here, *operands, *in_hbm(*[array for array, _, _ in fills]), *tokens)


def part_shape(array, index):
    kept = [i.size for i in index if not isinstance(i, int)]
    return tuple(kept) + array.shape[len(index) :]


def slots_of(src, count):
    segs = src.shape[1]
    named = (iota((count, segs), 0) == src).astype(BF16)
    earlier = (iota((segs, segs), 0) < iota((segs, segs), 1)).astype(BF16)
    before = dot(named, earlier)
    rank = jnp.sum(named.astype(F32) * before, axis=0, keepdims=True).astype(jnp.int32)
    return named, rank


def request_kernel(blocks, take, out, give):
    src, master = take(0)[0], take(1)[0]
    count = out[0].shape[0]
    named, rank = slots_of(src, count)
    segs = named.shape[1]
    wants = (iota((CAPACITY * blocks, segs), 0) == rank * blocks + master).astype(BF16)
    out[0][...] = dot(named, wants, ((1,), (1,)))
    give(0)


def split3(rows):
    high = rows.astype(BF16)
    rest = rows - high.astype(F32)
    mid = rest.astype(BF16)
    low = (rest - mid.astype(F32)).astype(BF16)
    return jnp.concatenate([high, mid, low], axis=0)


def prep_kernel(take, out, give):
    put_ref, get_ref, take_ref, sum_ref, normal_rows_ref, low_ref, high_ref, surface_ref, _, get_v, put_v, normal_v, known_ref = out
    surface = take(3)[...].astype(BF16)
    surface_ref[...] = copies(surface)
    high_ref[...] = surface
    low_ref[...] = take(4)[...].astype(BF16)
    give(5)
    give(6)
    src, slave, normals = take(0)[0], take(1)[0], take(2)[...]
    blocks = normals.shape[0]
    slots, segs = put_ref.shape
    _, rank = slots_of(src, slots // CAPACITY)
    put = (iota((slots, segs), 0) == src * CAPACITY + rank).astype(F32)
    put_ref[...] = put.astype(BF16)
    give(0)
    get_ref[...] = jnp.transpose(put).astype(BF16)
    give(1)
    spread = (lax.rem(iota((4 * blocks, segs), 0), blocks) == slave).astype(F32)
    pick = jnp.transpose(spread)[:, : 3 * blocks].astype(BF16)
    take_ref[...] = pick
    give(2)
    once = spread[:blocks].astype(BF16)
    sum_ref[...] = jnp.concatenate([once, once], axis=1)
    give(3)
    normal_rows = dot(pick, split3(normals))
    normal_rows_ref[...] = normal_rows
    give(4)
    put_v[...] = put_ref[...]
    get_v[...] = get_ref[...]
    normal_v[...] = normal_rows
    known_ref[...] = known(take(5)[...], normal_rows, dot(pick, split3(take(3)[...])))


def known(gap, normal_rows, slave_rows):
    x, y, z = columns(normal_rows * slave_rows)
    return gap - (x + y + z)


def columns(rows):
    nodes = rows.shape[1] // 3
    return [rows[:, c * nodes : (c + 1) * nodes] for c in range(3)]


def known_kernel(take, out, give):
    slave_rows = dot(take(1)[...], split3(take(0)[...]))
    out[0][...] = known(take(3)[...], take(2)[...], slave_rows)


def place(rows, scratch, out_ref, send):
    scratch[...] = rows
    pairs = out_ref.shape[0] // 2
    part = pairs // PIECES
    for j in range(pairs):
        both = scratch[2 * CAPACITY * j : 2 * CAPACITY * (j + 1), :].astype(BF16)
        out_ref[2 * j] = both[:CAPACITY]
        out_ref[2 * j + 1] = both[CAPACITY:]
        if (j + 1) % part == 0:
            send(j // part, pl.ds(2 * (j + 1 - part), 2 * part))


def gathered(in_ref, scratch):
    for j in range(in_ref.shape[0] // 2):
        both = jnp.concatenate([in_ref[2 * j].astype(F32), in_ref[2 * j + 1].astype(F32)], axis=0)
        scratch[2 * CAPACITY * j : 2 * CAPACITY * (j + 1), :] = both
    return scratch[...].astype(BF16)


def copies(rows):
    return jnp.concatenate([rows] * CAPACITY, axis=0)


def first_kernel(asked_ref, surface_ref, take, out, give, scratch):
    pick_ref, out_ref = out
    slots, wide = pick_ref.shape
    count, blocks = slots // CAPACITY, wide // CAPACITY
    expand = (lax.div(iota((slots, count), 0), CAPACITY) == iota((slots, count), 1)).astype(BF16)
    mine = lax.div(iota((slots, wide), 1), blocks) == lax.rem(iota((slots, wide), 0), CAPACITY)
    rows = dot(expand, asked_ref[...].astype(BF16))
    pick = jnp.where(mine, rows, 0.0).astype(BF16)
    pick_ref[...] = pick
    give(0)
    place(dot(pick, surface_ref[...]), scratch, out_ref, lambda piece, part: give(1, part, piece))


def contact_kernel(
    in_ref, early_ref, get_ref, put_ref, normal_ref, known_ref, mortar_hbm, low_token, high_token,
    out_hbm, pushed_hbm, scratch, back_ref, out_ref, pushed_ref, later_ref, sems, later_sems,
):
    early, _, nodes = early_ref.shape
    segs = early + later_ref.shape[0]
    later = []
    for k in range(0, segs - early, GROUP):
        copy = pltpu.make_async_copy(
            mortar_hbm.at[0, 0, pl.ds(early + k, GROUP)], later_ref.at[pl.ds(k, GROUP)], later_sems.at[k // GROUP]
        )
        copy.start()
        later.append(copy)
    member = lax.rem(iota((3 * GROUP, nodes), 0), GROUP)
    place_in = lax.rem(member, 4)
    block_of = lax.div(member, 4)
    odd = lax.rem(place_in, 2) == 1
    late = place_in >= 2
    zero = jnp.zeros((3 * GROUP, nodes), BF16)
    master = dot(get_ref[...], gathered(in_ref, scratch)).astype(BF16)

    def choose(parts):
        result = parts[0]
        for b in range(1, GROUP // 4):
            result = jnp.where(block_of == b, parts[b], result)
        return result

    for g in range(segs // GROUP):
        own = slice(GROUP * g, GROUP * (g + 1))
        um = jnp.concatenate(columns(master[own]), axis=0)
        normal = jnp.concatenate(columns(normal_ref[own, :]), axis=0)
        mortar_ref, start = early_ref, GROUP * g
        if start >= early:
            mortar_ref, start = later_ref, start - early
            later[start // GROUP].wait()
        weights = []
        for s in range(start, start + GROUP, 4):
            left = mortar_ref[s : s + 2].reshape(2 * nodes, nodes)
            right = mortar_ref[s + 2 : s + 4].reshape(2 * nodes, nodes)
            weights.append(jnp.concatenate([left, right], axis=1))
        lhs = jnp.concatenate([jnp.where(late, zero, um), jnp.where(late, um, zero)], axis=1)
        parts = []
        for w in weights:
            r = dot(lhs, w, ((1,), (1,)))
            parts.append(jnp.where(odd, r[:, nodes:], r[:, :nodes]))
        terms = normal * choose(parts)
        gap = known_ref[own, :] + (terms[:GROUP] + terms[GROUP : 2 * GROUP] + terms[2 * GROUP :])
        pressure = PENALTY * jnp.maximum(-gap, 0.0)
        pushed = jnp.concatenate([pressure] * 3, axis=0) * normal
        high = pushed.astype(BF16)
        rest = (pushed - high.astype(F32)).astype(BF16)
        lhs = jnp.concatenate([jnp.where(odd, zero, high), jnp.where(odd, high, zero)], axis=1)
        parts = []
        for w in weights:
            r = dot(lhs, w)
            parts.append(jnp.where(late, r[:, nodes:], r[:, :nodes]))
        back = (-choose(parts)).astype(BF16)
        for c in range(3):
            rows = slice(GROUP * c, GROUP * (c + 1))
            cols = slice(nodes * c, nodes * (c + 1))
            back_ref[own, cols] = back[rows]
            pushed_ref[own, cols] = high[rows]
            pushed_ref[segs + GROUP * g : segs + GROUP * (g + 1), cols] = rest[rows]
    store = pltpu.make_async_copy(pushed_ref, pushed_hbm, sems.at[0])
    store.start()
    stores = [store]

    def send(piece, part):
        stores.append(pltpu.make_async_copy(out_ref.at[part], out_hbm.at[part], sems.at[1 + piece]))
        stores[-1].start()

    place(dot(put_ref[...], back_ref[...]), scratch, out_ref, send)
    for copy in stores:
        copy.wait()


def bulk_kernel(take, out, give, rounded_ref, product_ref):
    out_ref, base_ref, near_ref, pick_ref = out[:4]
    last_refs = out[4:5]
    pick_ref[...] = take(11)[...]
    _, layers, blocks, width = out_ref.shape
    rows = layers * blocks
    step = (rows + 2 * blocks) // PARTS
    low_ref, high_ref, field_ref, layer_ref = take(0), take(1), take(2), take(3)
    rounded_ref[:blocks] = low_ref[...]
    rounded_ref[blocks : 2 * blocks] = layer_ref[...].astype(BF16)
    for l in range(1, layers):
        rounded_ref[(l + 1) * blocks : (l + 2) * blocks] = field_ref[0, l].astype(BF16)
    rounded_ref[rows + blocks :] = high_ref[...]
    weight_refs = [take(i) for i in (4, 5, 6)]

    @pl.loop(0, PARTS)
    def multiply(p):
        here = pl.ds(pl.multiple_of(p * step, 16), step)
        part = rounded_ref[here]
        for k, weight_ref in enumerate(weight_refs):
            product_ref[here, k * width : (k + 1) * width] = dot(part, weight_ref[...])

    block = iota((blocks, width), 0)

    def inner(l):
        def product(layer, k):
            return product_ref[pl.ds(pl.multiple_of(layer * blocks, blocks), blocks), k * width : (k + 1) * width]

        side = product(l + 1, 2)
        left = jnp.where(block == 0, 0.0, pltpu.roll(side, 1, 0))
        right = jnp.where(block == blocks - 1, 0.0, pltpu.roll(side, blocks - 1, 0))
        return product(l + 1, 0) + (product(l, 1) + product(l + 2, 1)) + (left + right)

    load_ref, scale_ref = take(7), take(8)

    def stepped(old, l, force):
        return old + scale_ref[0, l].astype(F32) * (load_ref[0, l].astype(F32) - force)

    base_ref[...] = stepped(layer_ref[...], 0, inner(0) + dot(take(10)[...], take(9)[...]))
    near_ref[...] = scale_ref[0, 0].astype(F32)

    @pl.loop(1, layers)
    def update(l):
        out_ref[0, l] = stepped(field_ref[0, l], l, inner(l))

    give(0, (0, pl.ds(1, layers - 1)))
    for last_ref in last_refs:
        last_ref[...] = out_ref[0, layers - 1].astype(BF16)
        give(4)


def summed(in_ref, pick_ref, base_ref, scale_ref, scratch):
    sums = dot(pick_ref[...], gathered(in_ref, scratch), ((0,), (0,)))
    blocks = base_ref.shape[0]
    total = sums[:blocks]
    for k in range(1, CAPACITY):
        total = total + sums[k * blocks : (k + 1) * blocks]
    return base_ref[...] - scale_ref[...] * total


def next_kernel(in_ref, pick_ref, base_ref, scale_ref, take, out, give, scratch):
    out_ref, layer_ref, high_ref = out
    first = summed(in_ref, pick_ref, base_ref, scale_ref, scratch)
    layer_ref[0, 0] = first
    give(1)
    surface = first.astype(BF16)
    high_ref[...] = surface
    give(2)
    place(dot(pick_ref[...], copies(surface)), scratch, out_ref, lambda piece, part: give(0, part, piece))


def last_kernel(in_ref, pick_ref, base_ref, scale_ref, field_hbm, out_hbm, scratch, layer_ref, sem):
    layer_ref[...] = summed(in_ref, pick_ref, base_ref, scale_ref, scratch)
    store = pltpu.make_async_copy(layer_ref, out_hbm.at[0, 0], sem)
    store.start()
    store.wait()


def shift(block, step):
    count = lax.axis_size("slab")
    pairs = [(i, i + step) for i in range(count) if 0 <= i + step < count]
    return lax.ppermute(block, "slab", pairs)


def exchange(parts):
    return lax.all_to_all(parts, "dom", 0, 0, tiled=True)


def on_device(
    disp, f_ext, inv_diag, k_self, k_layer, k_side, mortar, gap0, normals, seg_slave, seg_src, seg_master
):
    _, layers, blocks, width = disp.shape
    segs = seg_slave.shape[2]
    count = lax.axis_size("dom")
    slots = count * CAPACITY
    wide = CAPACITY * blocks
    rows_scratch = VMEM((slots, width), F32)
    message = shaped((count, CAPACITY, width), BF16)
    edge = shaped((blocks, width), BF16)
    layer = shaped((blocks, width), F32)

    early = max(segs // 2, GROUP)
    early_part = (0, 0, pl.ds(0, early))
    (asked,) = staged(
        lambda *refs: request_kernel(blocks, *refs), [seg_src, seg_master], [shaped((count, wide), F32)], free_outs=True
    )
    put, get, pick3, back_sum, normal_rows, low, high, surface, *ready, gap = staged(
        prep_kernel,
        [seg_src, seg_slave, (normals, (0, 0)), (disp, (0, 0)), (disp, (0, layers - 1)), (gap0, (0, 0))],
        [
            shaped((slots, segs), BF16),
            shaped((segs, slots), BF16),
            shaped((segs, 3 * blocks), BF16),
            shaped((blocks, 2 * segs), BF16),
            shaped((segs, width), F32),
            edge,
            edge,
            shaped((CAPACITY * blocks, width), BF16),
            shaped((early,) + mortar.shape[3:], BF16),
            shaped((segs, slots), BF16),
            shaped((slots, segs), BF16),
            shaped((segs, width), F32),
            shaped(gap0.shape[2:], F32),
        ],
        tokens=[asked],
        kept=(7, 8, 9, 10, 11, 12),
        fills=[(mortar, early_part, 8)],
    )
    asked = exchange(asked.reshape(count, 1, wide)).reshape(count, wide)
    pick, sent = staged(
        first_kernel, [], [shaped((slots, wide), BF16), message], [rows_scratch], direct=(asked, surface)
    )

    def contact(arrived, near_arrays, low, high):
        here = [pltpu.with_memory_space_constraint(array, pltpu.VMEM) for array in (arrived, *near_arrays)]
        pushed = shaped((2 * segs, width), BF16)
        return pl.pallas_call(
            contact_kernel,
            out_shape=[pltpu.HBM(message.shape, BF16), pltpu.HBM(pushed.shape, BF16)],
            in_specs=[IN_VMEM] * 6 + [ANY] * 3,
            out_specs=[ANY] * 2,
            scratch_shapes=[
                rows_scratch,
                VMEM((segs, width), BF16),
                VMEM(message.shape, BF16),
                VMEM(pushed.shape, BF16),
                VMEM((segs - early,) + mortar.shape[3:], BF16),
                pltpu.SemaphoreType.DMA((1 + PIECES,)),
                pltpu.SemaphoreType.DMA(((segs - early) // GROUP,)),
            ],
            compiler_params=pltpu.CompilerParams(vmem_limit_bytes=16 * 2**20),
        )(*here, *in_hbm(mortar), low, high)

    def bulk(field, layer0, low, high, pushed, more):
        outs = [shaped(disp.shape, F32), layer, layer, shaped(pick.shape, BF16)]
        if more:
            outs += [edge] + [shaped(array.shape, array.dtype) for array in ready]
        rows = (layers + 2) * blocks
        return staged(
            bulk_kernel,
            [low, high, field, layer0, k_self, k_layer, k_side, f_ext, inv_diag, pushed, back_sum, pick],
            outs,
            [VMEM((rows, width), BF16), VMEM((rows, 3 * width), F32)],
            loose=(0, 1),
            kept=(1, 2, 3, 5, 6, 7, 8) if more else (1, 2, 3),
            fills=[(mortar, early_part, 5), (get, (), 6), (put, (), 7), (normal_rows, (), 8)] if more else [],
        )

    arrived = exchange(sent)
    low, high = shift(low, 1), shift(high, -1)
    sent, pushed = contact(arrived, [*ready, gap], low, high)
    returned = exchange(sent)
    field, base, scale, near, last, *ready = bulk(disp, (disp, (0, 0)), low, high, pushed, True)
    sent, layer0, high = staged(
        next_kernel, [], [message, shaped((1, 1, blocks, width), F32), edge], [rows_scratch], direct=(returned, near, base, scale)
    )
    arrived = exchange(sent)
    low, high = shift(last, 1), shift(high, -1)
    (gap,) = staged(
        known_kernel, [(layer0, (0, 0)), pick3, normal_rows, (gap0, (0, 0))], [shaped(gap0.shape[2:], F32)], kept=(0,)
    )
    sent, pushed = contact(arrived, [*ready, gap], low, high)
    returned = exchange(sent)
    field, base, scale, near = bulk(field, (layer0, (0, 0)), low, high, pushed, False)
    return pl.pallas_call(
        last_kernel,
        out_shape=pltpu.HBM(disp.shape, F32),
        in_specs=[IN_VMEM] * 4 + [HBM],
        out_specs=HBM,
        scratch_shapes=[rows_scratch, VMEM(base.shape, F32), pltpu.SemaphoreType.DMA],
        input_output_aliases={4: 0},
        compiler_params=pltpu.CompilerParams(vmem_limit_bytes=16 * 2**20),
    )(
        *[pltpu.with_memory_space_constraint(array, pltpu.VMEM) for array in (returned, near, base, scale)],
        *in_hbm(field),
    )


def solution(mesh):
    in_specs = (
        P("dom", "slab", None, None),
        P("dom", "slab", None, None),
        P("dom", "slab", None, None),
        P(),
        P(),
        P(),
        P("dom", "slab", None, None, None),
        P("dom", "slab", None, None),
        P("dom", "slab", None, None),
        P("dom", "slab", None),
        P("dom", "slab", None),
        P("dom", "slab", None),
    )
    return jax.shard_map(
        on_device, mesh=mesh, in_specs=in_specs, out_specs=P("dom", "slab", None, None), check_vma=False
    )
```

```python
import jax
import jax.numpy as jnp
from jax import lax
from jax.experimental import pallas as pl
from jax.experimental.pallas import tpu as pltpu
from jax.sharding import PartitionSpec as P

PENALTY = 2.0
CAPACITY = 4
GROUP = 16
PIECES = 4
PARTS = 2
VMEM = pltpu.VMEM
HBM = pl.BlockSpec(memory_space=pltpu.HBM)
ANY = pl.BlockSpec(memory_space=pl.ANY)
IN_VMEM = pl.BlockSpec(memory_space=VMEM)
BF16 = jnp.bfloat16
F32 = jnp.float32


def dot(a, b, dims=((1,), (0,))):
    return lax.dot_general(a, b, (dims, ((), ())), preferred_element_type=F32)


def iota(shape, axis):
    return lax.broadcasted_iota(jnp.int32, shape, axis)


def shaped(shape, dtype):
    return jax.ShapeDtypeStruct(shape, dtype)


def in_hbm(*arrays):
    return [pltpu.with_memory_space_constraint(array, pltpu.HBM) for array in arrays]


def staged(body, ins, outs, scratch=(), tokens=(), loose=(), free_outs=False, direct=(), kept=(), fills=()):
    ins = [item if isinstance(item, tuple) else (item, ()) for item in ins]
    operands = [array if i in loose else in_hbm(array)[0] for i, (array, _) in enumerate(ins)]
    held = [VMEM(part_shape(array, index), array.dtype) for array, index in ins]
    given = [VMEM(out.shape, out.dtype) for i, out in enumerate(outs) if i not in kept]
    here = [pltpu.with_memory_space_constraint(array, pltpu.VMEM) for array in direct]

    def kernel(*refs):
        refs = list(refs)

        def pop(count):
            taken = refs[:count]
            del refs[:count]
            return taken

        landed, sources, fill_sources = pop(len(here)), pop(len(ins)), pop(len(fills))
        _, targets = pop(len(tokens)), pop(len(outs))
        inside, leaving, (in_sems, out_sems, fill_sems), extra = pop(len(ins)), pop(len(given)), pop(3), refs
        leaving = [targets[i] if i in kept else leaving.pop(0) for i in range(len(outs))]
        loads = {}
        for i, (source, ref, (_, index)) in enumerate(zip(sources, inside, ins)):
            loads[i] = pltpu.make_async_copy(source.at[index] if index else source, ref, in_sems.at[i])
            loads[i].start()

        stores = []
        for i, (source, (_, index, out)) in enumerate(zip(fill_sources, fills)):
            stores.append(pltpu.make_async_copy(source.at[index] if index else source, targets[out], fill_sems.at[i]))
            stores[-1].start()

        def take(i):
            if i in loads:
                loads.pop(i).wait()
            return inside[i]

        def give(i, index=None, piece=None):
            source, target = leaving[i], targets[i]
            if index is not None:
                source, target = source.at[index], target.at[index]
            sem = out_sems.at[i if piece is None else len(outs) + piece]
            stores.append(pltpu.make_async_copy(source, target, sem))
            stores[-1].start()

        body(*landed, take, leaving, give, *extra)
        assert not loads
        for store in stores:
            store.wait()

    def space(i, out):
        return out if free_outs else (pltpu.VMEM if i in kept else pltpu.HBM)(out.shape, out.dtype)

    return pl.pallas_call(
        kernel,
        out_shape=tuple(space(i, out) for i, out in enumerate(outs)),
        in_specs=[IN_VMEM] * len(here) + [ANY] * (len(ins) + len(fills) + len(tokens)),
        out_specs=tuple(IN_VMEM if i in kept else ANY for i in range(len(outs))),
        scratch_shapes=held
        + given
        + [pltpu.SemaphoreType.DMA((max(count, 1),)) for count in (len(ins), len(outs) + PIECES, len(fills))]
        + list(scratch),
        compiler_params=pltpu.CompilerParams(vmem_limit_bytes=32 * 2**20),
    )(*here, *operands, *in_hbm(*[array for array, _, _ in fills]), *tokens)


def part_shape(array, index):
    kept = [i.size for i in index if not isinstance(i, int)]
    return tuple(kept) + array.shape[len(index) :]


def slots_of(src, count):
    segs = src.shape[1]
    named = (iota((count, segs), 0) == src).astype(BF16)
    earlier = (iota((segs, segs), 0) < iota((segs, segs), 1)).astype(BF16)
    before = dot(named, earlier)
    rank = jnp.sum(named.astype(F32) * before, axis=0, keepdims=True).astype(jnp.int32)
    return named, rank


def request_kernel(blocks, take, out, give):
    src, master = take(0)[0], take(1)[0]
    count = out[0].shape[0]
    named, rank = slots_of(src, count)
    segs = named.shape[1]
    wants = (iota((CAPACITY * blocks, segs), 0) == rank * blocks + master).astype(BF16)
    out[0][...] = dot(named, wants, ((1,), (1,)))
    give(0)


def split3(rows):
    high = rows.astype(BF16)
    rest = rows - high.astype(F32)
    mid = rest.astype(BF16)
    low = (rest - mid.astype(F32)).astype(BF16)
    return jnp.concatenate([high, mid, low], axis=0)


def prep_kernel(take, out, give):
    put_ref, get_ref, take_ref, sum_ref, normal_rows_ref, low_ref, high_ref, surface_ref, _, get_v, put_v, known_ref = out
    surface = take(3)[...].astype(BF16)
    surface_ref[...] = copies(surface)
    high_ref[...] = surface
    low_ref[...] = take(4)[...].astype(BF16)
    give(5)
    give(6)
    src, slave, normals = take(0)[0], take(1)[0], take(2)[...]
    blocks = normals.shape[0]
    slots, segs = put_ref.shape
    _, rank = slots_of(src, slots // CAPACITY)
    put = (iota((slots, segs), 0) == src * CAPACITY + rank).astype(F32)
    put_ref[...] = put.astype(BF16)
    give(0)
    get_ref[...] = jnp.transpose(put).astype(BF16)
    give(1)
    spread = (lax.rem(iota((4 * blocks, segs), 0), blocks) == slave).astype(F32)
    pick = jnp.transpose(spread)[:, : 3 * blocks].astype(BF16)
    take_ref[...] = pick
    give(2)
    once = spread[:blocks].astype(BF16)
    sum_ref[...] = jnp.concatenate([once, once], axis=1)
    give(3)
    normal_rows = dot(pick, split3(normals))
    normal_rows_ref[...] = normal_rows
    give(4)
    put_v[...] = put_ref[...]
    get_v[...] = get_ref[...]
    known_ref[...] = known(take(5)[...], normal_rows, dot(pick, split3(take(3)[...])))


def known(gap, normal_rows, slave_rows):
    x, y, z = columns(normal_rows * slave_rows)
    return gap - (x + y + z)


def columns(rows):
    nodes = rows.shape[1] // 3
    return [rows[:, c * nodes : (c + 1) * nodes] for c in range(3)]


def known_kernel(take, out, give):
    slave_rows = dot(take(1)[...], split3(take(0)[...]))
    out[0][...] = known(take(3)[...], take(2)[...], slave_rows)


def place(rows, scratch, out_ref, send):
    scratch[...] = rows
    pairs = out_ref.shape[0] // 2
    part = pairs // PIECES
    for j in range(pairs):
        both = scratch[2 * CAPACITY * j : 2 * CAPACITY * (j + 1), :].astype(BF16)
        out_ref[2 * j] = both[:CAPACITY]
        out_ref[2 * j + 1] = both[CAPACITY:]
        if (j + 1) % part == 0:
            send(j // part, pl.ds(2 * (j + 1 - part), 2 * part))


def gathered(in_ref, scratch):
    for j in range(in_ref.shape[0] // 2):
        both = jnp.concatenate([in_ref[2 * j].astype(F32), in_ref[2 * j + 1].astype(F32)], axis=0)
        scratch[2 * CAPACITY * j : 2 * CAPACITY * (j + 1), :] = both
    return scratch[...].astype(BF16)


def copies(rows):
    return jnp.concatenate([rows] * CAPACITY, axis=0)


def first_kernel(asked_ref, surface_ref, take, out, give, scratch):
    pick_ref, out_ref = out
    slots, wide = pick_ref.shape
    count, blocks = slots // CAPACITY, wide // CAPACITY
    expand = (lax.div(iota((slots, count), 0), CAPACITY) == iota((slots, count), 1)).astype(BF16)
    mine = lax.div(iota((slots, wide), 1), blocks) == lax.rem(iota((slots, wide), 0), CAPACITY)
    rows = dot(expand, asked_ref[...].astype(BF16))
    pick = jnp.where(mine, rows, 0.0).astype(BF16)
    pick_ref[...] = pick
    give(0)
    place(dot(pick, surface_ref[...]), scratch, out_ref, lambda piece, part: give(1, part, piece))


def contact_kernel(
    in_ref, early_ref, get_ref, put_ref, known_ref, normal_hbm, mortar_hbm, low_token, high_token,
    out_hbm, pushed_hbm, scratch, back_ref, out_ref, pushed_ref, normal_ref, later_ref, sems, later_sems,
):
    early, _, nodes = early_ref.shape
    segs = early + later_ref.shape[0]
    normals = pltpu.make_async_copy(normal_hbm, normal_ref, later_sems.at[0])
    later = pltpu.make_async_copy(mortar_hbm.at[0, 0, pl.ds(early, segs - early)], later_ref, later_sems.at[1])
    normals.start()
    later.start()
    member = lax.rem(iota((3 * GROUP, nodes), 0), GROUP)
    place_in = lax.rem(member, 4)
    block_of = lax.div(member, 4)
    odd = lax.rem(place_in, 2) == 1
    late = place_in >= 2
    zero = jnp.zeros((3 * GROUP, nodes), BF16)
    master = dot(get_ref[...], gathered(in_ref, scratch)).astype(BF16)

    def choose(parts):
        result = parts[0]
        for b in range(1, GROUP // 4):
            result = jnp.where(block_of == b, parts[b], result)
        return result

    normals.wait()
    for g in range(segs // GROUP):
        own = slice(GROUP * g, GROUP * (g + 1))
        if GROUP * g == early:
            later.wait()
        um = jnp.concatenate(columns(master[own]), axis=0)
        normal = jnp.concatenate(columns(normal_ref[own, :]), axis=0)
        mortar_ref, start = early_ref, GROUP * g
        if start >= early:
            mortar_ref, start = later_ref, start - early
        weights = []
        for s in range(start, start + GROUP, 4):
            left = mortar_ref[s : s + 2].reshape(2 * nodes, nodes)
            right = mortar_ref[s + 2 : s + 4].reshape(2 * nodes, nodes)
            weights.append(jnp.concatenate([left, right], axis=1))
        lhs = jnp.concatenate([jnp.where(late, zero, um), jnp.where(late, um, zero)], axis=1)
        parts = []
        for w in weights:
            r = dot(lhs, w, ((1,), (1,)))
            parts.append(jnp.where(odd, r[:, nodes:], r[:, :nodes]))
        terms = normal * choose(parts)
        gap = known_ref[own, :] + (terms[:GROUP] + terms[GROUP : 2 * GROUP] + terms[2 * GROUP :])
        pressure = PENALTY * jnp.maximum(-gap, 0.0)
        pushed = jnp.concatenate([pressure] * 3, axis=0) * normal
        high = pushed.astype(BF16)
        rest = (pushed - high.astype(F32)).astype(BF16)
        lhs = jnp.concatenate([jnp.where(odd, zero, high), jnp.where(odd, high, zero)], axis=1)
        parts = []
        for w in weights:
            r = dot(lhs, w)
            parts.append(jnp.where(late, r[:, nodes:], r[:, :nodes]))
        back = (-choose(parts)).astype(BF16)
        for c in range(3):
            rows = slice(GROUP * c, GROUP * (c + 1))
            cols = slice(nodes * c, nodes * (c + 1))
            back_ref[own, cols] = back[rows]
            pushed_ref[own, cols] = high[rows]
            pushed_ref[segs + GROUP * g : segs + GROUP * (g + 1), cols] = rest[rows]
    store = pltpu.make_async_copy(pushed_ref, pushed_hbm, sems.at[0])
    store.start()
    stores = [store]

    def send(piece, part):
        stores.append(pltpu.make_async_copy(out_ref.at[part], out_hbm.at[part], sems.at[1 + piece]))
        stores[-1].start()

    place(dot(put_ref[...], back_ref[...]), scratch, out_ref, send)
    for copy in stores:
        copy.wait()


def bulk_kernel(take, out, give, rounded_ref, product_ref):
    out_ref, base_ref, near_ref, pick_ref = out[:4]
    last_refs = out[4:5]
    pick_ref[...] = take(11)[...]
    _, layers, blocks, width = out_ref.shape
    rows = layers * blocks
    step = (rows + 2 * blocks) // PARTS
    low_ref, high_ref, field_ref, layer_ref = take(0), take(1), take(2), take(3)
    rounded_ref[:blocks] = low_ref[...]
    rounded_ref[blocks : 2 * blocks] = layer_ref[...].astype(BF16)
    for l in range(1, layers):
        rounded_ref[(l + 1) * blocks : (l + 2) * blocks] = field_ref[0, l].astype(BF16)
    rounded_ref[rows + blocks :] = high_ref[...]
    weight_refs = [take(i) for i in (4, 5, 6)]

    @pl.loop(0, PARTS)
    def multiply(p):
        here = pl.ds(pl.multiple_of(p * step, 16), step)
        part = rounded_ref[here]
        for k, weight_ref in enumerate(weight_refs):
            product_ref[here, k * width : (k + 1) * width] = dot(part, weight_ref[...])

    block = iota((blocks, width), 0)

    def inner(l):
        def product(layer, k):
            return product_ref[pl.ds(pl.multiple_of(layer * blocks, blocks), blocks), k * width : (k + 1) * width]

        side = product(l + 1, 2)
        left = jnp.where(block == 0, 0.0, pltpu.roll(side, 1, 0))
        right = jnp.where(block == blocks - 1, 0.0, pltpu.roll(side, blocks - 1, 0))
        return product(l + 1, 0) + (product(l, 1) + product(l + 2, 1)) + (left + right)

    load_ref, scale_ref = take(7), take(8)

    def stepped(old, l, force):
        return old + scale_ref[0, l].astype(F32) * (load_ref[0, l].astype(F32) - force)

    base_ref[...] = stepped(layer_ref[...], 0, inner(0) + dot(take(10)[...], take(9)[...]))
    near_ref[...] = scale_ref[0, 0].astype(F32)

    @pl.loop(1, layers)
    def update(l):
        out_ref[0, l] = stepped(field_ref[0, l], l, inner(l))

    give(0, (0, pl.ds(1, layers - 1)))
    for last_ref in last_refs:
        last_ref[...] = out_ref[0, layers - 1].astype(BF16)
        give(4)


def summed(in_ref, pick_ref, base_ref, scale_ref, scratch):
    sums = dot(pick_ref[...], gathered(in_ref, scratch), ((0,), (0,)))
    blocks = base_ref.shape[0]
    total = sums[:blocks]
    for k in range(1, CAPACITY):
        total = total + sums[k * blocks : (k + 1) * blocks]
    return base_ref[...] - scale_ref[...] * total


def next_kernel(in_ref, pick_ref, base_ref, scale_ref, take, out, give, scratch):
    out_ref, layer_ref, high_ref = out
    first = summed(in_ref, pick_ref, base_ref, scale_ref, scratch)
    layer_ref[0, 0] = first
    give(1)
    surface = first.astype(BF16)
    high_ref[...] = surface
    give(2)
    place(dot(pick_ref[...], copies(surface)), scratch, out_ref, lambda piece, part: give(0, part, piece))


def last_kernel(in_ref, pick_ref, base_ref, scale_ref, field_hbm, out_hbm, scratch, layer_ref, sem):
    layer_ref[...] = summed(in_ref, pick_ref, base_ref, scale_ref, scratch)
    store = pltpu.make_async_copy(layer_ref, out_hbm.at[0, 0], sem)
    store.start()
    store.wait()


def shift(block, step):
    count = lax.axis_size("slab")
    pairs = [(i, i + step) for i in range(count) if 0 <= i + step < count]
    return lax.ppermute(block, "slab", pairs)


def exchange(parts):
    return lax.all_to_all(parts, "dom", 0, 0, tiled=True)


def on_device(
    disp, f_ext, inv_diag, k_self, k_layer, k_side, mortar, gap0, normals, seg_slave, seg_src, seg_master
):
    _, layers, blocks, width = disp.shape
    segs = seg_slave.shape[2]
    count = lax.axis_size("dom")
    slots = count * CAPACITY
    wide = CAPACITY * blocks
    rows_scratch = VMEM((slots, width), F32)
    message = shaped((count, CAPACITY, width), BF16)
    edge = shaped((blocks, width), BF16)
    layer = shaped((blocks, width), F32)

    early = max(segs * 5 // 8 // GROUP, 1) * GROUP
    early_part = (0, 0, pl.ds(0, early))
    (asked,) = staged(
        lambda *refs: request_kernel(blocks, *refs), [seg_src, seg_master], [shaped((count, wide), F32)], free_outs=True
    )
    put, get, pick3, back_sum, normal_rows, low, high, surface, *ready, gap = staged(
        prep_kernel,
        [seg_src, seg_slave, (normals, (0, 0)), (disp, (0, 0)), (disp, (0, layers - 1)), (gap0, (0, 0))],
        [
            shaped((slots, segs), BF16),
            shaped((segs, slots), BF16),
            shaped((segs, 3 * blocks), BF16),
            shaped((blocks, 2 * segs), BF16),
            shaped((segs, width), F32),
            edge,
            edge,
            shaped((CAPACITY * blocks, width), BF16),
            shaped((early,) + mortar.shape[3:], BF16),
            shaped((segs, slots), BF16),
            shaped((slots, segs), BF16),
            shaped(gap0.shape[2:], F32),
        ],
        tokens=[asked],
        kept=(7, 8, 9, 10, 11),
        fills=[(mortar, early_part, 8)],
    )
    asked = exchange(asked.reshape(count, 1, wide)).reshape(count, wide)
    pick, sent = staged(
        first_kernel, [], [shaped((slots, wide), BF16), message], [rows_scratch], direct=(asked, surface)
    )

    def contact(arrived, near_arrays, low, high):
        here = [pltpu.with_memory_space_constraint(array, pltpu.VMEM) for array in (arrived, *near_arrays)]
        pushed = shaped((2 * segs, width), BF16)
        return pl.pallas_call(
            contact_kernel,
            out_shape=[pltpu.HBM(message.shape, BF16), pltpu.HBM(pushed.shape, BF16)],
            in_specs=[IN_VMEM] * 5 + [ANY] * 4,
            out_specs=[ANY] * 2,
            scratch_shapes=[
                rows_scratch,
                VMEM((segs, width), BF16),
                VMEM(message.shape, BF16),
                VMEM(pushed.shape, BF16),
                VMEM(normal_rows.shape, F32),
                VMEM((segs - early,) + mortar.shape[3:], BF16),
                pltpu.SemaphoreType.DMA((1 + PIECES,)),
                pltpu.SemaphoreType.DMA((2,)),
            ],
            compiler_params=pltpu.CompilerParams(vmem_limit_bytes=16 * 2**20),
        )(*here, *in_hbm(normal_rows, mortar), low, high)

    def bulk(field, layer0, low, high, pushed, more):
        outs = [shaped(disp.shape, F32), layer, layer, shaped(pick.shape, BF16)]
        if more:
            outs += [edge] + [shaped(array.shape, array.dtype) for array in ready]
        rows = (layers + 2) * blocks
        return staged(
            bulk_kernel,
            [low, high, field, layer0, k_self, k_layer, k_side, f_ext, inv_diag, pushed, back_sum, pick],
            outs,
            [VMEM((rows, width), BF16), VMEM((rows, 3 * width), F32)],
            loose=(0, 1),
            kept=(1, 2, 3, 5, 6, 7) if more else (1, 2, 3),
            fills=[(mortar, early_part, 5), (get, (), 6), (put, (), 7)] if more else [],
        )

    arrived = exchange(sent)
    low, high = shift(low, 1), shift(high, -1)
    sent, pushed = contact(arrived, [*ready, gap], low, high)
    returned = exchange(sent)
    field, base, scale, near, last, *ready = bulk(disp, (disp, (0, 0)), low, high, pushed, True)
    sent, layer0, high = staged(
        next_kernel, [], [message, shaped((1, 1, blocks, width), F32), edge], [rows_scratch], direct=(returned, near, base, scale)
    )
    arrived = exchange(sent)
    low, high = shift(last, 1), shift(high, -1)
    (gap,) = staged(
        known_kernel, [(layer0, (0, 0)), pick3, normal_rows, (gap0, (0, 0))], [shaped(gap0.shape[2:], F32)], kept=(0,)
    )
    sent, pushed = contact(arrived, [*ready, gap], low, high)
    returned = exchange(sent)
    field, base, scale, near = bulk(field, (layer0, (0, 0)), low, high, pushed, False)
    return pl.pallas_call(
        last_kernel,
        out_shape=pltpu.HBM(disp.shape, F32),
        in_specs=[IN_VMEM] * 4 + [HBM],
        out_specs=HBM,
        scratch_shapes=[rows_scratch, VMEM(base.shape, F32), pltpu.SemaphoreType.DMA],
        input_output_aliases={4: 0},
        compiler_params=pltpu.CompilerParams(vmem_limit_bytes=16 * 2**20),
    )(
        *[pltpu.with_memory_space_constraint(array, pltpu.VMEM) for array in (returned, near, base, scale)],
        *in_hbm(field),
    )


def solution(mesh):
    in_specs = (
        P("dom", "slab", None, None),
        P("dom", "slab", None, None),
        P("dom", "slab", None, None),
        P(),
        P(),
        P(),
        P("dom", "slab", None, None, None),
        P("dom", "slab", None, None),
        P("dom", "slab", None, None),
        P("dom", "slab", None),
        P("dom", "slab", None),
        P("dom", "slab", None),
    )
    return jax.shard_map(
        on_device, mesh=mesh, in_specs=in_specs, out_specs=P("dom", "slab", None, None), check_vma=False
    )
```

```python
import jax
import jax.numpy as jnp
from jax import lax
from jax.experimental import pallas as pl
from jax.experimental.pallas import tpu as pltpu
from jax.sharding import PartitionSpec as P

PENALTY = 2.0
CAPACITY = 4
GROUP = 16
PIECES = 4
PARTS = 2
VMEM = pltpu.VMEM
HBM = pl.BlockSpec(memory_space=pltpu.HBM)
ANY = pl.BlockSpec(memory_space=pl.ANY)
IN_VMEM = pl.BlockSpec(memory_space=VMEM)
BF16 = jnp.bfloat16
F32 = jnp.float32


def dot(a, b, dims=((1,), (0,))):
    return lax.dot_general(a, b, (dims, ((), ())), preferred_element_type=F32)


def iota(shape, axis):
    return lax.broadcasted_iota(jnp.int32, shape, axis)


def shaped(shape, dtype):
    return jax.ShapeDtypeStruct(shape, dtype)


def in_hbm(*arrays):
    return [pltpu.with_memory_space_constraint(array, pltpu.HBM) for array in arrays]


def staged(body, ins, outs, scratch=(), tokens=(), loose=(), free_outs=False, direct=(), kept=(), fills=()):
    ins = [item if isinstance(item, tuple) else (item, ()) for item in ins]
    operands = [array if i in loose else in_hbm(array)[0] for i, (array, _) in enumerate(ins)]
    held = [VMEM(part_shape(array, index), array.dtype) for array, index in ins]
    given = [VMEM(out.shape, out.dtype) for i, out in enumerate(outs) if i not in kept]
    here = [pltpu.with_memory_space_constraint(array, pltpu.VMEM) for array in direct]

    def kernel(*refs):
        refs = list(refs)

        def pop(count):
            taken = refs[:count]
            del refs[:count]
            return taken

        landed, sources, fill_sources = pop(len(here)), pop(len(ins)), pop(len(fills))
        _, targets = pop(len(tokens)), pop(len(outs))
        inside, leaving, (in_sems, out_sems, fill_sems), extra = pop(len(ins)), pop(len(given)), pop(3), refs
        leaving = [targets[i] if i in kept else leaving.pop(0) for i in range(len(outs))]
        loads = {}
        for i, (source, ref, (_, index)) in enumerate(zip(sources, inside, ins)):
            loads[i] = pltpu.make_async_copy(source.at[index] if index else source, ref, in_sems.at[i])
            loads[i].start()

        stores = []
        for i, (source, (_, index, out)) in enumerate(zip(fill_sources, fills)):
            stores.append(pltpu.make_async_copy(source.at[index] if index else source, targets[out], fill_sems.at[i]))
            stores[-1].start()

        def take(i):
            if i in loads:
                loads.pop(i).wait()
            return inside[i]

        def give(i, index=None, piece=None):
            source, target = leaving[i], targets[i]
            if index is not None:
                source, target = source.at[index], target.at[index]
            sem = out_sems.at[i if piece is None else len(outs) + piece]
            stores.append(pltpu.make_async_copy(source, target, sem))
            stores[-1].start()

        body(*landed, take, leaving, give, *extra)
        assert not loads
        for store in stores:
            store.wait()

    def space(i, out):
        return out if free_outs else (pltpu.VMEM if i in kept else pltpu.HBM)(out.shape, out.dtype)

    return pl.pallas_call(
        kernel,
        out_shape=tuple(space(i, out) for i, out in enumerate(outs)),
        in_specs=[IN_VMEM] * len(here) + [ANY] * (len(ins) + len(fills) + len(tokens)),
        out_specs=tuple(IN_VMEM if i in kept else ANY for i in range(len(outs))),
        scratch_shapes=held
        + given
        + [pltpu.SemaphoreType.DMA((max(count, 1),)) for count in (len(ins), len(outs) + PIECES, len(fills))]
        + list(scratch),
        compiler_params=pltpu.CompilerParams(vmem_limit_bytes=32 * 2**20),
    )(*here, *operands, *in_hbm(*[array for array, _, _ in fills]), *tokens)


def part_shape(array, index):
    kept = [i.size for i in index if not isinstance(i, int)]
    return tuple(kept) + array.shape[len(index) :]


def slots_of(src, count):
    segs = src.shape[1]
    named = (iota((count, segs), 0) == src).astype(BF16)
    earlier = (iota((segs, segs), 0) < iota((segs, segs), 1)).astype(BF16)
    before = dot(named, earlier)
    rank = jnp.sum(named.astype(F32) * before, axis=0, keepdims=True).astype(jnp.int32)
    return named, rank


def request_kernel(blocks, take, out, give):
    src, master = take(0)[0], take(1)[0]
    count = out[0].shape[0]
    named, rank = slots_of(src, count)
    segs = named.shape[1]
    wants = (iota((CAPACITY * blocks, segs), 0) == rank * blocks + master).astype(BF16)
    out[0][...] = dot(named, wants, ((1,), (1,)))
    give(0)


def split3(rows):
    high = rows.astype(BF16)
    rest = rows - high.astype(F32)
    mid = rest.astype(BF16)
    low = (rest - mid.astype(F32)).astype(BF16)
    return jnp.concatenate([high, mid, low], axis=0)


def prep_kernel(take, out, give):
    put_ref, get_ref, take_ref, sum_ref, normal_rows_ref, low_ref, high_ref, surface_ref, _, get_v, put_v, normal_v, known_ref = out
    surface = take(3)[...].astype(BF16)
    surface_ref[...] = copies(surface)
    high_ref[...] = surface
    low_ref[...] = take(4)[...].astype(BF16)
    give(5)
    give(6)
    src, slave, normals = take(0)[0], take(1)[0], take(2)[...]
    blocks = normals.shape[0]
    slots, segs = put_ref.shape
    _, rank = slots_of(src, slots // CAPACITY)
    put = (iota((slots, segs), 0) == src * CAPACITY + rank).astype(F32)
    put_ref[...] = put.astype(BF16)
    give(0)
    get_ref[...] = jnp.transpose(put).astype(BF16)
    give(1)
    spread = (lax.rem(iota((4 * blocks, segs), 0), blocks) == slave).astype(F32)
    pick = jnp.transpose(spread)[:, : 3 * blocks].astype(BF16)
    take_ref[...] = pick
    give(2)
    once = spread[:blocks].astype(BF16)
    sum_ref[...] = jnp.concatenate([once, once], axis=1)
    give(3)
    normal_rows = dot(pick, split3(normals))
    normal_rows_ref[...] = normal_rows
    give(4)
    put_v[...] = put_ref[...]
    get_v[...] = get_ref[...]
    normal_v[...] = normal_rows
    known_ref[...] = known(take(5)[...], normal_rows, dot(pick, split3(take(3)[...])))


def known(gap, normal_rows, slave_rows):
    x, y, z = columns(normal_rows * slave_rows)
    return gap - (x + y + z)


def columns(rows):
    nodes = rows.shape[1] // 3
    return [rows[:, c * nodes : (c + 1) * nodes] for c in range(3)]


def known_kernel(take, out, give):
    slave_rows = dot(take(1)[...], split3(take(0)[...]))
    out[0][...] = known(take(3)[...], take(2)[...], slave_rows)


def place(rows, scratch, out_ref, send):
    scratch[...] = rows
    pairs = out_ref.shape[0] // 2
    part = pairs // PIECES
    for j in range(pairs):
        both = scratch[2 * CAPACITY * j : 2 * CAPACITY * (j + 1), :].astype(BF16)
        out_ref[2 * j] = both[:CAPACITY]
        out_ref[2 * j + 1] = both[CAPACITY:]
        if (j + 1) % part == 0:
            send(j // part, pl.ds(2 * (j + 1 - part), 2 * part))


def gathered(in_ref, scratch):
    for j in range(in_ref.shape[0] // 2):
        both = jnp.concatenate([in_ref[2 * j].astype(F32), in_ref[2 * j + 1].astype(F32)], axis=0)
        scratch[2 * CAPACITY * j : 2 * CAPACITY * (j + 1), :] = both
    return scratch[...].astype(BF16)


def copies(rows):
    return jnp.concatenate([rows] * CAPACITY, axis=0)


def first_kernel(asked_ref, surface_ref, take, out, give, scratch):
    pick_ref, out_ref = out
    slots, wide = pick_ref.shape
    count, blocks = slots // CAPACITY, wide // CAPACITY
    expand = (lax.div(iota((slots, count), 0), CAPACITY) == iota((slots, count), 1)).astype(BF16)
    mine = lax.div(iota((slots, wide), 1), blocks) == lax.rem(iota((slots, wide), 0), CAPACITY)
    rows = dot(expand, asked_ref[...].astype(BF16))
    pick = jnp.where(mine, rows, 0.0).astype(BF16)
    pick_ref[...] = pick
    give(0)
    place(dot(pick, surface_ref[...]), scratch, out_ref, lambda piece, part: give(1, part, piece))


def contact_kernel(
    in_ref, early_ref, get_ref, put_ref, normal_ref, known_ref, mortar_hbm, low_hbm, high_hbm, token,
    out_hbm, pushed_hbm, low_out, high_out, scratch, back_ref, out_ref, pushed_ref, later_ref, sems, later_sems,
):
    early, _, nodes = early_ref.shape
    segs = early + later_ref.shape[0]
    later = pltpu.make_async_copy(mortar_hbm.at[0, 0, pl.ds(early, segs - early)], later_ref, later_sems.at[0])
    later.start()
    edges = [
        pltpu.make_async_copy(low_hbm, low_out, later_sems.at[1]),
        pltpu.make_async_copy(high_hbm, high_out, later_sems.at[2]),
    ]
    for edge in edges:
        edge.start()
    member = lax.rem(iota((3 * GROUP, nodes), 0), GROUP)
    place_in = lax.rem(member, 4)
    block_of = lax.div(member, 4)
    odd = lax.rem(place_in, 2) == 1
    late = place_in >= 2
    zero = jnp.zeros((3 * GROUP, nodes), BF16)
    master = dot(get_ref[...], gathered(in_ref, scratch)).astype(BF16)

    def choose(parts):
        result = parts[0]
        for b in range(1, GROUP // 4):
            result = jnp.where(block_of == b, parts[b], result)
        return result

    for g in range(segs // GROUP):
        own = slice(GROUP * g, GROUP * (g + 1))
        if GROUP * g == early:
            later.wait()
        um = jnp.concatenate(columns(master[own]), axis=0)
        normal = jnp.concatenate(columns(normal_ref[own, :]), axis=0)
        mortar_ref, start = early_ref, GROUP * g
        if start >= early:
            mortar_ref, start = later_ref, start - early
        weights = []
        for s in range(start, start + GROUP, 4):
            left = mortar_ref[s : s + 2].reshape(2 * nodes, nodes)
            right = mortar_ref[s + 2 : s + 4].reshape(2 * nodes, nodes)
            weights.append(jnp.concatenate([left, right], axis=1))
        lhs = jnp.concatenate([jnp.where(late, zero, um), jnp.where(late, um, zero)], axis=1)
        parts = []
        for w in weights:
            r = dot(lhs, w, ((1,), (1,)))
            parts.append(jnp.where(odd, r[:, nodes:], r[:, :nodes]))
        terms = normal * choose(parts)
        gap = known_ref[own, :] + (terms[:GROUP] + terms[GROUP : 2 * GROUP] + terms[2 * GROUP :])
        pressure = PENALTY * jnp.maximum(-gap, 0.0)
        pushed = jnp.concatenate([pressure] * 3, axis=0) * normal
        high = pushed.astype(BF16)
        rest = (pushed - high.astype(F32)).astype(BF16)
        lhs = jnp.concatenate([jnp.where(odd, zero, high), jnp.where(odd, high, zero)], axis=1)
        parts = []
        for w in weights:
            r = dot(lhs, w)
            parts.append(jnp.where(late, r[:, nodes:], r[:, :nodes]))
        back = (-choose(parts)).astype(BF16)
        for c in range(3):
            rows = slice(GROUP * c, GROUP * (c + 1))
            cols = slice(nodes * c, nodes * (c + 1))
            back_ref[own, cols] = back[rows]
            pushed_ref[own, cols] = high[rows]
            pushed_ref[segs + GROUP * g : segs + GROUP * (g + 1), cols] = rest[rows]
    store = pltpu.make_async_copy(pushed_ref, pushed_hbm, sems.at[0])
    store.start()
    stores = edges + [store]

    def send(piece, part):
        stores.append(pltpu.make_async_copy(out_ref.at[part], out_hbm.at[part], sems.at[1 + piece]))
        stores[-1].start()

    place(dot(put_ref[...], back_ref[...]), scratch, out_ref, send)
    for copy in stores:
        copy.wait()


def bulk_kernel(whole, take, out, give, rounded_ref, product_ref):
    out_ref = out[0]
    _, layers, blocks, width = out_ref.shape
    rows = layers * blocks
    step = (rows + 2 * blocks) // PARTS
    field_ref, layer_ref = take(0), take(1)
    zero = jnp.zeros((blocks, width), BF16)
    rounded_ref[:blocks] = take(7)[...] if whole else zero
    rounded_ref[blocks : 2 * blocks] = layer_ref[...].astype(BF16)
    for l in range(1, layers):
        rounded_ref[(l + 1) * blocks : (l + 2) * blocks] = field_ref[0, l].astype(BF16)
    rounded_ref[rows + blocks :] = take(8)[...] if whole else zero
    weight_refs = [take(i) for i in (2, 3, 4)]

    @pl.loop(0, PARTS)
    def multiply(p):
        here = pl.ds(pl.multiple_of(p * step, 16), step)
        part = rounded_ref[here]
        for k, weight_ref in enumerate(weight_refs):
            product_ref[here, k * width : (k + 1) * width] = dot(part, weight_ref[...])

    block = iota((blocks, width), 0)

    def inner(l):
        def product(layer, k):
            return product_ref[pl.ds(pl.multiple_of(layer * blocks, blocks), blocks), k * width : (k + 1) * width]

        side = product(l + 1, 2)
        left = jnp.where(block == 0, 0.0, pltpu.roll(side, 1, 0))
        right = jnp.where(block == blocks - 1, 0.0, pltpu.roll(side, blocks - 1, 0))
        return product(l + 1, 0) + (product(l, 1) + product(l + 2, 1)) + (left + right)

    load_ref, scale_ref = take(5), take(6)

    def stepped(old, l, force):
        return old + scale_ref[0, l].astype(F32) * (load_ref[0, l].astype(F32) - force)

    first = inner(0)
    if whole:
        base_ref, near_ref, pick_ref, last_ref = out[1:5]
        pick_ref[...] = take(11)[...]
        near_ref[...] = scale_ref[0, 0].astype(F32)
        first = first + dot(take(10)[...], take(9)[...])
        base_ref[...] = stepped(layer_ref[...], 0, first)
    out_ref[0, 0] = stepped(layer_ref[...], 0, first)

    @pl.loop(1, layers)
    def update(l):
        out_ref[0, l] = stepped(field_ref[0, l], l, inner(l))

    give(0)
    if whole:
        last_ref[...] = out_ref[0, layers - 1].astype(BF16)
        give(4)


def tail_kernel(take, out, give):
    first, last, first_scale, last_scale = [take(i)[...].astype(F32) for i in range(4)]
    base_ref, row_ref, scale0_ref, scale1_ref, pick_ref, weight_ref = out
    base_ref[...] = first - first_scale * dot(take(5)[...], take(4)[...])
    row_ref[...] = last
    scale0_ref[...] = first_scale
    scale1_ref[...] = last_scale
    pick_ref[...] = take(6)[...]
    weight_ref[...] = take(7)[...]


def summed(in_ref, pick_ref, base_ref, scale_ref, scratch):
    sums = dot(pick_ref[...], gathered(in_ref, scratch), ((0,), (0,)))
    blocks = base_ref.shape[0]
    total = sums[:blocks]
    for k in range(1, CAPACITY):
        total = total + sums[k * blocks : (k + 1) * blocks]
    return base_ref[...] - scale_ref[...] * total


def next_kernel(in_ref, pick_ref, base_ref, scale_ref, take, out, give, scratch):
    out_ref, layer_ref, high_ref = out
    first = summed(in_ref, pick_ref, base_ref, scale_ref, scratch)
    layer_ref[0, 0] = first
    give(1)
    surface = first.astype(BF16)
    high_ref[...] = surface
    give(2)
    place(dot(pick_ref[...], copies(surface)), scratch, out_ref, lambda piece, part: give(0, part, piece))


def last_kernel(
    in_ref, base_ref, row_ref, scale0_ref, scale1_ref, pick_ref, weight_ref, low_ref, high_ref, field_hbm,
    out_hbm, scratch, first_ref, last_ref, sems,
):
    end = out_hbm.shape[1] - 1
    last_ref[...] = row_ref[...] - scale1_ref[...] * dot(high_ref[...], weight_ref[...])
    stores = [pltpu.make_async_copy(last_ref, out_hbm.at[0, end], sems.at[0])]
    stores[0].start()
    below = scale0_ref[...] * dot(low_ref[...], weight_ref[...])
    first_ref[...] = summed(in_ref, pick_ref, base_ref, scale0_ref, scratch) - below
    stores.append(pltpu.make_async_copy(first_ref, out_hbm.at[0, 0], sems.at[1]))
    stores[1].start()
    for store in stores:
        store.wait()


def shift(block, step):
    count = lax.axis_size("slab")
    pairs = [(i, i + step) for i in range(count) if 0 <= i + step < count]
    return lax.ppermute(block, "slab", pairs)


def exchange(parts):
    return lax.all_to_all(parts, "dom", 0, 0, tiled=True)


def on_device(
    disp, f_ext, inv_diag, k_self, k_layer, k_side, mortar, gap0, normals, seg_slave, seg_src, seg_master
):
    _, layers, blocks, width = disp.shape
    segs = seg_slave.shape[2]
    count = lax.axis_size("dom")
    slots = count * CAPACITY
    wide = CAPACITY * blocks
    rows_scratch = VMEM((slots, width), F32)
    message = shaped((count, CAPACITY, width), BF16)
    edge = shaped((blocks, width), BF16)
    layer = shaped((blocks, width), F32)

    early = max(segs // 2, GROUP)
    early_part = (0, 0, pl.ds(0, early))
    (asked,) = staged(
        lambda *refs: request_kernel(blocks, *refs), [seg_src, seg_master], [shaped((count, wide), F32)], free_outs=True
    )
    put, get, pick3, back_sum, normal_rows, low, high, surface, *ready, gap = staged(
        prep_kernel,
        [seg_src, seg_slave, (normals, (0, 0)), (disp, (0, 0)), (disp, (0, layers - 1)), (gap0, (0, 0))],
        [
            shaped((slots, segs), BF16),
            shaped((segs, slots), BF16),
            shaped((segs, 3 * blocks), BF16),
            shaped((blocks, 2 * segs), BF16),
            shaped((segs, width), F32),
            edge,
            edge,
            shaped((CAPACITY * blocks, width), BF16),
            shaped((early,) + mortar.shape[3:], BF16),
            shaped((segs, slots), BF16),
            shaped((slots, segs), BF16),
            shaped((segs, width), F32),
            shaped(gap0.shape[2:], F32),
        ],
        tokens=[asked],
        kept=(7, 8, 9, 10, 11, 12),
        fills=[(mortar, early_part, 8)],
    )
    asked = exchange(asked.reshape(count, 1, wide)).reshape(count, wide)
    pick, sent = staged(
        first_kernel, [], [shaped((slots, wide), BF16), message], [rows_scratch], direct=(asked, surface)
    )

    def contact(arrived, near_arrays, low, high, token):
        here = [pltpu.with_memory_space_constraint(array, pltpu.VMEM) for array in (arrived, *near_arrays)]
        pushed = shaped((2 * segs, width), BF16)
        return pl.pallas_call(
            contact_kernel,
            out_shape=[pltpu.HBM(out.shape, BF16) for out in (message, pushed, edge, edge)],
            in_specs=[IN_VMEM] * 6 + [ANY] * 4,
            out_specs=[ANY] * 4,
            scratch_shapes=[
                rows_scratch,
                VMEM((segs, width), BF16),
                VMEM(message.shape, BF16),
                VMEM(pushed.shape, BF16),
                VMEM((segs - early,) + mortar.shape[3:], BF16),
                pltpu.SemaphoreType.DMA((1 + PIECES,)),
                pltpu.SemaphoreType.DMA((3,)),
            ],
            compiler_params=pltpu.CompilerParams(vmem_limit_bytes=16 * 2**20),
        )(*here, *in_hbm(mortar), low, high, *in_hbm(token))

    rows = (layers + 2) * blocks
    bulk_scratch = [VMEM((rows, width), BF16), VMEM((rows, 3 * width), F32)]
    steady = [k_self, k_layer, k_side, f_ext, inv_diag]
    near_shape = shaped((slots, wide), BF16)

    arrived = exchange(sent)
    low, high = shift(low, 1), shift(high, -1)
    sent, pushed, low, high = contact(arrived, [*ready, gap], low, high, pick)
    returned = exchange(sent)
    field, base, scale, near, last, *ready = staged(
        lambda *refs: bulk_kernel(True, *refs),
        [disp, (disp, (0, 0)), *steady, low, high, pushed, back_sum, pick],
        [shaped(disp.shape, F32), layer, layer, near_shape, edge] + [shaped(array.shape, array.dtype) for array in ready],
        bulk_scratch,
        kept=(1, 2, 3, 5, 6, 7, 8),
        fills=[(mortar, early_part, 5), (get, (), 6), (put, (), 7), (normal_rows, (), 8)],
    )
    sent, layer0, high = staged(
        next_kernel,
        [],
        [message, shaped((1, 1, blocks, width), F32), edge],
        [rows_scratch],
        direct=(returned, near, base, scale),
    )
    arrived = exchange(sent)
    (field,) = staged(
        lambda *refs: bulk_kernel(False, *refs),
        [field, (layer0, (0, 0)), *steady],
        [shaped(disp.shape, F32)],
        bulk_scratch,
    )
    (gap,) = staged(
        known_kernel, [(layer0, (0, 0)), pick3, normal_rows, (gap0, (0, 0))], [shaped(gap0.shape[2:], F32)], kept=(0,)
    )
    sent, pushed, low, high = contact(arrived, [*ready, gap], *in_hbm(last, high), field)
    returned = exchange(sent)
    low, high = shift(low, 1), shift(high, -1)
    ends = [(array, (0, l)) for array in (field, inv_diag) for l in (0, layers - 1)]
    held = staged(
        tail_kernel,
        ends + [pushed, back_sum, pick, k_layer],
        [layer, layer, layer, layer, near_shape, shaped(k_layer.shape, BF16)],
        kept=range(6),
    )
    return pl.pallas_call(
        last_kernel,
        out_shape=pltpu.HBM(disp.shape, F32),
        in_specs=[IN_VMEM] * 9 + [HBM],
        out_specs=HBM,
        scratch_shapes=[
            rows_scratch, VMEM(base.shape, F32), VMEM(base.shape, F32), pltpu.SemaphoreType.DMA((2,))
        ],
        input_output_aliases={9: 0},
        compiler_params=pltpu.CompilerParams(vmem_limit_bytes=16 * 2**20),
    )(
        *[pltpu.with_memory_space_constraint(array, pltpu.VMEM) for array in (returned, *held, low, high)],
        *in_hbm(field),
    )


def solution(mesh):
    in_specs = (
        P("dom", "slab", None, None),
        P("dom", "slab", None, None),
        P("dom", "slab", None, None),
        P(),
        P(),
        P(),
        P("dom", "slab", None, None, None),
        P("dom", "slab", None, None),
        P("dom", "slab", None, None),
        P("dom", "slab", None),
        P("dom", "slab", None),
        P("dom", "slab", None),
    )
    return jax.shard_map(
        on_device, mesh=mesh, in_specs=in_specs, out_specs=P("dom", "slab", None, None), check_vma=False
    )
```

```python
import jax
import jax.numpy as jnp
from jax import lax
from jax.experimental import pallas as pl
from jax.experimental.pallas import tpu as pltpu
from jax.sharding import PartitionSpec as P

PENALTY = 2.0
CAPACITY = 4
GROUP = 16
PIECES = 4
PARTS = 2
VMEM = pltpu.VMEM
HBM = pl.BlockSpec(memory_space=pltpu.HBM)
ANY = pl.BlockSpec(memory_space=pl.ANY)
IN_VMEM = pl.BlockSpec(memory_space=VMEM)
BF16 = jnp.bfloat16
F32 = jnp.float32


def dot(a, b, dims=((1,), (0,))):
    return lax.dot_general(a, b, (dims, ((), ())), preferred_element_type=F32)


def iota(shape, axis):
    return lax.broadcasted_iota(jnp.int32, shape, axis)


def shaped(shape, dtype):
    return jax.ShapeDtypeStruct(shape, dtype)


def in_hbm(*arrays):
    return [pltpu.with_memory_space_constraint(array, pltpu.HBM) for array in arrays]


def staged(body, ins, outs, scratch=(), tokens=(), loose=(), free_outs=False, direct=(), kept=(), fills=()):
    ins = [item if isinstance(item, tuple) else (item, ()) for item in ins]
    operands = [array if i in loose else in_hbm(array)[0] for i, (array, _) in enumerate(ins)]
    held = [VMEM(part_shape(array, index), array.dtype) for array, index in ins]
    given = [VMEM(out.shape, out.dtype) for i, out in enumerate(outs) if i not in kept]
    here = [pltpu.with_memory_space_constraint(array, pltpu.VMEM) for array in direct]

    def kernel(*refs):
        refs = list(refs)

        def pop(count):
            taken = refs[:count]
            del refs[:count]
            return taken

        landed, sources, fill_sources = pop(len(here)), pop(len(ins)), pop(len(fills))
        _, targets = pop(len(tokens)), pop(len(outs))
        inside, leaving, (in_sems, out_sems, fill_sems), extra = pop(len(ins)), pop(len(given)), pop(3), refs
        leaving = [targets[i] if i in kept else leaving.pop(0) for i in range(len(outs))]
        loads = {}
        for i, (source, ref, (_, index)) in enumerate(zip(sources, inside, ins)):
            loads[i] = pltpu.make_async_copy(source.at[index] if index else source, ref, in_sems.at[i])
            loads[i].start()

        stores = []
        for i, (source, (_, index, out)) in enumerate(zip(fill_sources, fills)):
            stores.append(pltpu.make_async_copy(source.at[index] if index else source, targets[out], fill_sems.at[i]))
            stores[-1].start()

        def take(i):
            if i in loads:
                loads.pop(i).wait()
            return inside[i]

        def give(i, index=None, piece=None):
            source, target = leaving[i], targets[i]
            if index is not None:
                source, target = source.at[index], target.at[index]
            sem = out_sems.at[i if piece is None else len(outs) + piece]
            stores.append(pltpu.make_async_copy(source, target, sem))
            stores[-1].start()

        body(*landed, take, leaving, give, *extra)
        assert not loads
        for store in stores:
            store.wait()

    def space(i, out):
        return out if free_outs else (pltpu.VMEM if i in kept else pltpu.HBM)(out.shape, out.dtype)

    return pl.pallas_call(
        kernel,
        out_shape=tuple(space(i, out) for i, out in enumerate(outs)),
        in_specs=[IN_VMEM] * len(here) + [ANY] * (len(ins) + len(fills) + len(tokens)),
        out_specs=tuple(IN_VMEM if i in kept else ANY for i in range(len(outs))),
        scratch_shapes=held
        + given
        + [pltpu.SemaphoreType.DMA((max(count, 1),)) for count in (len(ins), len(outs) + PIECES, len(fills))]
        + list(scratch),
        compiler_params=pltpu.CompilerParams(vmem_limit_bytes=32 * 2**20),
    )(*here, *operands, *in_hbm(*[array for array, _, _ in fills]), *tokens)


def part_shape(array, index):
    kept = [i.size for i in index if not isinstance(i, int)]
    return tuple(kept) + array.shape[len(index) :]


def slots_of(src, count):
    segs = src.shape[1]
    named = (iota((count, segs), 0) == src).astype(BF16)
    earlier = (iota((segs, segs), 0) < iota((segs, segs), 1)).astype(BF16)
    before = dot(named, earlier)
    rank = jnp.sum(named.astype(F32) * before, axis=0, keepdims=True).astype(jnp.int32)
    return named, rank


def request_kernel(blocks, take, out, give):
    src, master = take(0)[0], take(1)[0]
    count = out[0].shape[0]
    named, rank = slots_of(src, count)
    segs = named.shape[1]
    wants = (iota((CAPACITY * blocks, segs), 0) == rank * blocks + master).astype(BF16)
    out[0][...] = dot(named, wants, ((1,), (1,)))
    give(0)


def split3(rows):
    high = rows.astype(BF16)
    rest = rows - high.astype(F32)
    mid = rest.astype(BF16)
    low = (rest - mid.astype(F32)).astype(BF16)
    return jnp.concatenate([high, mid, low], axis=0)


def prep_kernel(take, out, give):
    put_ref, get_ref, take_ref, sum_ref, normal_rows_ref, low_ref, high_ref, surface_ref, _, get_v, put_v, normal_v, known_ref = out
    surface = take(3)[...].astype(BF16)
    surface_ref[...] = copies(surface)
    high_ref[...] = surface
    low_ref[...] = take(4)[...].astype(BF16)
    give(5)
    give(6)
    src, slave, normals = take(0)[0], take(1)[0], take(2)[...]
    blocks = normals.shape[0]
    slots, segs = put_ref.shape
    _, rank = slots_of(src, slots // CAPACITY)
    put = (iota((slots, segs), 0) == src * CAPACITY + rank).astype(F32)
    put_ref[...] = put.astype(BF16)
    give(0)
    get_ref[...] = jnp.transpose(put).astype(BF16)
    give(1)
    spread = (lax.rem(iota((4 * blocks, segs), 0), blocks) == slave).astype(F32)
    pick = jnp.transpose(spread)[:, : 3 * blocks].astype(BF16)
    take_ref[...] = pick
    give(2)
    once = spread[:blocks].astype(BF16)
    sum_ref[...] = jnp.concatenate([once, once], axis=1)
    give(3)
    normal_rows = dot(pick, split3(normals))
    normal_rows_ref[...] = normal_rows
    give(4)
    put_v[...] = put_ref[...]
    get_v[...] = get_ref[...]
    normal_v[...] = normal_rows
    known_ref[...] = known(take(5)[...], normal_rows, dot(pick, split3(take(3)[...])))


def known(gap, normal_rows, slave_rows):
    x, y, z = columns(normal_rows * slave_rows)
    return gap - (x + y + z)


def columns(rows):
    nodes = rows.shape[1] // 3
    return [rows[:, c * nodes : (c + 1) * nodes] for c in range(3)]


def known_kernel(take, out, give):
    slave_rows = dot(take(1)[...], split3(take(0)[...]))
    out[0][...] = known(take(3)[...], take(2)[...], slave_rows)


def place(rows, scratch, out_ref, send):
    scratch[...] = rows
    pairs = out_ref.shape[0] // 2
    part = pairs // PIECES
    for j in range(pairs):
        both = scratch[2 * CAPACITY * j : 2 * CAPACITY * (j + 1), :]
        out_ref[2 * j] = both[:CAPACITY].astype(BF16)
        out_ref[2 * j + 1] = both[CAPACITY:].astype(BF16)
        if (j + 1) % part == 0:
            send(j // part, pl.ds(2 * (j + 1 - part), 2 * part))


def gathered(in_ref, scratch):
    for j in range(in_ref.shape[0] // 2):
        both = jnp.concatenate([in_ref[2 * j].astype(F32), in_ref[2 * j + 1].astype(F32)], axis=0)
        scratch[2 * CAPACITY * j : 2 * CAPACITY * (j + 1), :] = both
    return scratch[...].astype(BF16)


def copies(rows):
    return jnp.concatenate([rows] * CAPACITY, axis=0)


def first_kernel(asked_ref, surface_ref, take, out, give, scratch):
    pick_ref, out_ref = out
    slots, wide = pick_ref.shape
    count, blocks = slots // CAPACITY, wide // CAPACITY
    expand = (lax.div(iota((slots, count), 0), CAPACITY) == iota((slots, count), 1)).astype(BF16)
    mine = lax.div(iota((slots, wide), 1), blocks) == lax.rem(iota((slots, wide), 0), CAPACITY)
    rows = dot(expand, asked_ref[...].astype(BF16))
    pick = jnp.where(mine, rows, 0.0).astype(BF16)
    pick_ref[...] = pick
    give(0)
    place(dot(pick, surface_ref[...]), scratch, out_ref, lambda piece, part: give(1, part, piece))


def contact_kernel(
    in_ref, early_ref, get_ref, put_ref, normal_ref, known_ref, mortar_hbm, low_hbm, high_hbm, token,
    out_hbm, pushed_hbm, low_out, high_out, scratch, back_ref, out_ref, pushed_ref, later_ref, sems, later_sems,
):
    early, _, nodes = early_ref.shape
    segs = early + later_ref.shape[0]
    later = pltpu.make_async_copy(mortar_hbm.at[0, 0, pl.ds(early, segs - early)], later_ref, later_sems.at[0])
    later.start()
    edges = [
        pltpu.make_async_copy(low_hbm, low_out, later_sems.at[1]),
        pltpu.make_async_copy(high_hbm, high_out, later_sems.at[2]),
    ]
    for edge in edges:
        edge.start()
    member = lax.rem(iota((3 * GROUP, nodes), 0), GROUP)
    place_in = lax.rem(member, 4)
    block_of = lax.div(member, 4)
    odd = lax.rem(place_in, 2) == 1
    late = place_in >= 2
    zero = jnp.zeros((3 * GROUP, nodes), BF16)
    master = dot(get_ref[...], gathered(in_ref, scratch)).astype(BF16)

    def choose(parts):
        result = parts[0]
        for b in range(1, GROUP // 4):
            result = jnp.where(block_of == b, parts[b], result)
        return result

    for g in range(segs // GROUP):
        own = slice(GROUP * g, GROUP * (g + 1))
        if GROUP * g == early:
            later.wait()
        um = jnp.concatenate(columns(master[own]), axis=0)
        normal = jnp.concatenate(columns(normal_ref[own, :]), axis=0)
        mortar_ref, start = early_ref, GROUP * g
        if start >= early:
            mortar_ref, start = later_ref, start - early
        weights = []
        for s in range(start, start + GROUP, 4):
            left = mortar_ref[s : s + 2].reshape(2 * nodes, nodes)
            right = mortar_ref[s + 2 : s + 4].reshape(2 * nodes, nodes)
            weights.append(jnp.concatenate([left, right], axis=1))
        lhs = jnp.concatenate([jnp.where(late, zero, um), jnp.where(late, um, zero)], axis=1)
        parts = []
        for w in weights:
            r = dot(lhs, w, ((1,), (1,)))
            parts.append(jnp.where(odd, r[:, nodes:], r[:, :nodes]))
        terms = normal * choose(parts)
        gap = known_ref[own, :] + (terms[:GROUP] + terms[GROUP : 2 * GROUP] + terms[2 * GROUP :])
        pressure = PENALTY * jnp.maximum(-gap, 0.0)
        pushed = jnp.concatenate([pressure] * 3, axis=0) * normal
        high = pushed.astype(BF16)
        rest = (pushed - high.astype(F32)).astype(BF16)
        lhs = jnp.concatenate([jnp.where(odd, zero, high), jnp.where(odd, high, zero)], axis=1)
        parts = []
        for w in weights:
            r = dot(lhs, w)
            parts.append(jnp.where(late, r[:, nodes:], r[:, :nodes]))
        back = (-choose(parts)).astype(BF16)
        for c in range(3):
            rows = slice(GROUP * c, GROUP * (c + 1))
            cols = slice(nodes * c, nodes * (c + 1))
            back_ref[own, cols] = back[rows]
            pushed_ref[own, cols] = high[rows]
            pushed_ref[segs + GROUP * g : segs + GROUP * (g + 1), cols] = rest[rows]
    store = pltpu.make_async_copy(pushed_ref, pushed_hbm, sems.at[0])
    store.start()
    stores = edges + [store]

    def send(piece, part):
        stores.append(pltpu.make_async_copy(out_ref.at[part], out_hbm.at[part], sems.at[1 + piece]))
        stores[-1].start()

    place(dot(put_ref[...], back_ref[...]), scratch, out_ref, send)
    for copy in stores:
        copy.wait()


def bulk_kernel(whole, take, out, give, rounded_ref, product_ref):
    out_ref = out[0]
    _, layers, blocks, width = out_ref.shape
    rows = layers * blocks
    step = (rows + 2 * blocks) // PARTS
    field_ref, layer_ref = take(0), take(1)
    zero = jnp.zeros((blocks, width), BF16)
    rounded_ref[:blocks] = take(7)[...] if whole else zero
    rounded_ref[blocks : 2 * blocks] = layer_ref[...].astype(BF16)
    for l in range(1, layers):
        rounded_ref[(l + 1) * blocks : (l + 2) * blocks] = field_ref[0, l].astype(BF16)
    rounded_ref[rows + blocks :] = take(8)[...] if whole else zero
    weight_refs = [take(i) for i in (2, 3, 4)]

    @pl.loop(0, PARTS)
    def multiply(p):
        here = pl.ds(pl.multiple_of(p * step, 16), step)
        part = rounded_ref[here]
        for k, weight_ref in enumerate(weight_refs):
            product_ref[here, k * width : (k + 1) * width] = dot(part, weight_ref[...])

    block = iota((blocks, width), 0)

    def inner(l):
        def product(layer, k):
            return product_ref[pl.ds(pl.multiple_of(layer * blocks, blocks), blocks), k * width : (k + 1) * width]

        side = product(l + 1, 2)
        left = jnp.where(block == 0, 0.0, pltpu.roll(side, 1, 0))
        right = jnp.where(block == blocks - 1, 0.0, pltpu.roll(side, blocks - 1, 0))
        return product(l + 1, 0) + (product(l, 1) + product(l + 2, 1)) + (left + right)

    load_ref, scale_ref = take(5), take(6)

    def stepped(old, l, force):
        return old + scale_ref[0, l].astype(F32) * (load_ref[0, l].astype(F32) - force)

    first = inner(0)
    if whole:
        base_ref, near_ref, pick_ref, last_ref = out[1:5]
        pick_ref[...] = take(11)[...]
        near_ref[...] = scale_ref[0, 0].astype(F32)
        first = first + dot(take(10)[...], take(9)[...])
        base_ref[...] = stepped(layer_ref[...], 0, first)
    out_ref[0, 0] = stepped(layer_ref[...], 0, first)

    @pl.loop(1, layers)
    def update(l):
        out_ref[0, l] = stepped(field_ref[0, l], l, inner(l))

    give(0)
    if whole:
        last_ref[...] = out_ref[0, layers - 1].astype(BF16)
        give(4)


def tail_kernel(take, out, give):
    first, last, first_scale, last_scale = [take(i)[...].astype(F32) for i in range(4)]
    base_ref, row_ref, scale0_ref, scale1_ref, pick_ref, weight_ref = out
    base_ref[...] = first - first_scale * dot(take(5)[...], take(4)[...])
    row_ref[...] = last
    scale0_ref[...] = first_scale
    scale1_ref[...] = last_scale
    pick_ref[...] = take(6)[...]
    weight_ref[...] = take(7)[...]


def summed(in_ref, pick_ref, base_ref, scale_ref, scratch):
    sums = dot(pick_ref[...], gathered(in_ref, scratch), ((0,), (0,)))
    blocks = base_ref.shape[0]
    total = sums[:blocks]
    for k in range(1, CAPACITY):
        total = total + sums[k * blocks : (k + 1) * blocks]
    return base_ref[...] - scale_ref[...] * total


def next_kernel(in_ref, pick_ref, base_ref, scale_ref, take, out, give, scratch):
    out_ref, layer_ref, high_ref = out
    first = summed(in_ref, pick_ref, base_ref, scale_ref, scratch)
    layer_ref[0, 0] = first
    give(1)
    surface = first.astype(BF16)
    high_ref[...] = surface
    give(2)
    place(dot(pick_ref[...], copies(surface)), scratch, out_ref, lambda piece, part: give(0, part, piece))


def last_kernel(
    in_ref, base_ref, row_ref, scale0_ref, scale1_ref, pick_ref, weight_ref, low_ref, high_ref, field_hbm,
    out_hbm, scratch, first_ref, last_ref, sems,
):
    end = out_hbm.shape[1] - 1
    last_ref[...] = row_ref[...] - scale1_ref[...] * dot(high_ref[...], weight_ref[...])
    stores = [pltpu.make_async_copy(last_ref, out_hbm.at[0, end], sems.at[0])]
    stores[0].start()
    below = scale0_ref[...] * dot(low_ref[...], weight_ref[...])
    first_ref[...] = summed(in_ref, pick_ref, base_ref, scale0_ref, scratch) - below
    stores.append(pltpu.make_async_copy(first_ref, out_hbm.at[0, 0], sems.at[1]))
    stores[1].start()
    for store in stores:
        store.wait()


def shift(block, step):
    count = lax.axis_size("slab")
    pairs = [(i, i + step) for i in range(count) if 0 <= i + step < count]
    return lax.ppermute(block, "slab", pairs)


def exchange(parts):
    return lax.all_to_all(parts, "dom", 0, 0, tiled=True)


def on_device(
    disp, f_ext, inv_diag, k_self, k_layer, k_side, mortar, gap0, normals, seg_slave, seg_src, seg_master
):
    _, layers, blocks, width = disp.shape
    segs = seg_slave.shape[2]
    count = lax.axis_size("dom")
    slots = count * CAPACITY
    wide = CAPACITY * blocks
    rows_scratch = VMEM((slots, width), F32)
    message = shaped((count, CAPACITY, width), BF16)
    edge = shaped((blocks, width), BF16)
    layer = shaped((blocks, width), F32)

    early = max(segs * 5 // 8 // GROUP, 1) * GROUP
    early_part = (0, 0, pl.ds(0, early))
    (asked,) = staged(
        lambda *refs: request_kernel(blocks, *refs), [seg_src, seg_master], [shaped((count, wide), F32)], free_outs=True
    )
    put, get, pick3, back_sum, normal_rows, low, high, surface, *ready, gap = staged(
        prep_kernel,
        [seg_src, seg_slave, (normals, (0, 0)), (disp, (0, 0)), (disp, (0, layers - 1)), (gap0, (0, 0))],
        [
            shaped((slots, segs), BF16),
            shaped((segs, slots), BF16),
            shaped((segs, 3 * blocks), BF16),
            shaped((blocks, 2 * segs), BF16),
            shaped((segs, width), F32),
            edge,
            edge,
            shaped((CAPACITY * blocks, width), BF16),
            shaped((early,) + mortar.shape[3:], BF16),
            shaped((segs, slots), BF16),
            shaped((slots, segs), BF16),
            shaped((segs, width), F32),
            shaped(gap0.shape[2:], F32),
        ],
        tokens=[asked],
        kept=(7, 8, 9, 10, 11, 12),
        fills=[(mortar, early_part, 8)],
    )
    asked = exchange(asked.reshape(count, 1, wide)).reshape(count, wide)
    pick, sent = staged(
        first_kernel, [], [shaped((slots, wide), BF16), message], [rows_scratch], direct=(asked, surface)
    )

    def contact(arrived, near_arrays, low, high, token):
        here = [pltpu.with_memory_space_constraint(array, pltpu.VMEM) for array in (arrived, *near_arrays)]
        pushed = shaped((2 * segs, width), BF16)
        return pl.pallas_call(
            contact_kernel,
            out_shape=[pltpu.HBM(out.shape, BF16) for out in (message, pushed, edge, edge)],
            in_specs=[IN_VMEM] * 6 + [ANY] * 4,
            out_specs=[ANY] * 4,
            scratch_shapes=[
                rows_scratch,
                VMEM((segs, width), BF16),
                VMEM(message.shape, BF16),
                VMEM(pushed.shape, BF16),
                VMEM((segs - early,) + mortar.shape[3:], BF16),
                pltpu.SemaphoreType.DMA((1 + PIECES,)),
                pltpu.SemaphoreType.DMA((3,)),
            ],
            compiler_params=pltpu.CompilerParams(vmem_limit_bytes=16 * 2**20),
        )(*here, *in_hbm(mortar), low, high, *in_hbm(token))

    rows = (layers + 2) * blocks
    bulk_scratch = [VMEM((rows, width), BF16), VMEM((rows, 3 * width), F32)]
    steady = [k_self, k_layer, k_side, f_ext, inv_diag]
    near_shape = shaped((slots, wide), BF16)

    arrived = exchange(sent)
    low, high = shift(low, 1), shift(high, -1)
    sent, pushed, low, high = contact(arrived, [*ready, gap], low, high, pick)
    returned = exchange(sent)
    field, base, scale, near, last, *ready = staged(
        lambda *refs: bulk_kernel(True, *refs),
        [disp, (disp, (0, 0)), *steady, low, high, pushed, back_sum, pick],
        [shaped(disp.shape, F32), layer, layer, near_shape, edge] + [shaped(array.shape, array.dtype) for array in ready],
        bulk_scratch,
        kept=(1, 2, 3, 5, 6, 7, 8),
        fills=[(mortar, early_part, 5), (get, (), 6), (put, (), 7), (normal_rows, (), 8)],
    )
    sent, layer0, high = staged(
        next_kernel,
        [],
        [message, shaped((1, 1, blocks, width), F32), edge],
        [rows_scratch],
        direct=(returned, near, base, scale),
    )
    arrived = exchange(sent)
    (field,) = staged(
        lambda *refs: bulk_kernel(False, *refs),
        [field, (layer0, (0, 0)), *steady],
        [shaped(disp.shape, F32)],
        bulk_scratch,
    )
    (gap,) = staged(
        known_kernel, [(layer0, (0, 0)), pick3, normal_rows, (gap0, (0, 0))], [shaped(gap0.shape[2:], F32)], kept=(0,)
    )
    sent, pushed, low, high = contact(arrived, [*ready, gap], *in_hbm(last, high), field)
    returned = exchange(sent)
    low, high = shift(low, 1), shift(high, -1)
    ends = [(array, (0, l)) for array in (field, inv_diag) for l in (0, layers - 1)]
    held = staged(
        tail_kernel,
        ends + [pushed, back_sum, pick, k_layer],
        [layer, layer, layer, layer, near_shape, shaped(k_layer.shape, BF16)],
        kept=range(6),
    )
    return pl.pallas_call(
        last_kernel,
        out_shape=pltpu.HBM(disp.shape, F32),
        in_specs=[IN_VMEM] * 9 + [HBM],
        out_specs=HBM,
        scratch_shapes=[
            rows_scratch, VMEM(base.shape, F32), VMEM(base.shape, F32), pltpu.SemaphoreType.DMA((2,))
        ],
        input_output_aliases={9: 0},
        compiler_params=pltpu.CompilerParams(vmem_limit_bytes=16 * 2**20),
    )(
        *[pltpu.with_memory_space_constraint(array, pltpu.VMEM) for array in (returned, *held, low, high)],
        *in_hbm(field),
    )


def solution(mesh):
    in_specs = (
        P("dom", "slab", None, None),
        P("dom", "slab", None, None),
        P("dom", "slab", None, None),
        P(),
        P(),
        P(),
        P("dom", "slab", None, None, None),
        P("dom", "slab", None, None),
        P("dom", "slab", None, None),
        P("dom", "slab", None),
        P("dom", "slab", None),
        P("dom", "slab", None),
    )
    return jax.shard_map(
        on_device, mesh=mesh, in_specs=in_specs, out_specs=P("dom", "slab", None, None), check_vma=False
    )
```

```python
import jax
import jax.numpy as jnp
from jax import lax
from jax.experimental import pallas as pl
from jax.experimental.pallas import tpu as pltpu
from jax.sharding import PartitionSpec as P

PENALTY = 2.0
CAPACITY = 4
GROUP = 16
HALF = 8
PIECES = 4
PARTS = 2
VMEM = pltpu.VMEM
HBM = pl.BlockSpec(memory_space=pltpu.HBM)
ANY = pl.BlockSpec(memory_space=pl.ANY)
IN_VMEM = pl.BlockSpec(memory_space=VMEM)
BF16 = jnp.bfloat16
F32 = jnp.float32


def dot(a, b, dims=((1,), (0,))):
    return lax.dot_general(a, b, (dims, ((), ())), preferred_element_type=F32)


def iota(shape, axis):
    return lax.broadcasted_iota(jnp.int32, shape, axis)


def shaped(shape, dtype):
    return jax.ShapeDtypeStruct(shape, dtype)


def in_hbm(*arrays):
    return [pltpu.with_memory_space_constraint(array, pltpu.HBM) for array in arrays]


def staged(body, ins, outs, scratch=(), tokens=(), loose=(), free_outs=False, direct=(), kept=(), fills=()):
    ins = [item if isinstance(item, tuple) else (item, ()) for item in ins]
    operands = [array if i in loose else in_hbm(array)[0] for i, (array, _) in enumerate(ins)]
    held = [VMEM(part_shape(array, index), array.dtype) for array, index in ins]
    given = [VMEM(out.shape, out.dtype) for i, out in enumerate(outs) if i not in kept]
    here = [pltpu.with_memory_space_constraint(array, pltpu.VMEM) for array in direct]

    def kernel(*refs):
        refs = list(refs)

        def pop(count):
            taken = refs[:count]
            del refs[:count]
            return taken

        landed, sources, fill_sources = pop(len(here)), pop(len(ins)), pop(len(fills))
        _, targets = pop(len(tokens)), pop(len(outs))
        inside, leaving, (in_sems, out_sems, fill_sems), extra = pop(len(ins)), pop(len(given)), pop(3), refs
        leaving = [targets[i] if i in kept else leaving.pop(0) for i in range(len(outs))]
        loads = {}
        for i, (source, ref, (_, index)) in enumerate(zip(sources, inside, ins)):
            loads[i] = pltpu.make_async_copy(source.at[index] if index else source, ref, in_sems.at[i])
            loads[i].start()

        stores = []
        for i, (source, (_, index, out)) in enumerate(zip(fill_sources, fills)):
            stores.append(pltpu.make_async_copy(source.at[index] if index else source, targets[out], fill_sems.at[i]))
            stores[-1].start()

        def take(i):
            if i in loads:
                loads.pop(i).wait()
            return inside[i]

        def give(i, index=None, piece=None):
            source, target = leaving[i], targets[i]
            if index is not None:
                source, target = source.at[index], target.at[index]
            sem = out_sems.at[i if piece is None else len(outs) + piece]
            stores.append(pltpu.make_async_copy(source, target, sem))
            stores[-1].start()

        body(*landed, take, leaving, give, *extra)
        assert not loads
        for store in stores:
            store.wait()

    def space(i, out):
        return out if free_outs else (pltpu.VMEM if i in kept else pltpu.HBM)(out.shape, out.dtype)

    return pl.pallas_call(
        kernel,
        out_shape=tuple(space(i, out) for i, out in enumerate(outs)),
        in_specs=[IN_VMEM] * len(here) + [ANY] * (len(ins) + len(fills) + len(tokens)),
        out_specs=tuple(IN_VMEM if i in kept else ANY for i in range(len(outs))),
        scratch_shapes=held
        + given
        + [pltpu.SemaphoreType.DMA((max(count, 1),)) for count in (len(ins), len(outs) + PIECES, len(fills))]
        + list(scratch),
        compiler_params=pltpu.CompilerParams(vmem_limit_bytes=32 * 2**20),
    )(*here, *operands, *in_hbm(*[array for array, _, _ in fills]), *tokens)


def part_shape(array, index):
    kept = [i.size for i in index if not isinstance(i, int)]
    return tuple(kept) + array.shape[len(index) :]


def slots_of(src, count):
    segs = src.shape[1]
    named = (iota((count, segs), 0) == src).astype(BF16)
    earlier = (iota((segs, segs), 0) < iota((segs, segs), 1)).astype(BF16)
    before = dot(named, earlier)
    rank = jnp.sum(named.astype(F32) * before, axis=0, keepdims=True).astype(jnp.int32)
    return named, rank


def request_kernel(blocks, take, out, give):
    src, master = take(0)[0], take(1)[0]
    count = out[0].shape[0]
    named, rank = slots_of(src, count)
    segs = named.shape[1]
    wants = (iota((CAPACITY * blocks, segs), 0) == rank * blocks + master).astype(BF16)
    out[0][...] = dot(named, wants, ((1,), (1,)))
    give(0)


def split3(rows):
    high = rows.astype(BF16)
    rest = rows - high.astype(F32)
    mid = rest.astype(BF16)
    low = (rest - mid.astype(F32)).astype(BF16)
    return jnp.concatenate([high, mid, low], axis=0)


def prep_kernel(take, out, give):
    put_ref, get_ref, take_ref, sum_ref, normal_rows_ref, low_ref, high_ref, surface_ref, _, get_v, put_v, normal_v, known_ref = out
    surface = take(3)[...].astype(BF16)
    surface_ref[...] = copies(surface)
    high_ref[...] = surface
    low_ref[...] = take(4)[...].astype(BF16)
    give(5)
    give(6)
    src, slave, normals = take(0)[0], take(1)[0], take(2)[...]
    blocks = normals.shape[0]
    slots, segs = put_ref.shape
    _, rank = slots_of(src, slots // CAPACITY)
    put = (iota((slots, segs), 0) == src * CAPACITY + rank).astype(F32)
    put_ref[...] = put.astype(BF16)
    give(0)
    get_ref[...] = jnp.transpose(put).astype(BF16)
    give(1)
    spread = (lax.rem(iota((4 * blocks, segs), 0), blocks) == slave).astype(F32)
    pick = jnp.transpose(spread)[:, : 3 * blocks].astype(BF16)
    take_ref[...] = pick
    give(2)
    once = spread[:blocks].astype(BF16)
    sum_ref[...] = jnp.concatenate([once, once], axis=1)
    give(3)
    normal_rows = dot(pick, split3(normals))
    normal_rows_ref[...] = normal_rows
    give(4)
    put_v[...] = put_ref[...]
    get_v[...] = get_ref[...]
    normal_v[...] = normal_rows
    known_ref[...] = known(take(5)[...], normal_rows, dot(pick, split3(take(3)[...])))


def known(gap, normal_rows, slave_rows):
    x, y, z = columns(normal_rows * slave_rows)
    return gap - (x + y + z)


def columns(rows):
    nodes = rows.shape[1] // 3
    return [rows[:, c * nodes : (c + 1) * nodes] for c in range(3)]


def known_kernel(take, out, give):
    slave_rows = dot(take(1)[...], split3(take(0)[...]))
    out[0][...] = known(take(3)[...], take(2)[...], slave_rows)


def place(rows, scratch, out_ref, send):
    scratch[...] = rows
    pairs = out_ref.shape[0] // 2
    part = pairs // PIECES
    for j in range(pairs):
        both = scratch[2 * CAPACITY * j : 2 * CAPACITY * (j + 1), :]
        out_ref[2 * j] = both[:CAPACITY].astype(BF16)
        out_ref[2 * j + 1] = both[CAPACITY:].astype(BF16)
        if (j + 1) % part == 0:
            send(j // part, pl.ds(2 * (j + 1 - part), 2 * part))


def gathered(in_ref, scratch):
    for j in range(in_ref.shape[0] // 2):
        both = jnp.concatenate([in_ref[2 * j].astype(F32), in_ref[2 * j + 1].astype(F32)], axis=0)
        scratch[2 * CAPACITY * j : 2 * CAPACITY * (j + 1), :] = both
    return scratch[...].astype(BF16)


def copies(rows):
    return jnp.concatenate([rows] * CAPACITY, axis=0)


def first_kernel(asked_ref, surface_ref, take, out, give, scratch):
    pick_ref, out_ref = out
    slots, wide = pick_ref.shape
    count, blocks = slots // CAPACITY, wide // CAPACITY
    expand = (lax.div(iota((slots, count), 0), CAPACITY) == iota((slots, count), 1)).astype(BF16)
    mine = lax.div(iota((slots, wide), 1), blocks) == lax.rem(iota((slots, wide), 0), CAPACITY)
    rows = dot(expand, asked_ref[...].astype(BF16))
    pick = jnp.where(mine, rows, 0.0).astype(BF16)
    pick_ref[...] = pick
    give(0)
    place(dot(pick, surface_ref[...]), scratch, out_ref, lambda piece, part: give(1, part, piece))


def contact_kernel(
    in_ref, early_ref, get_ref, put_ref, normal_ref, known_ref, mortar_hbm, low_hbm, high_hbm, token,
    out_hbm, pushed_hbm, low_out, high_out, scratch, back_ref, out_ref, pushed_ref, later_ref, sems, later_sems,
):
    early, _, nodes = early_ref.shape
    segs = early + later_ref.shape[0]
    later = pltpu.make_async_copy(mortar_hbm.at[0, 0, pl.ds(early, segs - early)], later_ref, later_sems.at[0])
    later.start()
    edges = [
        pltpu.make_async_copy(low_hbm, low_out, later_sems.at[1]),
        pltpu.make_async_copy(high_hbm, high_out, later_sems.at[2]),
    ]
    for edge in edges:
        edge.start()
    member = lax.rem(iota((3 * HALF, nodes), 0), HALF)
    place_in = lax.rem(member, 4)
    second = member >= 4
    odd = lax.rem(place_in, 2) == 1
    late = place_in >= 2
    master = dot(get_ref[...], gathered(in_ref, scratch))

    def apart(chosen, rows):
        return jnp.concatenate([jnp.where(chosen, 0.0, rows), jnp.where(chosen, rows, 0.0)], axis=1).astype(BF16)

    def joined(halves, c):
        return jnp.concatenate([half[HALF * c : HALF * (c + 1)] for half in halves], axis=0)

    for g in range(segs // GROUP):
        if GROUP * g == early:
            later.wait()
        backs, pushes = [], []
        for start in range(GROUP * g, GROUP * (g + 1), HALF):
            own = slice(start, start + HALF)
            um = jnp.concatenate(columns(master[own]), axis=0)
            normal = jnp.concatenate(columns(normal_ref[own, :]), axis=0)
            mortar_ref, s = (early_ref, start) if start < early else (later_ref, start - early)
            weights = []
            for k in (s, s + 4):
                left = mortar_ref[k : k + 2].reshape(2 * nodes, nodes)
                right = mortar_ref[k + 2 : k + 4].reshape(2 * nodes, nodes)
                weights.append(jnp.concatenate([left, right], axis=1))
            lhs = apart(late, um)
            parts = []
            for w in weights:
                r = dot(lhs, w, ((1,), (1,)))
                parts.append(jnp.where(odd, r[:, nodes:], r[:, :nodes]))
            terms = normal * jnp.where(second, parts[1], parts[0])
            gap = known_ref[own, :] + (terms[:HALF] + terms[HALF : 2 * HALF] + terms[2 * HALF :])
            pressure = PENALTY * jnp.maximum(-gap, 0.0)
            pushed = jnp.concatenate([pressure] * 3, axis=0) * normal
            lhs = apart(odd, pushed)
            parts = []
            for w in weights:
                r = dot(lhs, w)
                parts.append(jnp.where(late, r[:, nodes:], r[:, :nodes]))
            backs.append(-jnp.where(second, parts[1], parts[0]))
            pushes.append(pushed)
        own = slice(GROUP * g, GROUP * (g + 1))
        for c in range(3):
            cols = slice(nodes * c, nodes * (c + 1))
            back_ref[own, cols] = joined(backs, c).astype(BF16)
            pushed = joined(pushes, c)
            high = pushed.astype(BF16)
            pushed_ref[own, cols] = high
            pushed_ref[segs + GROUP * g : segs + GROUP * (g + 1), cols] = (pushed - high.astype(F32)).astype(BF16)
    store = pltpu.make_async_copy(pushed_ref, pushed_hbm, sems.at[0])
    store.start()
    stores = edges + [store]

    def send(piece, part):
        stores.append(pltpu.make_async_copy(out_ref.at[part], out_hbm.at[part], sems.at[1 + piece]))
        stores[-1].start()

    place(dot(put_ref[...], back_ref[...]), scratch, out_ref, send)
    for copy in stores:
        copy.wait()


def bulk_kernel(whole, take, out, give, rounded_ref, product_ref):
    out_ref = out[0]
    _, layers, blocks, width = out_ref.shape
    rows = layers * blocks
    step = (rows + 2 * blocks) // PARTS
    field_ref, layer_ref = take(0), take(1)
    zero = jnp.zeros((blocks, width), BF16)
    rounded_ref[:blocks] = take(7)[...] if whole else zero
    rounded_ref[blocks : 2 * blocks] = layer_ref[...].astype(BF16)
    for l in range(1, layers):
        rounded_ref[(l + 1) * blocks : (l + 2) * blocks] = field_ref[0, l].astype(BF16)
    rounded_ref[rows + blocks :] = take(8)[...] if whole else zero
    weight_refs = [take(i) for i in (2, 3, 4)]

    @pl.loop(0, PARTS)
    def multiply(p):
        here = pl.ds(pl.multiple_of(p * step, 16), step)
        part = rounded_ref[here]
        for k, weight_ref in enumerate(weight_refs):
            product_ref[here, k * width : (k + 1) * width] = dot(part, weight_ref[...])

    block = iota((blocks, width), 0)

    def inner(l):
        def product(layer, k):
            return product_ref[pl.ds(pl.multiple_of(layer * blocks, blocks), blocks), k * width : (k + 1) * width]

        side = product(l + 1, 2)
        left = jnp.where(block == 0, 0.0, pltpu.roll(side, 1, 0))
        right = jnp.where(block == blocks - 1, 0.0, pltpu.roll(side, blocks - 1, 0))
        return product(l + 1, 0) + (product(l, 1) + product(l + 2, 1)) + (left + right)

    load_ref, scale_ref = take(5), take(6)

    def stepped(old, l, force):
        return old + scale_ref[0, l].astype(F32) * (load_ref[0, l].astype(F32) - force)

    first = inner(0)
    if whole:
        base_ref, near_ref, pick_ref, last_ref = out[1:5]
        pick_ref[...] = take(11)[...]
        near_ref[...] = scale_ref[0, 0].astype(F32)
        first = first + dot(take(10)[...], take(9)[...])
        base_ref[...] = stepped(layer_ref[...], 0, first)
    out_ref[0, 0] = stepped(layer_ref[...], 0, first)

    @pl.loop(1, layers)
    def update(l):
        out_ref[0, l] = stepped(field_ref[0, l], l, inner(l))

    give(0)
    if whole:
        last_ref[...] = out_ref[0, layers - 1].astype(BF16)
        give(4)


def tail_kernel(take, out, give):
    first, last, first_scale, last_scale = [take(i)[...].astype(F32) for i in range(4)]
    base_ref, row_ref, scale0_ref, scale1_ref, pick_ref, weight_ref = out
    base_ref[...] = first - first_scale * dot(take(5)[...], take(4)[...])
    row_ref[...] = last
    scale0_ref[...] = first_scale
    scale1_ref[...] = last_scale
    pick_ref[...] = take(6)[...]
    weight_ref[...] = take(7)[...]


def summed(in_ref, pick_ref, base_ref, scale_ref, scratch):
    sums = dot(pick_ref[...], gathered(in_ref, scratch), ((0,), (0,)))
    blocks = base_ref.shape[0]
    total = sums[:blocks]
    for k in range(1, CAPACITY):
        total = total + sums[k * blocks : (k + 1) * blocks]
    return base_ref[...] - scale_ref[...] * total


def next_kernel(in_ref, pick_ref, base_ref, scale_ref, take, out, give, scratch):
    out_ref, layer_ref, high_ref = out
    first = summed(in_ref, pick_ref, base_ref, scale_ref, scratch)
    layer_ref[0, 0] = first
    give(1)
    surface = first.astype(BF16)
    high_ref[...] = surface
    give(2)
    place(dot(pick_ref[...], copies(surface)), scratch, out_ref, lambda piece, part: give(0, part, piece))


def last_kernel(
    in_ref, base_ref, row_ref, scale0_ref, scale1_ref, pick_ref, weight_ref, low_ref, high_ref, field_hbm,
    out_hbm, scratch, first_ref, last_ref, sems,
):
    end = out_hbm.shape[1] - 1
    last_ref[...] = row_ref[...] - scale1_ref[...] * dot(high_ref[...], weight_ref[...])
    stores = [pltpu.make_async_copy(last_ref, out_hbm.at[0, end], sems.at[0])]
    stores[0].start()
    below = scale0_ref[...] * dot(low_ref[...], weight_ref[...])
    first_ref[...] = summed(in_ref, pick_ref, base_ref, scale0_ref, scratch) - below
    stores.append(pltpu.make_async_copy(first_ref, out_hbm.at[0, 0], sems.at[1]))
    stores[1].start()
    for store in stores:
        store.wait()


def shift(block, step):
    count = lax.axis_size("slab")
    pairs = [(i, i + step) for i in range(count) if 0 <= i + step < count]
    return lax.ppermute(block, "slab", pairs)


def exchange(parts):
    return lax.all_to_all(parts, "dom", 0, 0, tiled=True)


def on_device(
    disp, f_ext, inv_diag, k_self, k_layer, k_side, mortar, gap0, normals, seg_slave, seg_src, seg_master
):
    _, layers, blocks, width = disp.shape
    segs = seg_slave.shape[2]
    count = lax.axis_size("dom")
    slots = count * CAPACITY
    wide = CAPACITY * blocks
    rows_scratch = VMEM((slots, width), F32)
    message = shaped((count, CAPACITY, width), BF16)
    edge = shaped((blocks, width), BF16)
    layer = shaped((blocks, width), F32)

    early = max(segs * 5 // 8 // GROUP, 1) * GROUP
    early_part = (0, 0, pl.ds(0, early))
    (asked,) = staged(
        lambda *refs: request_kernel(blocks, *refs), [seg_src, seg_master], [shaped((count, wide), F32)], free_outs=True
    )
    put, get, pick3, back_sum, normal_rows, low, high, surface, *ready, gap = staged(
        prep_kernel,
        [seg_src, seg_slave, (normals, (0, 0)), (disp, (0, 0)), (disp, (0, layers - 1)), (gap0, (0, 0))],
        [
            shaped((slots, segs), BF16),
            shaped((segs, slots), BF16),
            shaped((segs, 3 * blocks), BF16),
            shaped((blocks, 2 * segs), BF16),
            shaped((segs, width), F32),
            edge,
            edge,
            shaped((CAPACITY * blocks, width), BF16),
            shaped((early,) + mortar.shape[3:], BF16),
            shaped((segs, slots), BF16),
            shaped((slots, segs), BF16),
            shaped((segs, width), F32),
            shaped(gap0.shape[2:], F32),
        ],
        tokens=[asked],
        kept=(7, 8, 9, 10, 11, 12),
        fills=[(mortar, early_part, 8)],
    )
    asked = exchange(asked.reshape(count, 1, wide)).reshape(count, wide)
    pick, sent = staged(
        first_kernel, [], [shaped((slots, wide), BF16), message], [rows_scratch], direct=(asked, surface)
    )

    def contact(arrived, near_arrays, low, high, token):
        here = [pltpu.with_memory_space_constraint(array, pltpu.VMEM) for array in (arrived, *near_arrays)]
        pushed = shaped((2 * segs, width), BF16)
        return pl.pallas_call(
            contact_kernel,
            out_shape=[pltpu.HBM(out.shape, BF16) for out in (message, pushed, edge, edge)],
            in_specs=[IN_VMEM] * 6 + [ANY] * 4,
            out_specs=[ANY] * 4,
            scratch_shapes=[
                rows_scratch,
                VMEM((segs, width), BF16),
                VMEM(message.shape, BF16),
                VMEM(pushed.shape, BF16),
                VMEM((segs - early,) + mortar.shape[3:], BF16),
                pltpu.SemaphoreType.DMA((1 + PIECES,)),
                pltpu.SemaphoreType.DMA((3,)),
            ],
            compiler_params=pltpu.CompilerParams(vmem_limit_bytes=16 * 2**20),
        )(*here, *in_hbm(mortar), low, high, *in_hbm(token))

    rows = (layers + 2) * blocks
    bulk_scratch = [VMEM((rows, width), BF16), VMEM((rows, 3 * width), F32)]
    steady = [k_self, k_layer, k_side, f_ext, inv_diag]
    near_shape = shaped((slots, wide), BF16)

    arrived = exchange(sent)
    low, high = shift(low, 1), shift(high, -1)
    sent, pushed, low, high = contact(arrived, [*ready, gap], low, high, pick)
    returned = exchange(sent)
    field, base, scale, near, last, *ready = staged(
        lambda *refs: bulk_kernel(True, *refs),
        [disp, (disp, (0, 0)), *steady, low, high, pushed, back_sum, pick],
        [shaped(disp.shape, F32), layer, layer, near_shape, edge] + [shaped(array.shape, array.dtype) for array in ready],
        bulk_scratch,
        kept=(1, 2, 3, 5, 6, 7, 8),
        fills=[(mortar, early_part, 5), (get, (), 6), (put, (), 7), (normal_rows, (), 8)],
    )
    sent, layer0, high = staged(
        next_kernel,
        [],
        [message, shaped((1, 1, blocks, width), F32), edge],
        [rows_scratch],
        direct=(returned, near, base, scale),
    )
    arrived = exchange(sent)
    (field,) = staged(
        lambda *refs: bulk_kernel(False, *refs),
        [field, (layer0, (0, 0)), *steady],
        [shaped(disp.shape, F32)],
        bulk_scratch,
    )
    (gap,) = staged(
        known_kernel, [(layer0, (0, 0)), pick3, normal_rows, (gap0, (0, 0))], [shaped(gap0.shape[2:], F32)], kept=(0,)
    )
    sent, pushed, low, high = contact(arrived, [*ready, gap], *in_hbm(last, high), field)
    returned = exchange(sent)
    low, high = shift(low, 1), shift(high, -1)
    ends = [(array, (0, l)) for array in (field, inv_diag) for l in (0, layers - 1)]
    held = staged(
        tail_kernel,
        ends + [pushed, back_sum, pick, k_layer],
        [layer, layer, layer, layer, near_shape, shaped(k_layer.shape, BF16)],
        kept=range(6),
    )
    return pl.pallas_call(
        last_kernel,
        out_shape=pltpu.HBM(disp.shape, F32),
        in_specs=[IN_VMEM] * 9 + [HBM],
        out_specs=HBM,
        scratch_shapes=[
            rows_scratch, VMEM(base.shape, F32), VMEM(base.shape, F32), pltpu.SemaphoreType.DMA((2,))
        ],
        input_output_aliases={9: 0},
        compiler_params=pltpu.CompilerParams(vmem_limit_bytes=16 * 2**20),
    )(
        *[pltpu.with_memory_space_constraint(array, pltpu.VMEM) for array in (returned, *held, low, high)],
        *in_hbm(field),
    )


def solution(mesh):
    in_specs = (
        P("dom", "slab", None, None),
        P("dom", "slab", None, None),
        P("dom", "slab", None, None),
        P(),
        P(),
        P(),
        P("dom", "slab", None, None, None),
        P("dom", "slab", None, None),
        P("dom", "slab", None, None),
        P("dom", "slab", None),
        P("dom", "slab", None),
        P("dom", "slab", None),
    )
    return jax.shard_map(
        on_device, mesh=mesh, in_specs=in_specs, out_specs=P("dom", "slab", None, None), check_vma=False
    )
```

```python
import jax
import jax.numpy as jnp
from jax import lax
from jax.experimental import pallas as pl
from jax.experimental.pallas import tpu as pltpu
from jax.sharding import PartitionSpec as P

PENALTY = 2.0
CAPACITY = 4
GROUP = 16
PIECES = 4
PARTS = 2
VMEM = pltpu.VMEM
HBM = pl.BlockSpec(memory_space=pltpu.HBM)
ANY = pl.BlockSpec(memory_space=pl.ANY)
IN_VMEM = pl.BlockSpec(memory_space=VMEM)
BF16 = jnp.bfloat16
F32 = jnp.float32


def dot(a, b, dims=((1,), (0,))):
    return lax.dot_general(a, b, (dims, ((), ())), preferred_element_type=F32)


def iota(shape, axis):
    return lax.broadcasted_iota(jnp.int32, shape, axis)


def shaped(shape, dtype):
    return jax.ShapeDtypeStruct(shape, dtype)


def in_hbm(*arrays):
    return [pltpu.with_memory_space_constraint(array, pltpu.HBM) for array in arrays]


def staged(body, ins, outs, scratch=(), tokens=(), loose=(), free_outs=False, direct=(), kept=(), fills=()):
    ins = [item if isinstance(item, tuple) else (item, ()) for item in ins]
    operands = [array if i in loose else in_hbm(array)[0] for i, (array, _) in enumerate(ins)]
    held = [VMEM(part_shape(array, index), array.dtype) for array, index in ins]
    given = [VMEM(out.shape, out.dtype) for i, out in enumerate(outs) if i not in kept]
    here = [pltpu.with_memory_space_constraint(array, pltpu.VMEM) for array in direct]

    def kernel(*refs):
        refs = list(refs)

        def pop(count):
            taken = refs[:count]
            del refs[:count]
            return taken

        landed, sources, fill_sources = pop(len(here)), pop(len(ins)), pop(len(fills))
        _, targets = pop(len(tokens)), pop(len(outs))
        inside, leaving, (in_sems, out_sems, fill_sems), extra = pop(len(ins)), pop(len(given)), pop(3), refs
        leaving = [targets[i] if i in kept else leaving.pop(0) for i in range(len(outs))]
        loads = {}
        for i, (source, ref, (_, index)) in enumerate(zip(sources, inside, ins)):
            loads[i] = pltpu.make_async_copy(source.at[index] if index else source, ref, in_sems.at[i])
            loads[i].start()

        stores = []
        for i, (source, (_, index, out)) in enumerate(zip(fill_sources, fills)):
            stores.append(pltpu.make_async_copy(source.at[index] if index else source, targets[out], fill_sems.at[i]))
            stores[-1].start()

        def take(i):
            if i in loads:
                loads.pop(i).wait()
            return inside[i]

        def give(i, index=None, piece=None):
            source, target = leaving[i], targets[i]
            if index is not None:
                source, target = source.at[index], target.at[index]
            sem = out_sems.at[i if piece is None else len(outs) + piece]
            stores.append(pltpu.make_async_copy(source, target, sem))
            stores[-1].start()

        body(*landed, take, leaving, give, *extra)
        assert not loads
        for store in stores:
            store.wait()

    def space(i, out):
        return out if free_outs else (pltpu.VMEM if i in kept else pltpu.HBM)(out.shape, out.dtype)

    return pl.pallas_call(
        kernel,
        out_shape=tuple(space(i, out) for i, out in enumerate(outs)),
        in_specs=[IN_VMEM] * len(here) + [ANY] * (len(ins) + len(fills) + len(tokens)),
        out_specs=tuple(IN_VMEM if i in kept else ANY for i in range(len(outs))),
        scratch_shapes=held
        + given
        + [pltpu.SemaphoreType.DMA((max(count, 1),)) for count in (len(ins), len(outs) + PIECES, len(fills))]
        + list(scratch),
        compiler_params=pltpu.CompilerParams(vmem_limit_bytes=32 * 2**20),
    )(*here, *operands, *in_hbm(*[array for array, _, _ in fills]), *tokens)


def part_shape(array, index):
    kept = [i.size for i in index if not isinstance(i, int)]
    return tuple(kept) + array.shape[len(index) :]


def slots_of(src, count):
    segs = src.shape[1]
    named = (iota((count, segs), 0) == src).astype(BF16)
    earlier = (iota((segs, segs), 0) < iota((segs, segs), 1)).astype(BF16)
    before = dot(named, earlier)
    rank = jnp.sum(named.astype(F32) * before, axis=0, keepdims=True).astype(jnp.int32)
    return named, rank


def request_kernel(blocks, take, out, give):
    src, master = take(0)[0], take(1)[0]
    count = out[0].shape[0]
    named, rank = slots_of(src, count)
    segs = named.shape[1]
    wants = (iota((CAPACITY * blocks, segs), 0) == rank * blocks + master).astype(BF16)
    out[0][...] = dot(named, wants, ((1,), (1,)))
    give(0)


def split3(rows):
    high = rows.astype(BF16)
    rest = rows - high.astype(F32)
    mid = rest.astype(BF16)
    low = (rest - mid.astype(F32)).astype(BF16)
    return jnp.concatenate([high, mid, low], axis=0)


def prep_kernel(take, out, give):
    put_ref, get_ref, take_ref, sum_ref, normal_rows_ref, low_ref, high_ref, surface_ref, _, get_v, put_v, normal_v, known_ref = out
    surface = take(3)[...].astype(BF16)
    surface_ref[...] = copies(surface)
    high_ref[...] = surface
    low_ref[...] = take(4)[...].astype(BF16)
    give(5)
    give(6)
    src, slave, normals = take(0)[0], take(1)[0], take(2)[...]
    blocks = normals.shape[0]
    slots, segs = put_ref.shape
    _, rank = slots_of(src, slots // CAPACITY)
    put = (iota((slots, segs), 0) == src * CAPACITY + rank).astype(F32)
    put_ref[...] = put.astype(BF16)
    give(0)
    get_ref[...] = jnp.transpose(put).astype(BF16)
    give(1)
    spread = (lax.rem(iota((4 * blocks, segs), 0), blocks) == slave).astype(F32)
    pick = jnp.transpose(spread)[:, : 3 * blocks].astype(BF16)
    take_ref[...] = pick
    give(2)
    once = spread[:blocks].astype(BF16)
    sum_ref[...] = jnp.concatenate([once, once], axis=1)
    give(3)
    normal_rows = dot(pick, split3(normals))
    normal_rows_ref[...] = normal_rows
    give(4)
    put_v[...] = put_ref[...]
    get_v[...] = get_ref[...]
    normal_v[...] = normal_rows
    known_ref[...] = known(take(5)[...], normal_rows, dot(pick, split3(take(3)[...])))


def known(gap, normal_rows, slave_rows):
    x, y, z = columns(normal_rows * slave_rows)
    return gap - (x + y + z)


def columns(rows):
    nodes = rows.shape[1] // 3
    return [rows[:, c * nodes : (c + 1) * nodes] for c in range(3)]


def known_kernel(take, out, give):
    slave_rows = dot(take(1)[...], split3(take(0)[...]))
    out[0][...] = known(take(3)[...], take(2)[...], slave_rows)


def place(rows, scratch, out_ref, send):
    scratch[...] = rows
    pairs = out_ref.shape[0] // 2
    part = pairs // PIECES
    for j in range(pairs):
        both = scratch[2 * CAPACITY * j : 2 * CAPACITY * (j + 1), :]
        out_ref[2 * j] = both[:CAPACITY].astype(BF16)
        out_ref[2 * j + 1] = both[CAPACITY:].astype(BF16)
        if (j + 1) % part == 0:
            send(j // part, pl.ds(2 * (j + 1 - part), 2 * part))


def gathered(in_ref, scratch):
    for j in range(in_ref.shape[0] // 2):
        both = jnp.concatenate([in_ref[2 * j].astype(F32), in_ref[2 * j + 1].astype(F32)], axis=0)
        scratch[2 * CAPACITY * j : 2 * CAPACITY * (j + 1), :] = both
    return scratch[...].astype(BF16)


def copies(rows):
    return jnp.concatenate([rows] * CAPACITY, axis=0)


def first_kernel(asked_ref, surface_ref, take, out, give, scratch):
    pick_ref, out_ref = out
    slots, wide = pick_ref.shape
    count, blocks = slots // CAPACITY, wide // CAPACITY
    expand = (lax.div(iota((slots, count), 0), CAPACITY) == iota((slots, count), 1)).astype(BF16)
    mine = lax.div(iota((slots, wide), 1), blocks) == lax.rem(iota((slots, wide), 0), CAPACITY)
    rows = dot(expand, asked_ref[...].astype(BF16))
    pick = jnp.where(mine, rows, 0.0).astype(BF16)
    pick_ref[...] = pick
    give(0)
    place(dot(pick, surface_ref[...]), scratch, out_ref, lambda piece, part: give(1, part, piece))


def contact_kernel(
    in_ref, early_ref, get_ref, put_ref, normal_ref, known_ref, mortar_hbm, low_hbm, high_hbm, token,
    out_hbm, pushed_hbm, low_out, high_out, scratch, back_ref, out_ref, pushed_ref, later_ref, sems, later_sems,
):
    early, _, nodes = early_ref.shape
    segs = early + later_ref.shape[0]
    later = pltpu.make_async_copy(mortar_hbm.at[0, 0, pl.ds(early, segs - early)], later_ref, later_sems.at[0])
    later.start()
    edges = [
        pltpu.make_async_copy(low_hbm, low_out, later_sems.at[1]),
        pltpu.make_async_copy(high_hbm, high_out, later_sems.at[2]),
    ]
    for edge in edges:
        edge.start()
    member = lax.rem(iota((3 * GROUP, nodes), 0), GROUP)
    place_in = lax.rem(member, 4)
    block_of = lax.div(member, 4)
    odd = lax.rem(place_in, 2) == 1
    late = place_in >= 2
    zero = jnp.zeros((3 * GROUP, nodes), BF16)
    master = dot(get_ref[...], gathered(in_ref, scratch)).astype(BF16)

    def choose(parts):
        result = parts[0]
        for b in range(1, GROUP // 4):
            result = jnp.where(block_of == b, parts[b], result)
        return result

    def weights(g):
        ref, start = (early_ref, GROUP * g) if GROUP * g < early else (later_ref, GROUP * g - early)
        for k in range(start, start + GROUP, 4):
            left = ref[k : k + 2].reshape(2 * nodes, nodes)
            right = ref[k + 2 : k + 4].reshape(2 * nodes, nodes)
            yield jnp.concatenate([left, right], axis=1)

    for g in range(segs // GROUP):
        own = slice(GROUP * g, GROUP * (g + 1))
        if GROUP * g == early:
            later.wait()
        um = jnp.concatenate(columns(master[own]), axis=0)
        normal = jnp.concatenate(columns(normal_ref[own, :]), axis=0)
        lhs = jnp.concatenate([jnp.where(late, zero, um), jnp.where(late, um, zero)], axis=1)
        parts = []
        for w in weights(g):
            r = dot(lhs, w, ((1,), (1,)))
            parts.append(jnp.where(odd, r[:, nodes:], r[:, :nodes]))
        terms = normal * choose(parts)
        gap = known_ref[own, :] + (terms[:GROUP] + terms[GROUP : 2 * GROUP] + terms[2 * GROUP :])
        pressure = PENALTY * jnp.maximum(-gap, 0.0)
        for c, part in enumerate(columns(normal_ref[own, :])):
            cols = slice(nodes * c, nodes * (c + 1))
            pushed = pressure * part
            high = pushed.astype(BF16)
            pushed_ref[own, cols] = high
            pushed_ref[segs + GROUP * g : segs + GROUP * (g + 1), cols] = (pushed - high.astype(F32)).astype(BF16)
    store = pltpu.make_async_copy(pushed_ref, pushed_hbm, sems.at[0])
    store.start()
    for g in range(segs // GROUP):
        own = slice(GROUP * g, GROUP * (g + 1))
        high = jnp.concatenate(columns(pushed_ref[own, :]), axis=0)
        lhs = jnp.concatenate([jnp.where(odd, zero, high), jnp.where(odd, high, zero)], axis=1)
        parts = []
        for w in weights(g):
            r = dot(lhs, w)
            parts.append(jnp.where(late, r[:, nodes:], r[:, :nodes]))
        back = (-choose(parts)).astype(BF16)
        for c in range(3):
            back_ref[own, nodes * c : nodes * (c + 1)] = back[GROUP * c : GROUP * (c + 1)]
    stores = edges + [store]

    def send(piece, part):
        stores.append(pltpu.make_async_copy(out_ref.at[part], out_hbm.at[part], sems.at[1 + piece]))
        stores[-1].start()

    place(dot(put_ref[...], back_ref[...]), scratch, out_ref, send)
    for copy in stores:
        copy.wait()


def bulk_kernel(whole, take, out, give, rounded_ref, product_ref):
    out_ref = out[0]
    _, layers, blocks, width = out_ref.shape
    rows = layers * blocks
    step = (rows + 2 * blocks) // PARTS
    field_ref, layer_ref = take(0), take(1)
    zero = jnp.zeros((blocks, width), BF16)
    rounded_ref[:blocks] = take(7)[...] if whole else zero
    rounded_ref[blocks : 2 * blocks] = layer_ref[...].astype(BF16)
    for l in range(1, layers):
        rounded_ref[(l + 1) * blocks : (l + 2) * blocks] = field_ref[0, l].astype(BF16)
    rounded_ref[rows + blocks :] = take(8)[...] if whole else zero
    weight_refs = [take(i) for i in (2, 3, 4)]

    @pl.loop(0, PARTS)
    def multiply(p):
        here = pl.ds(pl.multiple_of(p * step, 16), step)
        part = rounded_ref[here]
        for k, weight_ref in enumerate(weight_refs):
            product_ref[here, k * width : (k + 1) * width] = dot(part, weight_ref[...])

    block = iota((blocks, width), 0)

    def inner(l):
        def product(layer, k):
            return product_ref[pl.ds(pl.multiple_of(layer * blocks, blocks), blocks), k * width : (k + 1) * width]

        side = product(l + 1, 2)
        left = jnp.where(block == 0, 0.0, pltpu.roll(side, 1, 0))
        right = jnp.where(block == blocks - 1, 0.0, pltpu.roll(side, blocks - 1, 0))
        return product(l + 1, 0) + (product(l, 1) + product(l + 2, 1)) + (left + right)

    load_ref, scale_ref = take(5), take(6)

    def stepped(old, l, force):
        return old + scale_ref[0, l].astype(F32) * (load_ref[0, l].astype(F32) - force)

    first = inner(0)
    if whole:
        base_ref, near_ref, pick_ref, last_ref = out[1:5]
        pick_ref[...] = take(11)[...]
        near_ref[...] = scale_ref[0, 0].astype(F32)
        first = first + dot(take(10)[...], take(9)[...])
        base_ref[...] = stepped(layer_ref[...], 0, first)
    out_ref[0, 0] = stepped(layer_ref[...], 0, first)

    @pl.loop(1, layers)
    def update(l):
        out_ref[0, l] = stepped(field_ref[0, l], l, inner(l))

    give(0)
    if whole:
        last_ref[...] = out_ref[0, layers - 1].astype(BF16)
        give(4)


def tail_kernel(take, out, give):
    first, last, first_scale, last_scale = [take(i)[...].astype(F32) for i in range(4)]
    base_ref, row_ref, scale0_ref, scale1_ref, pick_ref, weight_ref = out
    base_ref[...] = first - first_scale * dot(take(5)[...], take(4)[...])
    row_ref[...] = last
    scale0_ref[...] = first_scale
    scale1_ref[...] = last_scale
    pick_ref[...] = take(6)[...]
    weight_ref[...] = take(7)[...]


def summed(in_ref, pick_ref, base_ref, scale_ref, scratch):
    sums = dot(pick_ref[...], gathered(in_ref, scratch), ((0,), (0,)))
    blocks = base_ref.shape[0]
    total = sums[:blocks]
    for k in range(1, CAPACITY):
        total = total + sums[k * blocks : (k + 1) * blocks]
    return base_ref[...] - scale_ref[...] * total


def next_kernel(in_ref, pick_ref, base_ref, scale_ref, take, out, give, scratch):
    out_ref, layer_ref, high_ref = out
    first = summed(in_ref, pick_ref, base_ref, scale_ref, scratch)
    layer_ref[0, 0] = first
    give(1)
    surface = first.astype(BF16)
    high_ref[...] = surface
    give(2)
    place(dot(pick_ref[...], copies(surface)), scratch, out_ref, lambda piece, part: give(0, part, piece))


def last_kernel(
    in_ref, base_ref, row_ref, scale0_ref, scale1_ref, pick_ref, weight_ref, low_ref, high_ref, field_hbm,
    out_hbm, scratch, first_ref, last_ref, sems,
):
    end = out_hbm.shape[1] - 1
    last_ref[...] = row_ref[...] - scale1_ref[...] * dot(high_ref[...], weight_ref[...])
    stores = [pltpu.make_async_copy(last_ref, out_hbm.at[0, end], sems.at[0])]
    stores[0].start()
    below = scale0_ref[...] * dot(low_ref[...], weight_ref[...])
    first_ref[...] = summed(in_ref, pick_ref, base_ref, scale0_ref, scratch) - below
    stores.append(pltpu.make_async_copy(first_ref, out_hbm.at[0, 0], sems.at[1]))
    stores[1].start()
    for store in stores:
        store.wait()


def shift(block, step):
    count = lax.axis_size("slab")
    pairs = [(i, i + step) for i in range(count) if 0 <= i + step < count]
    return lax.ppermute(block, "slab", pairs)


def exchange(parts):
    return lax.all_to_all(parts, "dom", 0, 0, tiled=True)


def on_device(
    disp, f_ext, inv_diag, k_self, k_layer, k_side, mortar, gap0, normals, seg_slave, seg_src, seg_master
):
    _, layers, blocks, width = disp.shape
    segs = seg_slave.shape[2]
    count = lax.axis_size("dom")
    slots = count * CAPACITY
    wide = CAPACITY * blocks
    rows_scratch = VMEM((slots, width), F32)
    message = shaped((count, CAPACITY, width), BF16)
    edge = shaped((blocks, width), BF16)
    layer = shaped((blocks, width), F32)

    early = max(segs * 5 // 8 // GROUP, 1) * GROUP
    early_part = (0, 0, pl.ds(0, early))
    (asked,) = staged(
        lambda *refs: request_kernel(blocks, *refs), [seg_src, seg_master], [shaped((count, wide), F32)], free_outs=True
    )
    put, get, pick3, back_sum, normal_rows, low, high, surface, *ready, gap = staged(
        prep_kernel,
        [seg_src, seg_slave, (normals, (0, 0)), (disp, (0, 0)), (disp, (0, layers - 1)), (gap0, (0, 0))],
        [
            shaped((slots, segs), BF16),
            shaped((segs, slots), BF16),
            shaped((segs, 3 * blocks), BF16),
            shaped((blocks, 2 * segs), BF16),
            shaped((segs, width), F32),
            edge,
            edge,
            shaped((CAPACITY * blocks, width), BF16),
            shaped((early,) + mortar.shape[3:], BF16),
            shaped((segs, slots), BF16),
            shaped((slots, segs), BF16),
            shaped((segs, width), F32),
            shaped(gap0.shape[2:], F32),
        ],
        tokens=[asked],
        kept=(7, 8, 9, 10, 11, 12),
        fills=[(mortar, early_part, 8)],
    )
    asked = exchange(asked.reshape(count, 1, wide)).reshape(count, wide)
    pick, sent = staged(
        first_kernel, [], [shaped((slots, wide), BF16), message], [rows_scratch], direct=(asked, surface)
    )

    def contact(arrived, near_arrays, low, high, token):
        here = [pltpu.with_memory_space_constraint(array, pltpu.VMEM) for array in (arrived, *near_arrays)]
        pushed = shaped((2 * segs, width), BF16)
        return pl.pallas_call(
            contact_kernel,
            out_shape=[pltpu.HBM(out.shape, BF16) for out in (message, pushed, edge, edge)],
            in_specs=[IN_VMEM] * 6 + [ANY] * 4,
            out_specs=[ANY] * 4,
            scratch_shapes=[
                rows_scratch,
                VMEM((segs, width), BF16),
                VMEM(message.shape, BF16),
                VMEM(pushed.shape, BF16),
                VMEM((segs - early,) + mortar.shape[3:], BF16),
                pltpu.SemaphoreType.DMA((1 + PIECES,)),
                pltpu.SemaphoreType.DMA((3,)),
            ],
            compiler_params=pltpu.CompilerParams(vmem_limit_bytes=16 * 2**20),
        )(*here, *in_hbm(mortar), low, high, *in_hbm(token))

    rows = (layers + 2) * blocks
    bulk_scratch = [VMEM((rows, width), BF16), VMEM((rows, 3 * width), F32)]
    steady = [k_self, k_layer, k_side, f_ext, inv_diag]
    near_shape = shaped((slots, wide), BF16)

    arrived = exchange(sent)
    low, high = shift(low, 1), shift(high, -1)
    sent, pushed, low, high = contact(arrived, [*ready, gap], low, high, pick)
    returned = exchange(sent)
    field, base, scale, near, last, *ready = staged(
        lambda *refs: bulk_kernel(True, *refs),
        [disp, (disp, (0, 0)), *steady, low, high, pushed, back_sum, pick],
        [shaped(disp.shape, F32), layer, layer, near_shape, edge] + [shaped(array.shape, array.dtype) for array in ready],
        bulk_scratch,
        kept=(1, 2, 3, 5, 6, 7, 8),
        fills=[(mortar, early_part, 5), (get, (), 6), (put, (), 7), (normal_rows, (), 8)],
    )
    sent, layer0, high = staged(
        next_kernel,
        [],
        [message, shaped((1, 1, blocks, width), F32), edge],
        [rows_scratch],
        direct=(returned, near, base, scale),
    )
    arrived = exchange(sent)
    (field,) = staged(
        lambda *refs: bulk_kernel(False, *refs),
        [field, (layer0, (0, 0)), *steady],
        [shaped(disp.shape, F32)],
        bulk_scratch,
    )
    (gap,) = staged(
        known_kernel, [(layer0, (0, 0)), pick3, normal_rows, (gap0, (0, 0))], [shaped(gap0.shape[2:], F32)], kept=(0,)
    )
    sent, pushed, low, high = contact(arrived, [*ready, gap], *in_hbm(last, high), field)
    returned = exchange(sent)
    low, high = shift(low, 1), shift(high, -1)
    ends = [(array, (0, l)) for array in (field, inv_diag) for l in (0, layers - 1)]
    held = staged(
        tail_kernel,
        ends + [pushed, back_sum, pick, k_layer],
        [layer, layer, layer, layer, near_shape, shaped(k_layer.shape, BF16)],
        kept=range(6),
    )
    return pl.pallas_call(
        last_kernel,
        out_shape=pltpu.HBM(disp.shape, F32),
        in_specs=[IN_VMEM] * 9 + [HBM],
        out_specs=HBM,
        scratch_shapes=[
            rows_scratch, VMEM(base.shape, F32), VMEM(base.shape, F32), pltpu.SemaphoreType.DMA((2,))
        ],
        input_output_aliases={9: 0},
        compiler_params=pltpu.CompilerParams(vmem_limit_bytes=16 * 2**20),
    )(
        *[pltpu.with_memory_space_constraint(array, pltpu.VMEM) for array in (returned, *held, low, high)],
        *in_hbm(field),
    )


def solution(mesh):
    in_specs = (
        P("dom", "slab", None, None),
        P("dom", "slab", None, None),
        P("dom", "slab", None, None),
        P(),
        P(),
        P(),
        P("dom", "slab", None, None, None),
        P("dom", "slab", None, None),
        P("dom", "slab", None, None),
        P("dom", "slab", None),
        P("dom", "slab", None),
        P("dom", "slab", None),
    )
    return jax.shard_map(
        on_device, mesh=mesh, in_specs=in_specs, out_specs=P("dom", "slab", None, None), check_vma=False
    )
```

```python
import jax
import jax.numpy as jnp
from jax import lax
from jax.experimental import pallas as pl
from jax.experimental.pallas import tpu as pltpu
from jax.sharding import PartitionSpec as P

PENALTY = 2.0
CAPACITY = 4
GROUP = 32
PIECES = 4
PARTS = 2
VMEM = pltpu.VMEM
HBM = pl.BlockSpec(memory_space=pltpu.HBM)
ANY = pl.BlockSpec(memory_space=pl.ANY)
IN_VMEM = pl.BlockSpec(memory_space=VMEM)
BF16 = jnp.bfloat16
F32 = jnp.float32


def dot(a, b, dims=((1,), (0,))):
    return lax.dot_general(a, b, (dims, ((), ())), preferred_element_type=F32)


def iota(shape, axis):
    return lax.broadcasted_iota(jnp.int32, shape, axis)


def shaped(shape, dtype):
    return jax.ShapeDtypeStruct(shape, dtype)


def in_hbm(*arrays):
    return [pltpu.with_memory_space_constraint(array, pltpu.HBM) for array in arrays]


def staged(body, ins, outs, scratch=(), tokens=(), loose=(), free_outs=False, direct=(), kept=(), fills=()):
    ins = [item if isinstance(item, tuple) else (item, ()) for item in ins]
    operands = [array if i in loose else in_hbm(array)[0] for i, (array, _) in enumerate(ins)]
    held = [VMEM(part_shape(array, index), array.dtype) for array, index in ins]
    given = [VMEM(out.shape, out.dtype) for i, out in enumerate(outs) if i not in kept]
    here = [pltpu.with_memory_space_constraint(array, pltpu.VMEM) for array in direct]

    def kernel(*refs):
        refs = list(refs)

        def pop(count):
            taken = refs[:count]
            del refs[:count]
            return taken

        landed, sources, fill_sources = pop(len(here)), pop(len(ins)), pop(len(fills))
        _, targets = pop(len(tokens)), pop(len(outs))
        inside, leaving, (in_sems, out_sems, fill_sems), extra = pop(len(ins)), pop(len(given)), pop(3), refs
        leaving = [targets[i] if i in kept else leaving.pop(0) for i in range(len(outs))]
        loads = {}
        for i, (source, ref, (_, index)) in enumerate(zip(sources, inside, ins)):
            loads[i] = pltpu.make_async_copy(source.at[index] if index else source, ref, in_sems.at[i])
            loads[i].start()

        stores = []
        for i, (source, (_, index, out)) in enumerate(zip(fill_sources, fills)):
            stores.append(pltpu.make_async_copy(source.at[index] if index else source, targets[out], fill_sems.at[i]))
            stores[-1].start()

        def take(i):
            if i in loads:
                loads.pop(i).wait()
            return inside[i]

        def give(i, index=None, piece=None):
            source, target = leaving[i], targets[i]
            if index is not None:
                source, target = source.at[index], target.at[index]
            sem = out_sems.at[i if piece is None else len(outs) + piece]
            stores.append(pltpu.make_async_copy(source, target, sem))
            stores[-1].start()

        body(*landed, take, leaving, give, *extra)
        assert not loads
        for store in stores:
            store.wait()

    def space(i, out):
        return out if free_outs else (pltpu.VMEM if i in kept else pltpu.HBM)(out.shape, out.dtype)

    return pl.pallas_call(
        kernel,
        out_shape=tuple(space(i, out) for i, out in enumerate(outs)),
        in_specs=[IN_VMEM] * len(here) + [ANY] * (len(ins) + len(fills) + len(tokens)),
        out_specs=tuple(IN_VMEM if i in kept else ANY for i in range(len(outs))),
        scratch_shapes=held
        + given
        + [pltpu.SemaphoreType.DMA((max(count, 1),)) for count in (len(ins), len(outs) + PIECES, len(fills))]
        + list(scratch),
        compiler_params=pltpu.CompilerParams(vmem_limit_bytes=32 * 2**20),
    )(*here, *operands, *in_hbm(*[array for array, _, _ in fills]), *tokens)


def part_shape(array, index):
    kept = [i.size for i in index if not isinstance(i, int)]
    return tuple(kept) + array.shape[len(index) :]


def slots_of(src, count):
    segs = src.shape[1]
    named = (iota((count, segs), 0) == src).astype(BF16)
    earlier = (iota((segs, segs), 0) < iota((segs, segs), 1)).astype(BF16)
    before = dot(named, earlier)
    rank = jnp.sum(named.astype(F32) * before, axis=0, keepdims=True).astype(jnp.int32)
    return named, rank


def request_kernel(blocks, take, out, give):
    src, master = take(0)[0], take(1)[0]
    count = out[0].shape[0]
    named, rank = slots_of(src, count)
    segs = named.shape[1]
    wants = (iota((CAPACITY * blocks, segs), 0) == rank * blocks + master).astype(BF16)
    out[0][...] = dot(named, wants, ((1,), (1,)))
    give(0)


def split3(rows):
    high = rows.astype(BF16)
    rest = rows - high.astype(F32)
    mid = rest.astype(BF16)
    low = (rest - mid.astype(F32)).astype(BF16)
    return jnp.concatenate([high, mid, low], axis=0)


def prep_kernel(take, out, give):
    put_ref, get_ref, take_ref, sum_ref, normal_rows_ref, low_ref, high_ref, surface_ref, _, get_v, put_v, normal_v, known_ref = out
    surface = take(3)[...].astype(BF16)
    surface_ref[...] = copies(surface)
    high_ref[...] = surface
    low_ref[...] = take(4)[...].astype(BF16)
    give(5)
    give(6)
    src, slave, normals = take(0)[0], take(1)[0], take(2)[...]
    blocks = normals.shape[0]
    slots, segs = put_ref.shape
    _, rank = slots_of(src, slots // CAPACITY)
    put = (iota((slots, segs), 0) == src * CAPACITY + rank).astype(F32)
    put_ref[...] = put.astype(BF16)
    give(0)
    get_ref[...] = jnp.transpose(put).astype(BF16)
    give(1)
    spread = (lax.rem(iota((4 * blocks, segs), 0), blocks) == slave).astype(F32)
    pick = jnp.transpose(spread)[:, : 3 * blocks].astype(BF16)
    take_ref[...] = pick
    give(2)
    once = spread[:blocks].astype(BF16)
    sum_ref[...] = jnp.concatenate([once, once], axis=1)
    give(3)
    normal_rows = dot(pick, split3(normals))
    normal_rows_ref[...] = normal_rows
    give(4)
    put_v[...] = put_ref[...]
    get_v[...] = get_ref[...]
    normal_v[...] = normal_rows
    known_ref[...] = known(take(5)[...], normal_rows, dot(pick, split3(take(3)[...])))


def known(gap, normal_rows, slave_rows):
    x, y, z = columns(normal_rows * slave_rows)
    return gap - (x + y + z)


def columns(rows):
    nodes = rows.shape[1] // 3
    return [rows[:, c * nodes : (c + 1) * nodes] for c in range(3)]


def known_kernel(take, out, give):
    slave_rows = dot(take(1)[...], split3(take(0)[...]))
    out[0][...] = known(take(3)[...], take(2)[...], slave_rows)


def place(rows, scratch, out_ref, send):
    scratch[...] = rows
    pairs = out_ref.shape[0] // 2
    part = pairs // PIECES
    for j in range(pairs):
        both = scratch[2 * CAPACITY * j : 2 * CAPACITY * (j + 1), :]
        out_ref[2 * j] = both[:CAPACITY].astype(BF16)
        out_ref[2 * j + 1] = both[CAPACITY:].astype(BF16)
        if (j + 1) % part == 0:
            send(j // part, pl.ds(2 * (j + 1 - part), 2 * part))


def gathered(in_ref, scratch):
    for j in range(in_ref.shape[0] // 2):
        both = jnp.concatenate([in_ref[2 * j].astype(F32), in_ref[2 * j + 1].astype(F32)], axis=0)
        scratch[2 * CAPACITY * j : 2 * CAPACITY * (j + 1), :] = both
    return scratch[...].astype(BF16)


def copies(rows):
    return jnp.concatenate([rows] * CAPACITY, axis=0)


def first_kernel(asked_ref, surface_ref, take, out, give, scratch):
    pick_ref, out_ref = out
    slots, wide = pick_ref.shape
    count, blocks = slots // CAPACITY, wide // CAPACITY
    expand = (lax.div(iota((slots, count), 0), CAPACITY) == iota((slots, count), 1)).astype(BF16)
    mine = lax.div(iota((slots, wide), 1), blocks) == lax.rem(iota((slots, wide), 0), CAPACITY)
    rows = dot(expand, asked_ref[...].astype(BF16))
    pick = jnp.where(mine, rows, 0.0).astype(BF16)
    pick_ref[...] = pick
    give(0)
    place(dot(pick, surface_ref[...]), scratch, out_ref, lambda piece, part: give(1, part, piece))


def contact_kernel(
    in_ref, early_ref, get_ref, put_ref, normal_ref, known_ref, mortar_hbm, low_hbm, high_hbm, token,
    out_hbm, pushed_hbm, low_out, high_out, scratch, back_ref, out_ref, pushed_ref, later_ref, sems, later_sems,
):
    early, _, nodes = early_ref.shape
    segs = early + later_ref.shape[0]
    later = pltpu.make_async_copy(mortar_hbm.at[0, 0, pl.ds(early, segs - early)], later_ref, later_sems.at[0])
    later.start()
    edges = [
        pltpu.make_async_copy(low_hbm, low_out, later_sems.at[1]),
        pltpu.make_async_copy(high_hbm, high_out, later_sems.at[2]),
    ]
    for edge in edges:
        edge.start()
    member = lax.rem(iota((3 * GROUP, nodes), 0), GROUP)
    place_in = lax.rem(member, 4)
    block_of = lax.div(member, 4)
    odd = lax.rem(place_in, 2) == 1
    late = place_in >= 2
    zero = jnp.zeros((3 * GROUP, nodes), BF16)
    master = dot(get_ref[...], gathered(in_ref, scratch)).astype(BF16)

    def choose(parts):
        result = parts[0]
        for b in range(1, GROUP // 4):
            result = jnp.where(block_of == b, parts[b], result)
        return result

    def weights(g):
        ref, start = (early_ref, GROUP * g) if GROUP * g < early else (later_ref, GROUP * g - early)
        for k in range(start, start + GROUP, 4):
            left = ref[k : k + 2].reshape(2 * nodes, nodes)
            right = ref[k + 2 : k + 4].reshape(2 * nodes, nodes)
            yield jnp.concatenate([left, right], axis=1)

    for g in range(segs // GROUP):
        own = slice(GROUP * g, GROUP * (g + 1))
        if GROUP * g == early:
            later.wait()
        um = jnp.concatenate(columns(master[own]), axis=0)
        normal = jnp.concatenate(columns(normal_ref[own, :]), axis=0)
        lhs = jnp.concatenate([jnp.where(late, zero, um), jnp.where(late, um, zero)], axis=1)
        parts = []
        for w in weights(g):
            r = dot(lhs, w, ((1,), (1,)))
            parts.append(jnp.where(odd, r[:, nodes:], r[:, :nodes]))
        terms = normal * choose(parts)
        gap = known_ref[own, :] + (terms[:GROUP] + terms[GROUP : 2 * GROUP] + terms[2 * GROUP :])
        pressure = PENALTY * jnp.maximum(-gap, 0.0)
        for c, part in enumerate(columns(normal_ref[own, :])):
            cols = slice(nodes * c, nodes * (c + 1))
            pushed = pressure * part
            high = pushed.astype(BF16)
            pushed_ref[own, cols] = high
            pushed_ref[segs + GROUP * g : segs + GROUP * (g + 1), cols] = (pushed - high.astype(F32)).astype(BF16)
    store = pltpu.make_async_copy(pushed_ref, pushed_hbm, sems.at[0])
    store.start()
    for g in range(segs // GROUP):
        own = slice(GROUP * g, GROUP * (g + 1))
        high = jnp.concatenate(columns(pushed_ref[own, :]), axis=0)
        lhs = jnp.concatenate([jnp.where(odd, zero, high), jnp.where(odd, high, zero)], axis=1)
        parts = []
        for w in weights(g):
            r = dot(lhs, w)
            parts.append(jnp.where(late, r[:, nodes:], r[:, :nodes]))
        back = (-choose(parts)).astype(BF16)
        for c in range(3):
            back_ref[own, nodes * c : nodes * (c + 1)] = back[GROUP * c : GROUP * (c + 1)]
    stores = edges + [store]

    def send(piece, part):
        stores.append(pltpu.make_async_copy(out_ref.at[part], out_hbm.at[part], sems.at[1 + piece]))
        stores[-1].start()

    place(dot(put_ref[...], back_ref[...]), scratch, out_ref, send)
    for copy in stores:
        copy.wait()


def bulk_kernel(whole, take, out, give, rounded_ref, product_ref):
    out_ref = out[0]
    _, layers, blocks, width = out_ref.shape
    rows = layers * blocks
    step = (rows + 2 * blocks) // PARTS
    field_ref, layer_ref = take(0), take(1)
    zero = jnp.zeros((blocks, width), BF16)
    rounded_ref[:blocks] = take(7)[...] if whole else zero
    rounded_ref[blocks : 2 * blocks] = layer_ref[...].astype(BF16)
    for l in range(1, layers):
        rounded_ref[(l + 1) * blocks : (l + 2) * blocks] = field_ref[0, l].astype(BF16)
    rounded_ref[rows + blocks :] = take(8)[...] if whole else zero
    weight_refs = [take(i) for i in (2, 3, 4)]

    @pl.loop(0, PARTS)
    def multiply(p):
        here = pl.ds(pl.multiple_of(p * step, 16), step)
        part = rounded_ref[here]
        for k, weight_ref in enumerate(weight_refs):
            product_ref[here, k * width : (k + 1) * width] = dot(part, weight_ref[...])

    block = iota((blocks, width), 0)

    def inner(l):
        def product(layer, k):
            return product_ref[pl.ds(pl.multiple_of(layer * blocks, blocks), blocks), k * width : (k + 1) * width]

        side = product(l + 1, 2)
        left = jnp.where(block == 0, 0.0, pltpu.roll(side, 1, 0))
        right = jnp.where(block == blocks - 1, 0.0, pltpu.roll(side, blocks - 1, 0))
        return product(l + 1, 0) + (product(l, 1) + product(l + 2, 1)) + (left + right)

    load_ref, scale_ref = take(5), take(6)

    def stepped(old, l, force):
        return old + scale_ref[0, l].astype(F32) * (load_ref[0, l].astype(F32) - force)

    first = inner(0)
    if whole:
        base_ref, near_ref, pick_ref, last_ref = out[1:5]
        pick_ref[...] = take(11)[...]
        near_ref[...] = scale_ref[0, 0].astype(F32)
        first = first + dot(take(10)[...], take(9)[...])
        base_ref[...] = stepped(layer_ref[...], 0, first)
    out_ref[0, 0] = stepped(layer_ref[...], 0, first)

    @pl.loop(1, layers)
    def update(l):
        out_ref[0, l] = stepped(field_ref[0, l], l, inner(l))

    give(0)
    if whole:
        last_ref[...] = out_ref[0, layers - 1].astype(BF16)
        give(4)


def tail_kernel(take, out, give):
    first, last, first_scale, last_scale = [take(i)[...].astype(F32) for i in range(4)]
    base_ref, row_ref, scale0_ref, scale1_ref, pick_ref, weight_ref = out
    base_ref[...] = first - first_scale * dot(take(5)[...], take(4)[...])
    row_ref[...] = last
    scale0_ref[...] = first_scale
    scale1_ref[...] = last_scale
    pick_ref[...] = take(6)[...]
    weight_ref[...] = take(7)[...]


def summed(in_ref, pick_ref, base_ref, scale_ref, scratch):
    sums = dot(pick_ref[...], gathered(in_ref, scratch), ((0,), (0,)))
    blocks = base_ref.shape[0]
    total = sums[:blocks]
    for k in range(1, CAPACITY):
        total = total + sums[k * blocks : (k + 1) * blocks]
    return base_ref[...] - scale_ref[...] * total


def next_kernel(in_ref, pick_ref, base_ref, scale_ref, take, out, give, scratch):
    out_ref, layer_ref, high_ref = out
    first = summed(in_ref, pick_ref, base_ref, scale_ref, scratch)
    layer_ref[0, 0] = first
    give(1)
    surface = first.astype(BF16)
    high_ref[...] = surface
    give(2)
    place(dot(pick_ref[...], copies(surface)), scratch, out_ref, lambda piece, part: give(0, part, piece))


def last_kernel(
    in_ref, base_ref, row_ref, scale0_ref, scale1_ref, pick_ref, weight_ref, low_ref, high_ref, field_hbm,
    out_hbm, scratch, first_ref, last_ref, sems,
):
    end = out_hbm.shape[1] - 1
    last_ref[...] = row_ref[...] - scale1_ref[...] * dot(high_ref[...], weight_ref[...])
    stores = [pltpu.make_async_copy(last_ref, out_hbm.at[0, end], sems.at[0])]
    stores[0].start()
    below = scale0_ref[...] * dot(low_ref[...], weight_ref[...])
    first_ref[...] = summed(in_ref, pick_ref, base_ref, scale0_ref, scratch) - below
    stores.append(pltpu.make_async_copy(first_ref, out_hbm.at[0, 0], sems.at[1]))
    stores[1].start()
    for store in stores:
        store.wait()


def shift(block, step):
    count = lax.axis_size("slab")
    pairs = [(i, i + step) for i in range(count) if 0 <= i + step < count]
    return lax.ppermute(block, "slab", pairs)


def exchange(parts):
    return lax.all_to_all(parts, "dom", 0, 0, tiled=True)


def on_device(
    disp, f_ext, inv_diag, k_self, k_layer, k_side, mortar, gap0, normals, seg_slave, seg_src, seg_master
):
    _, layers, blocks, width = disp.shape
    segs = seg_slave.shape[2]
    count = lax.axis_size("dom")
    slots = count * CAPACITY
    wide = CAPACITY * blocks
    rows_scratch = VMEM((slots, width), F32)
    message = shaped((count, CAPACITY, width), BF16)
    edge = shaped((blocks, width), BF16)
    layer = shaped((blocks, width), F32)

    early = max(segs * 5 // 8 // GROUP, 1) * GROUP
    early_part = (0, 0, pl.ds(0, early))
    (asked,) = staged(
        lambda *refs: request_kernel(blocks, *refs), [seg_src, seg_master], [shaped((count, wide), F32)], free_outs=True
    )
    put, get, pick3, back_sum, normal_rows, low, high, surface, *ready, gap = staged(
        prep_kernel,
        [seg_src, seg_slave, (normals, (0, 0)), (disp, (0, 0)), (disp, (0, layers - 1)), (gap0, (0, 0))],
        [
            shaped((slots, segs), BF16),
            shaped((segs, slots), BF16),
            shaped((segs, 3 * blocks), BF16),
            shaped((blocks, 2 * segs), BF16),
            shaped((segs, width), F32),
            edge,
            edge,
            shaped((CAPACITY * blocks, width), BF16),
            shaped((early,) + mortar.shape[3:], BF16),
            shaped((segs, slots), BF16),
            shaped((slots, segs), BF16),
            shaped((segs, width), F32),
            shaped(gap0.shape[2:], F32),
        ],
        tokens=[asked],
        kept=(7, 8, 9, 10, 11, 12),
        fills=[(mortar, early_part, 8)],
    )
    asked = exchange(asked.reshape(count, 1, wide)).reshape(count, wide)
    pick, sent = staged(
        first_kernel, [], [shaped((slots, wide), BF16), message], [rows_scratch], direct=(asked, surface)
    )

    def contact(arrived, near_arrays, low, high, token):
        here = [pltpu.with_memory_space_constraint(array, pltpu.VMEM) for array in (arrived, *near_arrays)]
        pushed = shaped((2 * segs, width), BF16)
        return pl.pallas_call(
            contact_kernel,
            out_shape=[pltpu.HBM(out.shape, BF16) for out in (message, pushed, edge, edge)],
            in_specs=[IN_VMEM] * 6 + [ANY] * 4,
            out_specs=[ANY] * 4,
            scratch_shapes=[
                rows_scratch,
                VMEM((segs, width), BF16),
                VMEM(message.shape, BF16),
                VMEM(pushed.shape, BF16),
                VMEM((segs - early,) + mortar.shape[3:], BF16),
                pltpu.SemaphoreType.DMA((1 + PIECES,)),
                pltpu.SemaphoreType.DMA((3,)),
            ],
            compiler_params=pltpu.CompilerParams(vmem_limit_bytes=16 * 2**20),
        )(*here, *in_hbm(mortar), low, high, *in_hbm(token))

    rows = (layers + 2) * blocks
    bulk_scratch = [VMEM((rows, width), BF16), VMEM((rows, 3 * width), F32)]
    steady = [k_self, k_layer, k_side, f_ext, inv_diag]
    near_shape = shaped((slots, wide), BF16)

    arrived = exchange(sent)
    low, high = shift(low, 1), shift(high, -1)
    sent, pushed, low, high = contact(arrived, [*ready, gap], low, high, pick)
    returned = exchange(sent)
    field, base, scale, near, last, *ready = staged(
        lambda *refs: bulk_kernel(True, *refs),
        [disp, (disp, (0, 0)), *steady, low, high, pushed, back_sum, pick],
        [shaped(disp.shape, F32), layer, layer, near_shape, edge] + [shaped(array.shape, array.dtype) for array in ready],
        bulk_scratch,
        kept=(1, 2, 3, 5, 6, 7, 8),
        fills=[(mortar, early_part, 5), (get, (), 6), (put, (), 7), (normal_rows, (), 8)],
    )
    sent, layer0, high = staged(
        next_kernel,
        [],
        [message, shaped((1, 1, blocks, width), F32), edge],
        [rows_scratch],
        direct=(returned, near, base, scale),
    )
    arrived = exchange(sent)
    (field,) = staged(
        lambda *refs: bulk_kernel(False, *refs),
        [field, (layer0, (0, 0)), *steady],
        [shaped(disp.shape, F32)],
        bulk_scratch,
    )
    (gap,) = staged(
        known_kernel, [(layer0, (0, 0)), pick3, normal_rows, (gap0, (0, 0))], [shaped(gap0.shape[2:], F32)], kept=(0,)
    )
    sent, pushed, low, high = contact(arrived, [*ready, gap], *in_hbm(last, high), field)
    returned = exchange(sent)
    low, high = shift(low, 1), shift(high, -1)
    ends = [(array, (0, l)) for array in (field, inv_diag) for l in (0, layers - 1)]
    held = staged(
        tail_kernel,
        ends + [pushed, back_sum, pick, k_layer],
        [layer, layer, layer, layer, near_shape, shaped(k_layer.shape, BF16)],
        kept=range(6),
    )
    return pl.pallas_call(
        last_kernel,
        out_shape=pltpu.HBM(disp.shape, F32),
        in_specs=[IN_VMEM] * 9 + [HBM],
        out_specs=HBM,
        scratch_shapes=[
            rows_scratch, VMEM(base.shape, F32), VMEM(base.shape, F32), pltpu.SemaphoreType.DMA((2,))
        ],
        input_output_aliases={9: 0},
        compiler_params=pltpu.CompilerParams(vmem_limit_bytes=16 * 2**20),
    )(
        *[pltpu.with_memory_space_constraint(array, pltpu.VMEM) for array in (returned, *held, low, high)],
        *in_hbm(field),
    )


def solution(mesh):
    in_specs = (
        P("dom", "slab", None, None),
        P("dom", "slab", None, None),
        P("dom", "slab", None, None),
        P(),
        P(),
        P(),
        P("dom", "slab", None, None, None),
        P("dom", "slab", None, None),
        P("dom", "slab", None, None),
        P("dom", "slab", None),
        P("dom", "slab", None),
        P("dom", "slab", None),
    )
    return jax.shard_map(
        on_device, mesh=mesh, in_specs=in_specs, out_specs=P("dom", "slab", None, None), check_vma=False
    )
```
